32 devices in a mesh: rows: 2 (over x), heads: 8 (over z, y), seq: 2 (over core).
Axes of the slice: x: 2, y: 2, z: 4, core: 2. Of those that a mesh axis runs over, the one named last changes fastest.
Arguments:
- inputs: bfloat16 [4, 2, 2, 1024, 2048], P(None, 'rows', 'seq', 'heads'), may hold values from -6 to 6
- segment_ids: int32 [4, 2, 2048], P(None, 'rows'), may hold values from 0 to 6, as said below
- cotangent: bfloat16 [4, 2, 2, 1024, 2048], P(None, 'rows', 'seq', 'heads'), may hold values from -6 to 6
- attn_gain: bfloat16 [2048], P(('rows', 'heads', 'seq')), may hold values from 0.5 to 1.5
- ffn_gain: bfloat16 [2048], P(('rows', 'heads', 'seq')), may hold values from 0.5 to 1.5
- query_weight: bfloat16 [2048, 2048], P(('rows', 'seq'), 'heads'), may hold values from -0.125 to 0.125
- key_weight: bfloat16 [2048, 512], P(('rows', 'seq')), may hold values from -0.125 to 0.125
- value_weight: bfloat16 [2048, 512], P(('rows', 'seq')), may hold values from -0.125 to 0.125
- output_weight: bfloat16 [2048, 2048], P('heads', ('rows', 'seq')), may hold values from -1 to 1
- query_down: bfloat16 [2048, 8], P(('rows', 'heads', 'seq')), may hold values from -0.125 to 0.125
- query_lift: bfloat16 [8, 2048], P(('rows', 'seq'), 'heads'), may hold values from -1.5 to 1.5
- key_down: bfloat16 [2048, 8], P(('rows', 'heads', 'seq')), may hold values from -0.125 to 0.125
- key_lift: bfloat16 [8, 512], P(('rows', 'seq')), may hold values from -1.5 to 1.5
- value_down: bfloat16 [2048, 8], P(('rows', 'heads', 'seq')), may hold values from -0.125 to 0.125
- value_lift: bfloat16 [8, 512], P(('rows', 'seq')), may hold values from -1.5 to 1.5
- output_down: bfloat16 [2048, 8], P('heads', ('rows', 'seq')), may hold values from -1 to 1
- output_lift: bfloat16 [8, 2048], P(None, ('rows', 'heads', 'seq')), may hold values from -1.5 to 1.5
- feature_maps: bfloat16 [32, 64, 64], P('heads', ('rows', 'seq')), may hold values from -0.75 to 0.75
- gate_weight: bfloat16 [2048, 8192], P(('rows', 'seq'), 'heads'), may hold values from -0.125 to 0.125
- up_weight: bfloat16 [2048, 8192], P(('rows', 'seq'), 'heads'), may hold values from -0.125 to 0.125
- down_weight: bfloat16 [8192, 2048], P('heads', ('rows', 'seq')), may hold values from -0.0625 to 0.0625
Outputs:
- output: bfloat16 [4, 2, 2, 1024, 2048], P(None, 'rows', 'seq', 'heads')
- input_grad: float32 [4, 2, 2, 1024, 2048], P(None, 'rows', 'seq', 'heads')
- attn_gain_grad: float32 [2048], P(('rows', 'heads', 'seq'))
- ffn_gain_grad: float32 [2048], P(('rows', 'heads', 'seq'))
- query_weight_grad: float32 [2048, 2048], P(('rows', 'seq'), 'heads')
- key_weight_grad: float32 [2048, 512], P(('rows', 'seq'))
- value_weight_grad: float32 [2048, 512], P(('rows', 'seq'))
- output_weight_grad: float32 [2048, 2048], P('heads', ('rows', 'seq'))
- query_down_grad: float32 [2048, 8], P(('rows', 'heads', 'seq'))
- query_lift_grad: float32 [8, 2048], P(('rows', 'seq'), 'heads')
- key_down_grad: float32 [2048, 8], P(('rows', 'heads', 'seq'))
- key_lift_grad: float32 [8, 512], P(('rows', 'seq'))
- value_down_grad: float32 [2048, 8], P(('rows', 'heads', 'seq'))
- value_lift_grad: float32 [8, 512], P(('rows', 'seq'))
- output_down_grad: float32 [2048, 8], P('heads', ('rows', 'seq'))
- output_lift_grad: float32 [8, 2048], P(None, ('rows', 'heads', 'seq'))
- feature_maps_grad: float32 [32, 64, 64], P('heads', ('rows', 'seq'))
- gate_weight_grad: float32 [2048, 8192], P(('rows', 'seq'), 'heads')
- up_weight_grad: float32 [2048, 8192], P(('rows', 'seq'), 'heads')
- down_weight_grad: float32 [8192, 2048], P('heads', ('rows', 'seq'))
The draws below stay inside these ranges and needn't reach their ends.
Inputs may be any that keep to these rules, and one draw needn't show every extreme that they name: `segment_ids`: each row's segment ids start at 0 on its first token and never fall from one token to the next.
All inputs are finite; a program needn't handle non-finite values.
Results may differ from the reference program's by a relative error of at most 0.014.
Values may be sent and summed in bfloat16 or wider, within the bound.
No kernel may reach another device: no remote copies, remote signals or barrier semaphores. Data moves between devices by JAX's collectives and lax.ppermute only.
A program may use at most 704 MiB of HBM per device.

```python
import jax
import jax.numpy as jnp
from jax import lax

D = 2048
FF = 8192
HEADS = 32
KV = 8
HD = 64
RANK = 8
WINDOW = 64
SEQ_LEN = 2048
MB = 4
ROWS = 2
SPLITS = 2
SPAN = 1024


def draw_segment_ids(key, part):
    key = jax.random.fold_in(key, 7)
    row_keys = jax.random.split(key, MB * ROWS)
    quarter = SEQ_LEN // 4

    def single_row(row_key):
        chosen = jax.random.permutation(row_key, 2 * quarter - 1)[:6]
        cut_points = jnp.where(chosen < quarter - 1, chosen + 1, chosen - (quarter - 1) + 3 * quarter)
        places = jnp.arange(SEQ_LEN)
        return jnp.sum((cut_points[None, :] <= places[:, None]).astype(jnp.int32), axis=1)
    return jax.vmap(single_row)(row_keys).reshape(MB, ROWS, SEQ_LEN).astype(jnp.int32)


def level_of(rng, extent, cuts, smallest, top_value):
    level = 1.0
    for position, shards_of in cuts:
        heights = jax.random.uniform(jax.random.fold_in(jax.random.fold_in(rng, 6), position), (shards_of,), jnp.float32, smallest / len(cuts), top_value / len(cuts))
        level = level * jnp.repeat(jnp.exp(heights), extent[position] // shards_of).reshape((-1,) + (1,) * (len(extent) - 1 - position))
    return level


def scatter_about(own_key, dims, deviation, bound, cuts=(), kind=jnp.bfloat16):
    level = level_of(own_key, dims, cuts, -0.22, 0.18) if cuts else 1.0
    array = jax.random.normal(own_key, dims, jnp.float32) * deviation * level
    return jnp.minimum(jnp.maximum(array, -bound), bound).astype(kind)


def setup_inputs(seed: int = 0) -> dict:
    key_of = jax.random.split(jax.random.key(seed), 22)
    inputs = scatter_about(key_of[0], (MB, ROWS, SPLITS, SPAN, D), 1.0, 6.0, ((1, 2), (2, 2), (3, 8)))
    segment_ids = draw_segment_ids(jax.random.fold_in(key_of[21], 71), 0)
    cotangent = scatter_about(key_of[2], (MB, ROWS, SPLITS, SPAN, D), 1.0, 6.0, ((1, 2), (2, 2), (3, 8)))
    attn_gain = jnp.clip(1.0 + 0.1 * jax.random.normal(key_of[3], (D,), jnp.float32), 0.5, 1.5).astype(jnp.bfloat16)
    ffn_gain = jnp.clip(1.0 + 0.1 * jax.random.normal(key_of[4], (D,), jnp.float32), 0.5, 1.5).astype(jnp.bfloat16)
    query_weight = scatter_about(key_of[5], (D, HEADS * HD), D ** -0.5, 0.125, ((0, 4), (1, 8)))
    key_weight = scatter_about(key_of[6], (D, KV * HD), D ** -0.5, 0.125, ((0, 4),))
    value_weight = scatter_about(key_of[7], (D, KV * HD), D ** -0.5, 0.125, ((0, 4),))
    output_weight = scatter_about(key_of[8], (HEADS * HD, D), (HEADS * HD // 64) ** -0.5, 1.0, ((0, 8), (1, 4)))
    query_down = scatter_about(key_of[9], (D, RANK), D ** -0.5, 0.125, ((0, 32),))
    query_lift = scatter_about(key_of[10], (RANK, HEADS * HD), (2 * RANK) ** -0.5, 1.5, ((0, 4), (1, 8)))
    key_down = scatter_about(key_of[11], (D, RANK), D ** -0.5, 0.125, ((0, 32),))
    key_lift = scatter_about(key_of[12], (RANK, KV * HD), (2 * RANK) ** -0.5, 1.5, ((0, 4),))
    value_down = scatter_about(key_of[13], (D, RANK), D ** -0.5, 0.125, ((0, 32),))
    value_lift = scatter_about(key_of[14], (RANK, KV * HD), (2 * RANK) ** -0.5, 1.5, ((0, 4),))
    output_down = scatter_about(key_of[15], (HEADS * HD, RANK), (HEADS * HD // 64) ** -0.5, 1.0, ((0, 8), (1, 4)))
    output_lift = scatter_about(key_of[16], (RANK, D), (2 * RANK) ** -0.5, 1.5, ((1, 32),))
    feature_maps = scatter_about(key_of[17], (HEADS, HD, HD), HD ** -0.5, 0.75, ((0, 8), (1, 4)))
    gate_weight = scatter_about(key_of[18], (D, FF), D ** -0.5, 0.125, ((0, 4), (1, 8)))
    up_weight = scatter_about(key_of[19], (D, FF), D ** -0.5, 0.125, ((0, 4), (1, 8)))
    down_weight = scatter_about(key_of[20], (FF, D), FF ** -0.5, 0.0625, ((0, 8), (1, 4)))
    return {"inputs": inputs, "segment_ids": segment_ids, "cotangent": cotangent, "attn_gain": attn_gain, "ffn_gain": ffn_gain, "query_weight": query_weight, "key_weight": key_weight, "value_weight": value_weight, "output_weight": output_weight, "query_down": query_down, "query_lift": query_lift, "key_down": key_down, "key_lift": key_lift, "value_down": value_down, "value_lift": value_lift, "output_down": output_down, "output_lift": output_lift, "feature_maps": feature_maps, "gate_weight": gate_weight, "up_weight": up_weight, "down_weight": down_weight}


highest = lax.Precision.HIGHEST

@jax.custom_vjp
def low(v):
    return lax.optimization_barrier(v.astype(jnp.bfloat16)).astype(jnp.float32)

@jax.custom_vjp
def low_back(v):
    return v

def low_keep(v):
    return (low(v), None)

def low_pass(kept, grad):
    return (grad,)

def back_keep(v):
    return (v, None)

def back_low(kept, grad):
    return (low(grad),)
low.defvjp(low_keep, low_pass)
low_back.defvjp(back_keep, back_low)

def matmul(left, right):
    return jnp.dot(left, right, precision=highest)

def rms_norm(values, gain):
    return values * lax.rsqrt(lax.optimization_barrier(jnp.mean(values * values, axis=-1, keepdims=True)) + 1e-05) * gain

def feature_map(vectors, maps):
    logits = jnp.einsum('che,hef->chf', vectors, maps, precision=highest)
    return jnp.concatenate([jax.nn.softmax(logits, axis=-1), jax.nn.softmax(-logits, axis=-1)], axis=-1)

def block_terms(features, values, segment):
    lasts = segment[:, -1]
    keeper = jnp.where(segment == lasts[:, None], 1.0, 0.0)
    weighted = features * keeper[:, :, None, None]
    states = jnp.einsum('nwhf,nwhe->nhfe', weighted, values, precision=highest)
    return (states, lax.optimization_barrier(jnp.sum(weighted, axis=1)), lasts[:, None, None, None])

def link_states(earlier, latter):
    early_states, early_totals, early_tags = earlier
    late_states, late_totals, late_tags = latter
    joined = jnp.where(early_tags == late_tags, 1.0, 0.0)
    vacant = late_tags < 0.0
    states = jnp.where(vacant, early_states, late_states + joined * early_states)
    totals = jnp.where(vacant[..., 0], early_totals, late_totals + joined[..., 0] * early_totals)
    return (states, totals, jnp.where(vacant, early_tags, late_tags))

def window_attend(queries, key_rows, value_rows, key_segment, query_segment, maps, initial):
    length, head_count, head_width = queries.shape
    block_count = length // WINDOW
    query_features = feature_map(queries, maps)
    key_features = feature_map(key_rows, maps)
    feat_width = key_features.shape[-1]
    key_blocks = key_rows.reshape(block_count + 1, WINDOW, head_count, head_width)
    value_blocks = value_rows.reshape(block_count + 1, WINDOW, head_count, head_width)
    feature_blocks = key_features.reshape(block_count + 1, WINDOW, head_count, feat_width)
    segment_blocks = key_segment.reshape(block_count + 1, WINDOW)
    terms = block_terms(feature_blocks, value_blocks, segment_blocks)
    empty = (jnp.zeros_like(terms[0][:1]), jnp.zeros_like(terms[1][:1]), jnp.full_like(terms[2][:1], -1.0))
    ordered = jax.tree.map(lambda first, others: jnp.concatenate([first, others[:block_count - 1]], axis=0), empty, terms)
    states = link_states(initial, lax.associative_scan(link_states, ordered))
    query_blocks = queries.reshape(block_count, WINDOW, head_count, head_width)
    query_feat_blocks = query_features.reshape(block_count, WINDOW, head_count, feat_width)
    own_segment = query_segment.reshape(block_count, WINDOW)
    pair_keys = jnp.concatenate([key_blocks[:-1], key_blocks[1:]], axis=1)
    pair_values = jnp.concatenate([value_blocks[:-1], value_blocks[1:]], axis=1)
    pair_features = jnp.concatenate([feature_blocks[:-1], feature_blocks[1:]], axis=1)
    pair_segment = jnp.concatenate([segment_blocks[:-1], segment_blocks[1:]], axis=1)
    places = jnp.arange(WINDOW)
    slots = jnp.arange(2 * WINDOW)
    earlier_block = slots[None, :] < WINDOW
    offsets = slots[None, :] % WINDOW
    inside = jnp.where(earlier_block, offsets > places[:, None], offsets <= places[:, None])
    linear = earlier_block & (offsets <= places[:, None])
    matched = own_segment[:, :, None] == pair_segment[:, None, :]
    window_mask = (inside[None] & matched)[:, None]
    linear_mask = jnp.where(linear[None] & matched, 1.0, 0.0)[:, None]
    scores = jnp.einsum('nqhe,nkhe->nhqk', query_blocks, pair_keys, precision=highest) * head_width ** (-0.5)
    peak = lax.optimization_barrier(jnp.max(jnp.where(window_mask, scores, -1e+30), axis=-1, keepdims=True))
    weights = jnp.where(window_mask, jnp.exp(jnp.where(window_mask, scores - peak, 0.0)), 0.0)
    linear_weights = jnp.einsum('nqhf,nkhf->nhqk', query_feat_blocks, pair_features, precision=highest) * linear_mask
    carried = jnp.where(own_segment == states[2][:, 0, 0, 0][:, None], 1.0, 0.0)
    state_num = jnp.einsum('nqhf,nhfe->nqhe', query_feat_blocks, states[0], precision=highest) * carried[:, :, None, None]
    state_den = jnp.einsum('nqhf,nhf->nqh', query_feat_blocks, states[1], precision=highest) * carried[:, :, None]
    damping = jnp.exp(-jnp.transpose(peak[..., 0], (0, 2, 1)))
    numerator = jnp.einsum('nhqk,nkhe->nqhe', weights, pair_values, precision=highest) + damping[..., None] * (jnp.einsum('nhqk,nkhe->nqhe', linear_weights, pair_values, precision=highest) + state_num)
    denominator = jnp.transpose(lax.optimization_barrier(jnp.sum(weights, axis=-1)), (0, 2, 1)) + damping * (jnp.transpose(lax.optimization_barrier(jnp.sum(linear_weights, axis=-1)), (0, 2, 1)) + state_den)
    return (numerator / denominator[..., None]).reshape(length, head_count * head_width)

def layer_row(row_in, row_segment, weights):
    attn_gain, ffn_gain, query_weight, key_weight, value_weight, output_weight, query_down, query_lift, key_down, key_lift, value_down, value_lift, output_down, output_lift, feature_maps, gate_weight, up_weight, down_weight = weights
    length = row_in.shape[0]
    normed = low(rms_norm(row_in, attn_gain))
    queries = low_back(matmul(normed, query_weight) + matmul(matmul(normed, query_down), query_lift))
    queries = queries.reshape(length, HEADS, HD)
    key_rows = (matmul(normed, key_weight) + matmul(matmul(normed, key_down), key_lift)).reshape(length, KV, HD)
    value_rows = (matmul(normed, value_weight) + matmul(matmul(normed, value_down), value_lift)).reshape(length, KV, HD)
    key_heads = low_back(jnp.repeat(key_rows, HEADS // KV, axis=1))
    value_heads = low_back(jnp.repeat(value_rows, HEADS // KV, axis=1))
    halo_zeros = jnp.zeros((WINDOW, HEADS, HD), jnp.float32)
    seg_float = row_segment.astype(jnp.float32)
    key_segment = jnp.concatenate([jnp.full((WINDOW,), -1.0, jnp.float32), seg_float])
    initial = (jnp.zeros((HEADS, 2 * HD, HD), jnp.float32), jnp.zeros((HEADS, 2 * HD), jnp.float32), jnp.full((1, 1, 1), -1.0, jnp.float32))
    mixed = low(window_attend(queries, jnp.concatenate([halo_zeros, key_heads], axis=0), jnp.concatenate([halo_zeros, value_heads], axis=0), key_segment, seg_float, feature_maps, initial))
    branch = low_back(matmul(mixed, output_weight) + matmul(matmul(mixed, output_down), output_lift))
    middle = row_in + branch
    ffn_rows = low(rms_norm(middle, ffn_gain))
    gate_pre = low_back(matmul(ffn_rows, gate_weight))
    upper_pre = low_back(matmul(ffn_rows, up_weight))
    hidden = low(jax.nn.silu(gate_pre) * upper_pre)
    return middle + low_back(matmul(hidden, down_weight))

def reference(inputs, segment_ids, cotangent, attn_gain, ffn_gain, query_weight, key_weight, value_weight, output_weight, query_down, query_lift, key_down, key_lift, value_down, value_lift, output_down, output_lift, feature_maps, gate_weight, up_weight, down_weight):
    params = tuple((weight.astype(jnp.float32) for weight in (attn_gain, ffn_gain, query_weight, key_weight, value_weight, output_weight, query_down, query_lift, key_down, key_lift, value_down, value_lift, output_down, output_lift, feature_maps, gate_weight, up_weight, down_weight)))
    row_total = inputs.shape[0] * inputs.shape[1]
    flat_segment = segment_ids.reshape(row_total, SEQ_LEN)
    flat_inputs = inputs.astype(jnp.float32).reshape(row_total, SEQ_LEN, D)

    def forward(rows_in, *weights):
        checked = jax.checkpoint(layer_row)
        return lax.map(lambda row_pair: checked(row_pair[0], row_pair[1], weights), (rows_in, flat_segment))
    result, pullback = jax.vjp(forward, flat_inputs, *params)
    grads = pullback(cotangent.astype(jnp.float32).reshape(row_total, SEQ_LEN, D))
    return (result.reshape(inputs.shape).astype(jnp.bfloat16), grads[0].reshape(inputs.shape), grads[1], grads[2], grads[3], grads[4], grads[5], grads[6], grads[7], grads[8], grads[9], grads[10], grads[11], grads[12], grads[13], grads[14], grads[15], grads[16], grads[17], grads[18])
```

```python
import functools

import jax
import jax.numpy as jnp
from jax import lax
from jax.experimental import pallas as pl
from jax.experimental.pallas import tpu as pltpu
from jax.sharding import PartitionSpec as P

HEADS = 32
KV = 8
HD = 64
WINDOW = 64
CHUNK = 2 * WINDOW
FEATS = 2 * HD
AUG = HD + 16
F32 = jnp.float32
BF16 = jnp.bfloat16


def mm(left, right, left_dim=1, right_dim=0):
    return lax.dot_general(
        left, right, (((left_dim,), (right_dim,)), ((), ())), preferred_element_type=F32
    )


def chunk_masks(chunk, seg_row, seg_own, seg_prev):
    place = lax.broadcasted_iota(jnp.int32, (CHUNK, CHUNK), 1)
    key = lax.broadcasted_iota(jnp.int32, (CHUNK, CHUNK), 0)
    same_own = seg_own == seg_row
    same_prev = (seg_prev - jnp.where(chunk == 0, 100, 0)) == seg_row
    far = -1e30
    bias_own = jnp.where(same_own & (key <= place) & (key > place - WINDOW), 0.0, far)
    bias_prev = jnp.where(same_prev & (key > place + WINDOW), 0.0, far)
    linear_prev = jnp.where(same_prev & (key <= place + WINDOW), 1.0, 0.0)
    linear_own = jnp.where(same_own & (key <= place - WINDOW), 1.0, 0.0)
    return bias_prev[WINDOW:], bias_own, linear_prev, linear_own[:WINDOW]


def with_ones(values):
    return jnp.concatenate([values, jnp.ones((AUG - HD, CHUNK), values.dtype)], axis=0)


def features_of(vectors, maps_t):
    logits = mm(maps_t, vectors)
    high = jnp.exp(logits - jnp.max(logits, axis=0, keepdims=True))
    low = jnp.exp(jnp.min(logits, axis=0, keepdims=True) - logits)
    high = high * (1.0 / jnp.sum(high, axis=0, keepdims=True))
    low = low * (1.0 / jnp.sum(low, axis=0, keepdims=True))
    return jnp.concatenate([high, low], axis=0)


def features_back(features, grad):
    product = features * grad
    high = product[:HD] - features[:HD] * jnp.sum(product[:HD], axis=0, keepdims=True)
    low = product[HD:] - features[HD:] * jnp.sum(product[HD:], axis=0, keepdims=True)
    return high - low


def forward_kernel(
    last_ref, order_ref, seg_row_ref, seg_own_ref, seg_prev_ref,
    q_ref, kt_ref, k_ref, kp_ref, vt_ref, vtp_ref, maps_t_ref,
    mixed_ref, peak_ref, den_ref, fq_ref, fkt_ref, fk_ref, state_out_ref,
    state_ref, fk_prev_ref,
):
    chunk = pl.program_id(0)
    head_count = fq_ref.shape[0]
    per_key = head_count // k_ref.shape[0]

    @pl.when(chunk == 0)
    def _():
        state_ref[...] = jnp.zeros_like(state_ref)
        fk_prev_ref[...] = jnp.zeros_like(fk_prev_ref)

    seg_row = seg_row_ref[...]
    bias_prev, bias_own, linear_prev, linear_own = chunk_masks(
        chunk, seg_row, seg_own_ref[...], seg_prev_ref[...]
    )
    tag_state = jnp.where(chunk >= 2, last_ref[jnp.maximum(chunk - 2, 0)], -1)
    tag_prev = jnp.where(chunk >= 1, last_ref[jnp.maximum(chunk - 1, 0)], -2)
    carried = jnp.where(seg_row == tag_state, 1.0, 0.0)
    joined = jnp.where(tag_state == tag_prev, 1.0, 0.0)
    keep_prev = jnp.where(seg_prev_ref[...] == tag_prev, 1.0, 0.0).astype(BF16)
    for head in range(head_count):
        group = head // per_key
        rows = slice(head * HD, (head + 1) * HD)
        key_rows = slice(group * HD, (group + 1) * HD)
        query = q_ref[rows, :]
        maps_t = maps_t_ref[head]
        feat_q = features_of(query, maps_t)
        feat_kt = features_of(kt_ref[key_rows, :], maps_t)
        fq_ref[head] = feat_q.astype(BF16)
        fkt_ref[head] = feat_kt.astype(BF16)
        feat_k = jnp.transpose(feat_kt).astype(BF16)
        fk_ref[head] = feat_k
        scaled = query * jnp.asarray(HD**-0.5, BF16)
        score_prev = mm(kp_ref[group, WINDOW:, :], scaled) + bias_prev
        score_own = mm(k_ref[group], scaled) + bias_own
        peak = jnp.maximum(
            jnp.max(score_prev, axis=0, keepdims=True), jnp.max(score_own, axis=0, keepdims=True)
        )
        weight_prev = jnp.exp(score_prev - peak)
        weight_own = jnp.exp(score_own - peak)
        damped = feat_q * jnp.exp(-peak)
        damped_low = damped.astype(BF16)
        fk_prev = fk_prev_ref[head]
        lin_prev = mm(fk_prev, damped_low) * linear_prev
        lin_own = mm(feat_k[:WINDOW], damped_low) * linear_own
        all_prev = jnp.concatenate([lin_prev[:WINDOW], lin_prev[WINDOW:] + weight_prev], axis=0)
        all_own = jnp.concatenate([lin_own + weight_own[:WINDOW], weight_own[WINDOW:]], axis=0)
        value_prev = with_ones(vtp_ref[key_rows, :])
        state = state_ref[head]
        state_low = state.astype(BF16)
        state_out_ref[0, head] = state_low
        total = (
            mm(value_prev, all_prev.astype(BF16))
            + mm(with_ones(vt_ref[key_rows, :]), all_own.astype(BF16))
            + mm(state_low, (damped * carried).astype(BF16))
        )
        den = total[HD : HD + 1]
        mixed_ref[rows, :] = (total[:HD] * (1.0 / den)).astype(BF16)
        peak_ref[head : head + 1, :] = peak
        den_ref[head : head + 1, :] = den
        state_ref[head] = state * joined + mm(value_prev, fk_prev * keep_prev)
        fk_prev_ref[head] = feat_k


def backward_kernel(
    last_ref, order_ref, seg_row_ref, seg_own_ref, seg_prev_ref,
    q_ref, kt_ref, ktp_ref, k_ref, kp_ref, v_ref, vp_ref, vtp_ref, maps_ref, lift_ref,
    mixed_ref, grad_ref, peak_ref, den_ref, fq_ref, fkt_ref, fktp_ref, fk_ref, fkp_ref, state_ref,
    grows_ref, gmaps_ref,
    gstate_ref, cphi_ref, ck_ref, cv_ref,
):
    step = pl.program_id(0)
    chunk = pl.num_programs(0) - 1 - step
    head_count = fq_ref.shape[0]
    group_count = k_ref.shape[0]
    per_key = head_count // group_count

    @pl.when(step == 0)
    def _():
        gstate_ref[...] = jnp.zeros_like(gstate_ref)
        cphi_ref[...] = jnp.zeros_like(cphi_ref)
        ck_ref[...] = jnp.zeros_like(ck_ref)
        cv_ref[...] = jnp.zeros_like(cv_ref)
        gmaps_ref[...] = jnp.zeros_like(gmaps_ref)

    seg_row = seg_row_ref[...]
    bias_prev, bias_own, linear_prev, linear_own = chunk_masks(
        chunk, seg_row, seg_own_ref[...], seg_prev_ref[...]
    )
    tag_state = jnp.where(chunk >= 2, last_ref[jnp.maximum(chunk - 2, 0)], -1)
    tag_prev = jnp.where(chunk >= 1, last_ref[jnp.maximum(chunk - 1, 0)], -2)
    carried = jnp.where(seg_row == tag_state, 1.0, 0.0)
    joined = jnp.where(tag_state == tag_prev, 1.0, 0.0)
    keep_col = jnp.where(seg_prev_ref[...] == tag_prev, 1.0, 0.0)
    keep_prev = jnp.transpose(jnp.broadcast_to(keep_col, (CHUNK, CHUNK)))[:1]
    scale = HD**-0.5
    none = jnp.zeros((WINDOW, CHUNK), F32)
    for group in range(group_count):
        key_rows = slice(group * HD, (group + 1) * HD)
        key_t = kt_ref[key_rows, :]
        value_prev = with_ones(vtp_ref[key_rows, :])
        own_k = ck_ref[group]
        own_v = cv_ref[group]
        next_k = None
        next_v = None
        for head in range(group * per_key, (group + 1) * per_key):
            rows = slice(head * HD, (head + 1) * HD)
            query = q_ref[rows, :]
            scaled = query * jnp.asarray(scale, BF16)
            peak = peak_ref[head : head + 1, :]
            den = den_ref[head : head + 1, :]
            weight_prev = jnp.exp(mm(kp_ref[group, WINDOW:, :], scaled) + bias_prev - peak)
            weight_own = jnp.exp(mm(k_ref[group], scaled) + bias_own - peak)
            damp = jnp.exp(-peak)
            feat_q = fq_ref[head].astype(F32)
            damped = feat_q * damp
            damped_low = damped.astype(BF16)
            carried_low = (damped * carried).astype(BF16)
            lin_prev = mm(fkp_ref[head], damped_low) * linear_prev
            lin_own = mm(fk_ref[head, :WINDOW, :], damped_low) * linear_own
            all_prev = jnp.concatenate([lin_prev[:WINDOW], lin_prev[WINDOW:] + weight_prev], axis=0)
            all_own = jnp.concatenate([lin_own + weight_own[:WINDOW], weight_own[WINDOW:]], axis=0)
            grad = grad_ref[rows, :].astype(F32)
            dnum = grad * (1.0 / den)
            dden = -jnp.sum(dnum * mixed_ref[rows, :].astype(F32), axis=0, keepdims=True)
            dnum_low = dnum.astype(BF16)
            dtotal = jnp.concatenate(
                [dnum, dden, jnp.zeros((AUG - HD - 1, CHUNK), F32)], axis=0
            ).astype(BF16)
            dall_prev = mm(vp_ref[group], dnum_low) + dden
            dall_own = mm(v_ref[group], dnum_low) + dden
            dscore_prev = jnp.concatenate([none, weight_prev * dall_prev[WINDOW:]], axis=0).astype(BF16)
            dscore_own = (weight_own * dall_own).astype(BF16)
            dlin_prev = (linear_prev * dall_prev).astype(BF16)
            dlin_own = jnp.concatenate([linear_own * dall_own[:WINDOW], none], axis=0).astype(BF16)
            gstate = gstate_ref[head]
            gstate_low = gstate.astype(BF16)
            ddamped = (
                mm(fktp_ref[head], dlin_prev)
                + mm(fkt_ref[head], dlin_own)
                + carried * mm(state_ref[0, head], dtotal, 0, 0)
            )
            dlogit_q = features_back(feat_q, ddamped * damp).astype(BF16)
            maps = maps_ref[head]
            grad_q = (
                mm(ktp_ref[key_rows, :], dscore_prev) + mm(key_t, dscore_own)
            ) * scale + mm(maps, dlogit_q)
            grows_ref[rows, :] = grad_q.astype(BF16)
            dphi_own = cphi_ref[head] + mm(damped_low, dlin_own, 1, 1)
            cphi_ref[head] = (
                mm(damped_low, dlin_prev, 1, 1) + mm(gstate_low, value_prev, 0, 0) * keep_prev
            )
            dlogit_k = features_back(fkt_ref[head].astype(F32), dphi_own).astype(BF16)
            gmaps_ref[head] += mm(dlogit_q, query, 1, 1) + mm(dlogit_k, key_t, 1, 1)
            own_k += mm(scaled, dscore_own, 1, 1) + mm(maps, dlogit_k)
            part_k = mm(scaled, dscore_prev, 1, 1)
            own_v += mm(dnum_low, all_own.astype(BF16), 1, 1)
            part_v = (
                mm(dnum_low, all_prev.astype(BF16), 1, 1)
                + mm(gstate_low[:HD], fktp_ref[head]) * keep_prev
            )
            next_k = part_k if next_k is None else next_k + part_k
            next_v = part_v if next_v is None else next_v + part_v
            gstate_ref[head] = gstate * joined + mm(dtotal, carried_low, 1, 1)
        key_start = (head_count + group) * HD
        value_start = (head_count + group_count + group) * HD
        grows_ref[key_start : key_start + HD, :] = own_k.astype(BF16)
        grows_ref[value_start : value_start + HD, :] = own_v.astype(BF16)
        ck_ref[group] = next_k
        cv_ref[group] = next_v
    width = lift_ref.shape[1]
    grows_ref[width:, :] = mm(lift_ref[...], grows_ref[:width, :]).astype(BF16)


def attend_forward(last, order, seg_row, seg_col, rows, natural, maps_t):
    heads = maps_t.shape[0]
    groups, length = natural.shape[0] // 2, natural.shape[1]
    chunks = length // CHUNK
    first = heads // groups

    def before(c):
        return jnp.maximum(c - 1, 0)

    def spec(count, block, shift):
        return pl.BlockSpec((count * HD, CHUNK), lambda c, last, order: (block, order[shift(c)]))

    def nat(block, shift):
        return pl.BlockSpec((groups, CHUNK, HD), lambda c, last, order: (block, order[shift(c)], 0))

    def here(c):
        return c

    stat = pl.BlockSpec((heads, CHUNK), lambda c, last, order: (0, c))
    feat_t = pl.BlockSpec((heads, FEATS, CHUNK), lambda c, last, order: (0, 0, c))
    return pl.pallas_call(
        forward_kernel,
        grid_spec=pltpu.PrefetchScalarGridSpec(
            num_scalar_prefetch=2,
            grid=(chunks,),
            in_specs=[
                pl.BlockSpec((1, CHUNK), lambda c, last, order: (0, c)),
                pl.BlockSpec((CHUNK, 1), lambda c, last, order: (c, 0)),
                pl.BlockSpec((CHUNK, 1), lambda c, last, order: (before(c), 0)),
                spec(heads, 0, here),
                spec(groups, first, here),
                nat(0, here),
                nat(0, before),
                spec(groups, first + 1, here),
                spec(groups, first + 1, before),
                pl.BlockSpec((heads, HD, HD), lambda c, last, order: (0, 0, 0)),
            ],
            out_specs=[
                spec(heads, 0, here), stat, stat,
                feat_t, feat_t,
                pl.BlockSpec((heads, CHUNK, FEATS), lambda c, last, order: (0, c, 0)),
                pl.BlockSpec((1, heads, AUG, FEATS), lambda c, last, order: (c, 0, 0, 0)),
            ],
            scratch_shapes=[
                pltpu.VMEM((heads, AUG, FEATS), F32),
                pltpu.VMEM((heads, CHUNK, FEATS), BF16),
            ],
        ),
        out_shape=[
            jax.ShapeDtypeStruct((heads * HD, length), BF16),
            jax.ShapeDtypeStruct((heads, length), F32),
            jax.ShapeDtypeStruct((heads, length), F32),
            jax.ShapeDtypeStruct((heads, FEATS, length), BF16),
            jax.ShapeDtypeStruct((heads, FEATS, length), BF16),
            jax.ShapeDtypeStruct((heads, length, FEATS), BF16),
            jax.ShapeDtypeStruct((chunks, heads, AUG, FEATS), BF16),
        ],
        compiler_params=pltpu.CompilerParams(
            dimension_semantics=("arbitrary",), vmem_limit_bytes=32 * 2**20
        ),
        cost_estimate=pl.CostEstimate(
            flops=heads * length * 3600000, bytes_accessed=heads * length * 1600, transcendentals=0
        ),
        name="attend_forward",
    )(last, order, seg_row, seg_col, seg_col, rows, rows, natural, natural, rows, rows, maps_t)


def attend_backward(last, order, seg_row, seg_col, rows, natural, maps, lift, saved, grad):
    mixed, peak, den, fq, fkt, fk, states = saved
    heads = maps.shape[0]
    groups, length = natural.shape[0] // 2, natural.shape[1]
    chunks = length // CHUNK
    first = heads // groups
    height = lift.shape[0] + lift.shape[1]

    def here(s):
        return chunks - 1 - s

    def before(s):
        return jnp.maximum(chunks - 2 - s, 0)

    def spec(count, block, shift):
        return pl.BlockSpec((count * HD, CHUNK), lambda s, last, order: (block, order[shift(s)]))

    def nat(block, shift):
        return pl.BlockSpec((groups, CHUNK, HD), lambda s, last, order: (block, order[shift(s)], 0))

    def feat_t(shift):
        return pl.BlockSpec((heads, FEATS, CHUNK), lambda s, last, order: (0, 0, shift(s)))

    def feat(shift):
        return pl.BlockSpec((heads, CHUNK, FEATS), lambda s, last, order: (0, shift(s), 0))

    stat = pl.BlockSpec((heads, CHUNK), lambda s, last, order: (0, here(s)))
    whole = pl.BlockSpec((heads, HD, HD), lambda s, last, order: (0, 0, 0))
    return pl.pallas_call(
        backward_kernel,
        grid_spec=pltpu.PrefetchScalarGridSpec(
            num_scalar_prefetch=2,
            grid=(chunks,),
            in_specs=[
                pl.BlockSpec((1, CHUNK), lambda s, last, order: (0, here(s))),
                pl.BlockSpec((CHUNK, 1), lambda s, last, order: (here(s), 0)),
                pl.BlockSpec((CHUNK, 1), lambda s, last, order: (before(s), 0)),
                spec(heads, 0, here),
                spec(groups, first, here), spec(groups, first, before),
                nat(0, here), nat(0, before),
                nat(1, here), nat(1, before),
                spec(groups, first + 1, before),
                whole,
                pl.BlockSpec(lift.shape, lambda s, last, order: (0, 0)),
                spec(heads, 0, here), spec(heads, 0, here), stat, stat,
                feat_t(here), feat_t(here), feat_t(before), feat(here), feat(before),
                pl.BlockSpec((1, heads, AUG, FEATS), lambda s, last, order: (here(s), 0, 0, 0)),
            ],
            out_specs=[
                pl.BlockSpec((height, CHUNK), lambda s, last, order: (0, order[here(s)])),
                whole,
            ],
            scratch_shapes=[
                pltpu.VMEM((heads, AUG, FEATS), F32),
                pltpu.VMEM((heads, FEATS, CHUNK), F32),
                pltpu.VMEM((groups, HD, CHUNK), F32),
                pltpu.VMEM((groups, HD, CHUNK), F32),
            ],
        ),
        out_shape=[
            jax.ShapeDtypeStruct((height, length), BF16),
            jax.ShapeDtypeStruct((heads, HD, HD), F32),
        ],
        compiler_params=pltpu.CompilerParams(
            dimension_semantics=("arbitrary",), vmem_limit_bytes=32 * 2**20
        ),
        cost_estimate=pl.CostEstimate(
            flops=heads * length * 7200000, bytes_accessed=heads * length * 2400, transcendentals=0
        ),
        name="attend_backward",
    )(
        last, order, seg_row, seg_col, seg_col, rows, rows, rows, natural, natural, natural, natural,
        rows, maps, lift, mixed, grad, peak, den, fq, fkt, fkt, fk, fk, states,
    )


ALL = ("rows", "heads", "seq")
SWAP = [(0, 1), (1, 0)]
LOWS = 32


def over_x(value):
    return lax.ppermute(value, "rows", SWAP)


def over_c(value):
    return lax.ppermute(value, "seq", SWAP)


def after(value, *others):
    return lax.optimization_barrier((value, others))[0]


def body(
    inputs,
    segment_ids,
    cotangent,
    attn_gain,
    ffn_gain,
    query_weight,
    key_weight,
    value_weight,
    output_weight,
    query_down,
    query_lift,
    key_down,
    key_lift,
    value_down,
    value_lift,
    output_down,
    output_lift,
    feature_maps,
    gate_weight,
    up_weight,
    down_weight,
):
    heads_size = lax.axis_size("heads")
    depth = inputs.shape[0]
    wide = heads_size // depth
    per = HEADS // heads_size
    near = depth // 2
    block_rows = per * HD
    rank = query_down.shape[1]
    width = inputs.shape[-1]
    half = width // 2
    share = inputs.shape[3]
    held = depth * share
    head_index = lax.axis_index("heads")
    x = lax.axis_index("rows")
    c = lax.axis_index("seq")
    z = head_index // wide
    y = head_index % wide
    kv_pick = y * per // (HEADS // KV)
    kv_depth = KV // depth

    def over_y(value, k):
        return lax.ppermute(
            value,
            "heads",
            [(a * wide + b, a * wide + (b ^ k)) for a in range(depth) for b in range(wide)],
        )

    def over_z(value, k=1):
        return lax.ppermute(
            value,
            "heads",
            [(a * wide + b, (a + k) % depth * wide + b) for a in range(depth) for b in range(wide)],
        )

    def trade_z(value):
        groups = [[a * wide + b for a in range(depth)] for b in range(wide)]
        return lax.all_to_all(
            value, "heads", split_axis=0, concat_axis=0, tiled=True, axis_index_groups=groups
        )

    def trade_c(value, split, concat):
        return lax.all_to_all(value, "seq", split_axis=split, concat_axis=concat, tiled=True)

    def turn(value, axis):
        return jnp.stack(
            [lax.dynamic_index_in_dim(value, (z - j) % depth, axis, False) for j in range(depth)],
            axis,
        )

    def in_order(kept, moved, axis):
        return jnp.where(
            c == 0,
            jnp.concatenate([kept, moved], axis=axis),
            jnp.concatenate([moved, kept], axis=axis),
        )

    def rotate(value):
        return jnp.where(
            x == 1, jnp.concatenate([value[..., half:], value[..., :half]], axis=-1), value
        )

    def ring(block):
        blocks = [block]
        for _ in range(depth - 1):
            blocks.append(over_z(blocks[-1]))
        return blocks

    def shift_sum(blocks):
        total = blocks[0].astype(F32)
        for k in range(1, depth):
            total = total + over_z(blocks[depth - k], k).astype(F32)
        return total

    def shifts(block):
        return [block] + [over_z(block, k) for k in range(1, depth)]

    def ring_sum(blocks):
        total = blocks[1]
        for j in list(range(2, depth)) + [0]:
            moved = over_z(total)
            total = (moved.astype(F32) + blocks[j].astype(F32)).astype(
                F32 if j == 0 else blocks[1].dtype
            )
        return total

    def gather_tokens(value):
        chip = jnp.concatenate([value, over_c(value)], axis=0)
        others = []
        for k in range(1, wide):
            moved = over_y(value, k)
            others += [moved, over_c(moved)]
        return chip, jnp.concatenate(others, axis=0)

    def reduce_tokens(make_chip, make_others, waits=()):
        others = make_others()
        sent = []
        arrived = []
        for k in range(1, wide):
            start = (k - 1) * 2 * held
            mine = others[start : start + held]
            moved = over_c(others[start + held : start + 2 * held])
            sent.append((mine.astype(F32) + moved.astype(F32)).astype(BF16))
            arrived.append(over_y(sent[-1], k))
        chip = make_chip()
        total = chip[:held].astype(F32) + over_c(chip[held:]).astype(F32)
        if waits:
            arrived = [after(piece, *waits) for piece in arrived]
        for piece in arrived:
            total = total + piece.astype(F32)
        return total, sent

    def rms(values):
        return lax.rsqrt(jnp.mean(values * values, axis=-1, keepdims=True) + 1e-05)

    def norm_back(values, gain, scale, grad):
        unit = values * scale
        scaled = grad * gain
        return (
            scale * (scaled - unit * jnp.mean(scaled * unit, axis=-1, keepdims=True)),
            jnp.sum(grad * unit, axis=0),
        )

    small = (
        attn_gain, ffn_gain, query_down, key_down, value_down, output_lift,
        query_lift, key_lift, value_lift, output_down, feature_maps,
    )
    packed = jnp.concatenate([piece.reshape(-1) for piece in small])
    near_small = in_order(packed[None], over_c(packed)[None], 0)[None]
    step = 1
    while step < wide:
        moved = over_y(near_small, step)
        near_small = jnp.where(
            (y // step) % 2 == 0,
            jnp.concatenate([near_small, moved], axis=0),
            jnp.concatenate([moved, near_small], axis=0),
        )
        step *= 2
    layer_in = rotate(trade_z(after(inputs[:, 0, 0], near_small)).reshape(held, width)).astype(F32)
    near_small = turn(jnp.stack(shifts(near_small)), 0).reshape(heads_size, 2, -1)
    far_small = over_x(near_small)
    turned_small = jnp.stack([near_small, far_small])
    spread_small = jnp.where(x == 0, turned_small, jnp.stack([far_small, near_small]))
    starts = [0]
    for piece in small:
        starts.append(starts[-1] + piece.size)

    def piece(index, turned):
        source = turned_small if turned else spread_small
        return source[..., starts[index] : starts[index + 1]].reshape(
            (2, heads_size, 2) + small[index].shape
        )

    def pick_heads(value):
        value = value.reshape((depth, wide) + value.shape[1:])
        value = lax.dynamic_index_in_dim(value, y, 1, False)
        return lax.dynamic_slice_in_dim(value, c * near, near, 0)

    gain_one = piece(0, True).reshape(width).astype(F32)
    gain_two = piece(1, True).reshape(width).astype(F32)
    downs = [piece(i, True).reshape(width, rank) for i in (2, 3, 4)]
    downs_t = jnp.concatenate(downs + [jnp.zeros((width, LOWS - 3 * rank), BF16)], axis=1).T
    out_lift = jnp.moveaxis(piece(5, True), 3, 0).reshape(rank, width)
    query_raise = jnp.transpose(
        piece(6, False).reshape(2, heads_size, 2, -1, per, HD), (1, 4, 0, 2, 3, 5)
    ).reshape(heads_size, per, rank, HD)
    query_raise = jnp.moveaxis(pick_heads(query_raise), 2, 0).reshape(rank, -1)

    def pick_keys(value):
        value = value.reshape(value.shape[0], depth, kv_depth, HD)
        value = lax.dynamic_index_in_dim(value, kv_pick, 2, False)
        return lax.dynamic_slice_in_dim(value, c * near, near, 1).reshape(value.shape[0], -1)

    def pick_near(value):
        value = value.reshape(value.shape[0], depth, kv_depth, HD)
        value = lax.dynamic_index_in_dim(value, kv_pick, 2, False).reshape(value.shape[0], -1).T
        rows_near = near * HD
        kept = lax.dynamic_slice_in_dim(value, c * rows_near, rows_near, 0)
        return in_order(kept, over_c(lax.dynamic_slice_in_dim(value, (1 - c) * rows_near, rows_near, 0)), 1)

    key_raise = pick_keys(piece(7, False)[:, 0].reshape(rank, KV * HD))
    value_raise = pick_keys(piece(8, False)[:, 0].reshape(rank, KV * HD))
    out_down = jnp.transpose(
        piece(9, False).reshape(2, heads_size, 2, per, HD, -1), (1, 3, 4, 0, 2, 5)
    ).reshape(heads_size, per, HD, rank)
    out_down = pick_heads(out_down).reshape(-1, rank)
    maps = jnp.transpose(piece(10, False), (1, 3, 0, 2, 4, 5)).reshape(heads_size, per, HD, HD)
    maps = pick_heads(maps).reshape(-1, HD, HD)
    query_rows = near * block_rows
    key_rows = near * HD
    lift = jnp.concatenate(
        [
            jnp.pad(query_raise, ((0, 0), (0, 2 * key_rows))),
            jnp.pad(key_raise, ((0, 0), (query_rows, key_rows))),
            jnp.pad(value_raise, ((0, 0), (query_rows + key_rows, 0))),
            jnp.zeros((LOWS - 3 * rank, query_rows + 2 * key_rows), BF16),
        ],
        axis=0,
    )
    row_count = query_rows + 2 * key_rows

    def spread_heads(block):
        blocks = turn(jnp.stack(shifts(block)), 0)
        kept = lax.dynamic_slice_in_dim(blocks, c * near, near, 0)
        moved = over_c(lax.dynamic_slice_in_dim(blocks, (1 - c) * near, near, 0))
        return in_order(kept, moved, 2).reshape(near * block_rows, half)

    query_own = spread_heads(query_weight.T)
    kv_own = jnp.concatenate([pick_near(key_weight), pick_near(value_weight)], axis=0)
    both_own = jnp.concatenate([query_own, kv_own], axis=0)
    both = jnp.concatenate([both_own, over_x(both_own)], axis=1)
    project = jnp.concatenate([both, downs_t], axis=0)

    pack_one = jnp.stack([after(gate_weight, near_small).T, after(up_weight, near_small).T])
    own_one = [trade_c(pack_one, 1, 2)]
    own_two = [trade_c(after(down_weight, near_small), 0, 1)]
    other_one = [over_x(own_one[0])]
    other_two = [over_x(own_two[0])]
    project = after(project, other_one[0])

    def next_block(*waits):
        one, two = own_one[-1], own_two[-1]
        if waits:
            one, two = after(one, *waits), after(two, *waits)
        own_one.append(over_z(one))
        own_two.append(over_z(two))

    def next_half():
        place = len(other_one)
        other_one.append(over_x(own_one[place]))
        other_two.append(over_x(own_two[place]))

    next_block(layer_in)

    scale_one = rms(layer_in)
    normed = gather_tokens((layer_in * scale_one * gain_one).astype(BF16))

    def project_rows(tokens):
        flat = mm(project, tokens, 1, 1)
        low = flat[row_count:].astype(BF16)
        return (flat[:row_count] + mm(lift, low, 0, 0)).astype(BF16), low

    pieces = [project_rows(tokens) for tokens in normed]
    rows = jnp.concatenate([piece_rows for piece_rows, _ in pieces], axis=1)
    low_rows = jnp.concatenate([low for _, low in pieces], axis=1)

    def flips(value, y_axis, c_axis):
        value = jnp.where(c == 1, jnp.flip(value, c_axis), value)
        step = 1
        while step < wide:
            shape = value.shape
            apart = value.reshape(
                shape[:y_axis] + (wide // (2 * step), 2, step) + shape[y_axis + 1 :]
            )
            value = jnp.where((y // step) % 2 == 1, jnp.flip(apart, y_axis + 1), apart).reshape(shape)
            step *= 2
        return value

    length = wide * 2 * held
    chunks = length // CHUNK
    if share % CHUNK == 0:
        across = share // CHUNK
        numbers = jnp.arange(chunks, dtype=jnp.int32).reshape(2, depth, wide, across)
        order = flips(
            jnp.arange(chunks, dtype=jnp.int32).reshape(wide, 2, depth, across), 0, 1
        )
        order = jnp.transpose(order, (1, 2, 0, 3)).reshape(-1)

        def to_natural(value):
            return value

        from_natural = to_natural
    else:
        order = jnp.arange(chunks, dtype=jnp.int32)

        def to_natural(value):
            apart = flips(value.reshape(-1, wide, 2, depth, share), 1, 2)
            return jnp.transpose(apart, (0, 2, 3, 1, 4)).reshape(value.shape)

        def from_natural(value):
            apart = jnp.transpose(value.reshape(-1, 2, depth, wide, share), (0, 3, 1, 2, 4))
            return flips(apart, 1, 2).reshape(value.shape)

    segment = lax.dynamic_index_in_dim(segment_ids[:, 0], z, 0, False)
    last = segment.reshape(chunks, CHUNK)[:, -1]
    seg_row = segment[None, :]
    seg_col = segment[:, None]
    rows_nat = to_natural(rows)
    key_nat = jnp.transpose(rows_nat[query_rows:].reshape(-1, HD, length), (0, 2, 1))
    key_nat = after(key_nat, own_one[1], own_two[1])
    next_block()
    next_half()
    saved = attend_forward(
        last, order, seg_row, seg_col, rows_nat, key_nat, jnp.transpose(maps, (0, 2, 1))
    )
    mixed = from_natural(saved[0])

    out_own = spread_heads(after(output_weight, rows))
    out_mat = jnp.concatenate([out_own, over_x(out_own)], axis=1)
    rank_rows = mm(out_down, mixed, 0, 0).astype(BF16)
    split = 2 * held

    def branch(part, *waits):
        def make():
            rows_in = after(mixed[:, part], *waits)
            return (mm(rows_in, out_mat, 0, 0) + mm(rank_rows[:, part], out_lift, 0, 0)).astype(BF16)

        return make

    chip_part, other_part = slice(0, split), slice(split, length)
    branch_sum, _ = reduce_tokens(
        branch(chip_part, own_one[2], own_two[2], other_one[1], other_two[1]), branch(other_part)
    )
    middle = layer_in + branch_sum
    next_block()
    next_half()
    next_half()

    scale_two = rms(middle)
    ffn_rows = gather_tokens((middle * scale_two * gain_two).astype(BF16))
    ffn_rows = (ffn_rows[0], after(ffn_rows[1], own_one[3], other_one[2]))
    grad_out = rotate(
        trade_z(after(cotangent[:, 0, 0], own_two[3])).reshape(held, width)
    )
    grads = gather_tokens(grad_out)
    own_gate, own_up = [jnp.concatenate([b[i] for b in own_one], axis=0) for i in range(2)]
    other_gate, other_up = [jnp.concatenate([b[i] for b in other_one], axis=0) for i in range(2)]
    own_down = jnp.concatenate(own_two, axis=0)
    other_down = jnp.concatenate(other_two, axis=0)

    def from_width(tokens, own, other):
        return mm(tokens[:, :half], own, 1, 1) + mm(tokens[:, half:], other, 1, 1)

    gates = [from_width(tokens, own_gate, other_gate).astype(BF16) for tokens in ffn_rows]
    ups = [from_width(tokens, own_up, other_up).astype(BF16) for tokens in ffn_rows]

    def activate(gate, up):
        gate = gate.astype(F32)
        return (gate * jax.nn.sigmoid(gate) * up.astype(F32)).astype(BF16)

    hidden = [activate(gate, up) for gate, up in zip(gates, ups)]

    def ffn_forward(part):
        return lambda: jnp.concatenate(
            [mm(hidden[part], own_down).astype(BF16), mm(hidden[part], other_down).astype(BF16)],
            axis=1,
        )

    ffn_out, ffn_sent = reduce_tokens(ffn_forward(0), ffn_forward(1))
    grads = (grads[0], after(grads[1], *ffn_sent))

    def over_tokens(left, right):
        total = mm(left[0], right[0], 0, 0)
        for a, b in zip(left[1:], right[1:]):
            total = total + mm(a, b, 0, 0)
        return total.astype(BF16)

    def send_other(left, right):
        return over_x(over_tokens(left, [b[:, half:] for b in right]))

    def keep_own(left, right):
        return over_tokens(left, [b[:, :half] for b in right])

    def add_up(kept, moved):
        kept = jnp.split(kept, depth, axis=0)
        moved = jnp.split(moved, depth, axis=0)
        return [(a.astype(F32) + b.astype(F32)).astype(BF16) for a, b in zip(kept, moved)]

    down_moved = send_other(hidden, grads)
    grad_gates, grad_ups = [], []
    for grad, gate, up in zip(grads, gates, ups):
        grad_hidden = from_width(grad, own_down, other_down)
        gate = gate.astype(F32)
        sigmoid = jax.nn.sigmoid(gate)
        grad_gates.append(
            (grad_hidden * up.astype(F32) * sigmoid * (1.0 + gate * (1.0 - sigmoid))).astype(BF16)
        )
        grad_ups.append((grad_hidden * gate * sigmoid).astype(BF16))

    def ffn_back(part):
        return lambda: jnp.concatenate(
            [
                (mm(grad_gates[part], a) + mm(grad_ups[part], b)).astype(BF16)
                for a, b in ((own_gate, own_up), (other_gate, other_up))
            ],
            axis=1,
        )

    grad_ffn, grad_ffn_sent = reduce_tokens(ffn_back(0), ffn_back(1))
    ffn_out = after(ffn_out, *grad_ffn_sent)
    output = trade_z(rotate((middle + ffn_out).astype(BF16)).reshape(depth, share, width))
    gate_moved = send_other(grad_gates, ffn_rows)
    up_moved = send_other(grad_ups, ffn_rows)

    grad_mid_norm, gain_two_grad = norm_back(middle, gain_two, scale_two, grad_ffn)
    grad_middle = grad_out.astype(F32) + grad_mid_norm

    down_kept = keep_own(hidden, grads)
    gate_kept = keep_own(grad_gates, ffn_rows)
    up_kept = keep_own(grad_ups, ffn_rows)

    grad_branch = jnp.concatenate(gather_tokens(grad_middle.astype(BF16)), axis=0)
    grad_olow = mm(out_lift, grad_branch, 1, 1).astype(BF16)
    grad_mixed = (mm(out_mat, grad_branch, 1, 1) + mm(out_down, grad_olow)).astype(BF16)
    down_sums = add_up(down_kept, after(down_moved, grad_middle))
    down_step = after(over_z(down_sums[1]), grad_branch)
    down_step = (down_step.astype(F32) + down_sums[2].astype(F32)).astype(BF16)
    down_step = over_z(down_step)
    gate_sums = add_up(gate_kept, after(gate_moved, grad_branch))
    out_lift_grad = mm(rank_rows, grad_branch)
    out_down_grad = mm(mixed, grad_olow, 1, 1)
    out_weight_grad = mm(mixed, grad_branch).astype(BF16)

    grad_mixed = after(grad_mixed, gate_sums[1:], output)
    gate_shifted = [over_z(gate_sums[depth - k], k) for k in range(1, depth)]
    grad_rows, maps_grad = attend_backward(
        last, order, seg_row, seg_col, rows_nat, key_nat, maps, lift, saved, to_natural(grad_mixed)
    )
    grad_rows = after(from_natural(grad_rows), down_step, gate_shifted)

    def project_back(part):
        return lambda: mm(grad_rows[:, part], project, 0, 0).astype(BF16)

    grad_normed, normed_sent = reduce_tokens(project_back(chip_part), project_back(other_part))

    late_rows = after(grad_rows, *normed_sent)
    project_grad = [
        mm(late_rows[:, chip_part], normed[0][:, cut]) + mm(late_rows[:, other_part], normed[1][:, cut])
        for cut in (slice(0, half), slice(half, width))
    ]
    lift_grad = mm(low_rows, late_rows[:row_count], 1, 1)[: 3 * rank].reshape(3, rank, row_count)
    column = lax.broadcasted_iota(jnp.int32, (3, 1, row_count), 2)
    owner_of = (column >= query_rows).astype(jnp.int32) + (column >= query_rows + key_rows)
    kind = lax.broadcasted_iota(jnp.int32, (3, 1, row_count), 0)
    lift_grad = jnp.sum(jnp.where(owner_of == kind, lift_grad, 0.0), axis=0).T

    def halves(value):
        middle_at = value.shape[-1] // 2
        first, second = value[..., :middle_at], value[..., middle_at:]
        return jnp.where(x == 0, first, second), jnp.where(x == 0, second, first)

    quarter = half // 2
    rank_own = rank // 4
    maps_own = HD // 4

    def part_of(value, place):
        sizes = (quarter, rank_own, maps_own)
        start = 0
        parts = []
        for size in sizes:
            if start < value.shape[1]:
                parts.append(lax.dynamic_slice_in_dim(value, start + place * size, size, 1))
            start += 2 * size
        return jnp.concatenate(parts, axis=1).astype(BF16)

    def by_depth(value, height):
        return value.reshape(near, height, value.shape[-1])

    def collect(own_half, other_half, blocks):
        summed = own_half.astype(F32) + over_x(other_half.astype(BF16)).astype(F32)

        def ready(place):
            return blocks(part_of(summed, place))

        return shift_sum(list(turn(in_order(ready(c), over_c(ready(1 - c)), 0), 0)))

    down_lift = halves(out_down_grad)
    out_sum = collect(
        *[
            jnp.concatenate([out_weight_grad[:, i * half : (i + 1) * half], down_lift[i]], axis=1)
            for i in range(2)
        ],
        lambda value: by_depth(value, block_rows),
    )
    out_grad = out_sum[:, :quarter]
    output_down_grad = out_sum[:, quarter : quarter + rank_own]

    lift_halves = halves(lift_grad)
    maps_halves = halves(
        jnp.concatenate(
            [maps_grad.reshape(query_rows, HD), jnp.zeros((2 * key_rows, HD), F32)], axis=0
        )
    )
    late_sum = collect(
        *[
            jnp.concatenate([project_grad[i][:row_count], lift_halves[i], maps_halves[i]], axis=1)
            for i in range(2)
        ],
        lambda value: jnp.concatenate(
            [
                by_depth(value[:query_rows], block_rows),
                by_depth(value[query_rows : query_rows + key_rows], HD),
                by_depth(value[query_rows + key_rows :], HD),
            ],
            axis=1,
        ),
    )
    query_grad = late_sum[:block_rows, :quarter].T
    query_lift_grad = late_sum[:block_rows, quarter : quarter + rank_own].T
    feature_maps_grad = jnp.transpose(
        late_sum[:block_rows, quarter + rank_own :].reshape(per, HD, maps_own), (0, 2, 1)
    )
    kv_sum = late_sum[block_rows:, : quarter + rank_own].reshape(2, HD, quarter + rank_own)
    kv_sum = jnp.where(
        lax.broadcasted_iota(jnp.int32, (kv_depth, 1, 1, 1), 0) == kv_pick, kv_sum[None], 0.0
    ).astype(BF16)
    step = 1
    while step < wide:
        kv_sum = (kv_sum.astype(F32) + over_y(kv_sum, step).astype(F32)).astype(BF16)
        step *= 2
    kv_sum = turn(jnp.stack(shifts(kv_sum)), 0)
    kv_sum = jnp.transpose(kv_sum, (2, 4, 0, 1, 3)).reshape(2, quarter + rank_own, KV * HD)
    kv_sum = kv_sum.astype(F32)

    gate_total = gate_sums[0].astype(F32)
    for block in gate_shifted:
        gate_total = gate_total + block.astype(F32)
    down_step = (down_step.astype(F32) + down_sums[3].astype(F32)).astype(BF16)
    down_total = over_z(down_step).astype(F32) + down_sums[0].astype(F32)
    up_total = ring_sum(add_up(up_kept, after(up_moved, *normed_sent)))

    def to_owner(total):
        return trade_c(total.astype(BF16), 1, 0)

    down_grad = to_owner(down_total).astype(F32)
    gate_grad = to_owner(gate_total).T.astype(F32)
    up_grad = to_owner(up_total).T.astype(F32)

    grad_in_norm, gain_one_grad = norm_back(layer_in, gain_one, scale_one, grad_normed)
    input_grad = trade_z(
        rotate((grad_middle + grad_in_norm).astype(BF16)).reshape(depth, share, width)
    ).astype(F32)

    minor = jnp.concatenate(
        [
            gain_one_grad[None],
            gain_two_grad[None],
            jnp.concatenate([part[row_count : row_count + 3 * rank] for part in project_grad], axis=1),
            out_lift_grad,
        ],
        axis=0,
    )
    minor = minor[:, :half] + over_x(minor[:, half:])
    minor = jnp.moveaxis(minor.reshape(-1, depth, wide, 2, half // (2 * heads_size)), 0, 3)
    minor = shift_sum(list(turn(minor, 0)))
    total = lax.dynamic_index_in_dim(minor, y, 0, False)
    for k in range(1, wide):
        total = total + over_y(lax.dynamic_index_in_dim(minor, y ^ k, 0, False), k)
    minor = lax.dynamic_index_in_dim(total, c, 0, False) + over_c(
        lax.dynamic_index_in_dim(total, 1 - c, 0, False)
    )
    minor = minor.T
    return (
        output[:, None, None],
        input_grad[:, None, None],
        minor[:, 0],
        minor[:, 1],
        query_grad,
        kv_sum[0, :quarter],
        kv_sum[1, :quarter],
        out_grad,
        minor[:, 2 : 2 + rank],
        query_lift_grad,
        minor[:, 2 + rank : 2 + 2 * rank],
        kv_sum[0, quarter:],
        minor[:, 2 + 2 * rank : 2 + 3 * rank],
        kv_sum[1, quarter:],
        output_down_grad,
        minor[:, 2 + 3 * rank :].T,
        feature_maps_grad,
        gate_grad,
        up_grad,
        down_grad,
    )


def solution(mesh):
    placed = (
        P(None, "rows", "seq", "heads", None),
        P(None, "rows", None),
        P(None, "rows", "seq", "heads", None),
        P(("rows", "heads", "seq")),
        P(("rows", "heads", "seq")),
        P(("rows", "seq"), "heads"),
        P(("rows", "seq"), None),
        P(("rows", "seq"), None),
        P("heads", ("rows", "seq")),
        P(("rows", "heads", "seq"), None),
        P(("rows", "seq"), "heads"),
        P(("rows", "heads", "seq"), None),
        P(("rows", "seq"), None),
        P(("rows", "heads", "seq"), None),
        P(("rows", "seq"), None),
        P("heads", ("rows", "seq")),
        P(None, ("rows", "heads", "seq")),
        P("heads", ("rows", "seq"), None),
        P(("rows", "seq"), "heads"),
        P(("rows", "seq"), "heads"),
        P("heads", ("rows", "seq")),
    )
    return jax.shard_map(
        body,
        mesh=mesh,
        in_specs=placed,
        out_specs=(
            P(None, "rows", "seq", "heads", None),
            P(None, "rows", "seq", "heads", None),
            P(("rows", "heads", "seq")),
            P(("rows", "heads", "seq")),
            P(("rows", "seq"), "heads"),
            P(("rows", "seq"), None),
            P(("rows", "seq"), None),
            P("heads", ("rows", "seq")),
            P(("rows", "heads", "seq"), None),
            P(("rows", "seq"), "heads"),
            P(("rows", "heads", "seq"), None),
            P(("rows", "seq"), None),
            P(("rows", "heads", "seq"), None),
            P(("rows", "seq"), None),
            P("heads", ("rows", "seq")),
            P(None, ("rows", "heads", "seq")),
            P("heads", ("rows", "seq"), None),
            P(("rows", "seq"), "heads"),
            P(("rows", "seq"), "heads"),
            P("heads", ("rows", "seq")),
        ),
        check_vma=False,
    )
```

```python
import math

import jax
import jax.numpy as jnp
from jax import lax
from jax.experimental import pallas as pl
from jax.experimental.pallas import tpu as pltpu
from jax.sharding import PartitionSpec as P

HEADS = 32
KV = 8
HD = 64
WINDOW = 64
CHUNK = 2 * WINDOW
FEATS = 2 * HD
AUG = HD + 16
F32 = jnp.float32
PART = 512
BF16 = jnp.bfloat16


def mm(left, right, left_dim=1, right_dim=0):
    return lax.dot_general(
        left, right, (((left_dim,), (right_dim,)), ((), ())), preferred_element_type=F32
    )


def chunk_masks(chunk, seg_row, seg_own, seg_prev):
    place = lax.broadcasted_iota(jnp.int32, (CHUNK, CHUNK), 1)
    key = lax.broadcasted_iota(jnp.int32, (CHUNK, CHUNK), 0)
    same_own = seg_own == seg_row
    same_prev = (seg_prev - jnp.where(chunk == 0, 100, 0)) == seg_row
    far = -1e30
    bias_own = jnp.where(same_own & (key <= place) & (key > place - WINDOW), 0.0, far)
    bias_prev = jnp.where(same_prev & (key > place + WINDOW), 0.0, far)
    linear_prev = jnp.where(same_prev & (key <= place + WINDOW), 1.0, 0.0)
    linear_own = jnp.where(same_own & (key <= place - WINDOW), 1.0, 0.0)
    return bias_prev[WINDOW:], bias_own, linear_prev, linear_own[:WINDOW]


def turned(values):
    return jnp.transpose(values.astype(F32)).astype(BF16)


def with_ones(values):
    return jnp.concatenate([values, jnp.ones((AUG - HD, CHUNK), values.dtype)], axis=0)


def features_of(vectors, maps_t):
    logits = mm(maps_t, vectors)
    high = jnp.exp(logits - jnp.max(logits, axis=0, keepdims=True))
    low = jnp.exp(jnp.min(logits, axis=0, keepdims=True) - logits)
    high = high * (1.0 / jnp.sum(high, axis=0, keepdims=True))
    low = low * (1.0 / jnp.sum(low, axis=0, keepdims=True))
    return jnp.concatenate([high, low], axis=0)


def features_back(features, grad):
    product = features * grad
    high = product[:HD] - features[:HD] * jnp.sum(product[:HD], axis=0, keepdims=True)
    low = product[HD:] - features[HD:] * jnp.sum(product[HD:], axis=0, keepdims=True)
    return high - low


def forward_kernel(
    last_ref, order_ref, seg_row_ref, seg_own_ref, seg_prev_ref,
    q_ref, kt_ref, ktp_ref, vt_ref, vtp_ref, maps_t_ref,
    mixed_ref, peak_ref, den_ref, fq_ref, fkt_ref, fk_ref, state_out_ref,
    state_ref, fk_prev_ref,
):
    chunk = pl.program_id(0)
    head_count = fq_ref.shape[0]
    per_key = head_count * HD // kt_ref.shape[0]

    @pl.when(chunk == 0)
    def _():
        state_ref[...] = jnp.zeros_like(state_ref)
        fk_prev_ref[...] = jnp.zeros_like(fk_prev_ref)

    seg_row = seg_row_ref[...]
    bias_prev, bias_own, linear_prev, linear_own = chunk_masks(
        chunk, seg_row, seg_own_ref[...], seg_prev_ref[...]
    )
    tag_state = jnp.where(chunk >= 2, last_ref[jnp.maximum(chunk - 2, 0)], -1)
    tag_prev = jnp.where(chunk >= 1, last_ref[jnp.maximum(chunk - 1, 0)], -2)
    carried = jnp.where(seg_row == tag_state, 1.0, 0.0)
    joined = jnp.where(tag_state == tag_prev, 1.0, 0.0)
    keep_prev = jnp.where(seg_prev_ref[...] == tag_prev, 1.0, 0.0).astype(BF16)
    k_own = turned(kt_ref[...])
    k_prev = turned(ktp_ref[...])
    for head in range(head_count):
        group = head // per_key
        rows = slice(head * HD, (head + 1) * HD)
        key_rows = slice(group * HD, (group + 1) * HD)
        query = q_ref[rows, :]
        maps_t = maps_t_ref[head]
        feat_q = features_of(query, maps_t)
        feat_kt = features_of(kt_ref[key_rows, :], maps_t)
        fq_ref[head] = feat_q.astype(BF16)
        fkt_ref[head] = feat_kt.astype(BF16)
        feat_k = jnp.transpose(feat_kt).astype(BF16)
        fk_ref[head] = feat_k
        scaled = query * jnp.asarray(HD**-0.5, BF16)
        score_prev = mm(k_prev[WINDOW:, key_rows], scaled) + bias_prev
        score_own = mm(k_own[:, key_rows], scaled) + bias_own
        peak = jnp.maximum(
            jnp.max(score_prev, axis=0, keepdims=True), jnp.max(score_own, axis=0, keepdims=True)
        )
        weight_prev = jnp.exp(score_prev - peak)
        weight_own = jnp.exp(score_own - peak)
        damped = feat_q * jnp.exp(-peak)
        damped_low = damped.astype(BF16)
        fk_prev = fk_prev_ref[head]
        lin_prev = mm(fk_prev, damped_low) * linear_prev
        lin_own = mm(feat_k[:WINDOW], damped_low) * linear_own
        all_prev = jnp.concatenate([lin_prev[:WINDOW], lin_prev[WINDOW:] + weight_prev], axis=0)
        all_own = jnp.concatenate([lin_own + weight_own[:WINDOW], weight_own[WINDOW:]], axis=0)
        value_prev = with_ones(vtp_ref[key_rows, :])
        state = state_ref[head]
        state_low = state.astype(BF16)
        state_out_ref[0, head] = state_low
        total = (
            mm(value_prev, all_prev.astype(BF16))
            + mm(with_ones(vt_ref[key_rows, :]), all_own.astype(BF16))
            + mm(state_low, (damped * carried).astype(BF16))
        )
        den = total[HD : HD + 1]
        mixed_ref[rows, :] = (total[:HD] * (1.0 / den)).astype(BF16)
        peak_ref[head : head + 1, :] = peak
        den_ref[head : head + 1, :] = den
        state_ref[head] = state * joined + mm(value_prev, fk_prev * keep_prev)
        fk_prev_ref[head] = feat_k


def backward_kernel(
    last_ref, order_ref, seg_row_ref, seg_own_ref, seg_prev_ref,
    q_ref, kt_ref, ktp_ref, vt_ref, vtp_ref, maps_ref, lift_ref,
    mixed_ref, grad_ref, peak_ref, den_ref, fq_ref, fkt_ref, fktp_ref, fk_ref, fkp_ref, state_ref,
    grows_ref, gmaps_ref,
    gstate_ref, cphi_ref, ck_ref, cv_ref,
):
    step = pl.program_id(0)
    chunk = pl.num_programs(0) - 1 - step
    head_count = fq_ref.shape[0]
    group_count = kt_ref.shape[0] // HD
    per_key = head_count // group_count

    @pl.when(step == 0)
    def _():
        gstate_ref[...] = jnp.zeros_like(gstate_ref)
        cphi_ref[...] = jnp.zeros_like(cphi_ref)
        ck_ref[...] = jnp.zeros_like(ck_ref)
        cv_ref[...] = jnp.zeros_like(cv_ref)
        gmaps_ref[...] = jnp.zeros_like(gmaps_ref)

    seg_row = seg_row_ref[...]
    bias_prev, bias_own, linear_prev, linear_own = chunk_masks(
        chunk, seg_row, seg_own_ref[...], seg_prev_ref[...]
    )
    tag_state = jnp.where(chunk >= 2, last_ref[jnp.maximum(chunk - 2, 0)], -1)
    tag_prev = jnp.where(chunk >= 1, last_ref[jnp.maximum(chunk - 1, 0)], -2)
    carried = jnp.where(seg_row == tag_state, 1.0, 0.0)
    joined = jnp.where(tag_state == tag_prev, 1.0, 0.0)
    keep_col = jnp.where(seg_prev_ref[...] == tag_prev, 1.0, 0.0)
    keep_prev = jnp.transpose(jnp.broadcast_to(keep_col, (CHUNK, CHUNK)))[:1]
    scale = HD**-0.5
    none = jnp.zeros((WINDOW, CHUNK), F32)
    k_own = turned(kt_ref[...])
    k_prev = turned(ktp_ref[...])
    v_own = turned(vt_ref[...])
    v_prev = turned(vtp_ref[...])
    for group in range(group_count):
        key_rows = slice(group * HD, (group + 1) * HD)
        key_t = kt_ref[key_rows, :]
        value_prev = with_ones(vtp_ref[key_rows, :])
        own_k = ck_ref[group]
        own_v = cv_ref[group]
        next_k = None
        next_v = None
        for head in range(group * per_key, (group + 1) * per_key):
            rows = slice(head * HD, (head + 1) * HD)
            query = q_ref[rows, :]
            scaled = query * jnp.asarray(scale, BF16)
            peak = peak_ref[head : head + 1, :]
            den = den_ref[head : head + 1, :]
            weight_prev = jnp.exp(mm(k_prev[WINDOW:, key_rows], scaled) + bias_prev - peak)
            weight_own = jnp.exp(mm(k_own[:, key_rows], scaled) + bias_own - peak)
            damp = jnp.exp(-peak)
            feat_q = fq_ref[head].astype(F32)
            damped = feat_q * damp
            damped_low = damped.astype(BF16)
            carried_low = (damped * carried).astype(BF16)
            lin_prev = mm(fkp_ref[head], damped_low) * linear_prev
            lin_own = mm(fk_ref[head, :WINDOW, :], damped_low) * linear_own
            all_prev = jnp.concatenate([lin_prev[:WINDOW], lin_prev[WINDOW:] + weight_prev], axis=0)
            all_own = jnp.concatenate([lin_own + weight_own[:WINDOW], weight_own[WINDOW:]], axis=0)
            grad = grad_ref[rows, :].astype(F32)
            dnum = grad * (1.0 / den)
            dden = -jnp.sum(dnum * mixed_ref[rows, :].astype(F32), axis=0, keepdims=True)
            dnum_low = dnum.astype(BF16)
            dtotal = jnp.concatenate(
                [dnum, dden, jnp.zeros((AUG - HD - 1, CHUNK), F32)], axis=0
            ).astype(BF16)
            dall_prev = mm(v_prev[:, key_rows], dnum_low) + dden
            dall_own = mm(v_own[:, key_rows], dnum_low) + dden
            dscore_prev = jnp.concatenate([none, weight_prev * dall_prev[WINDOW:]], axis=0).astype(BF16)
            dscore_own = (weight_own * dall_own).astype(BF16)
            dlin_prev = (linear_prev * dall_prev).astype(BF16)
            dlin_own = jnp.concatenate([linear_own * dall_own[:WINDOW], none], axis=0).astype(BF16)
            gstate = gstate_ref[head]
            gstate_low = gstate.astype(BF16)
            ddamped = (
                mm(fktp_ref[head], dlin_prev)
                + mm(fkt_ref[head], dlin_own)
                + carried * mm(state_ref[0, head], dtotal, 0, 0)
            )
            dlogit_q = features_back(feat_q, ddamped * damp).astype(BF16)
            maps = maps_ref[head]
            grad_q = (
                mm(ktp_ref[key_rows, :], dscore_prev) + mm(key_t, dscore_own)
            ) * scale + mm(maps, dlogit_q)
            grows_ref[rows, :] = grad_q.astype(BF16)
            dphi_own = cphi_ref[head] + mm(damped_low, dlin_own, 1, 1)
            cphi_ref[head] = (
                mm(damped_low, dlin_prev, 1, 1) + mm(gstate_low, value_prev, 0, 0) * keep_prev
            )
            dlogit_k = features_back(fkt_ref[head].astype(F32), dphi_own).astype(BF16)
            gmaps_ref[head] += mm(dlogit_q, query, 1, 1) + mm(dlogit_k, key_t, 1, 1)
            own_k += mm(scaled, dscore_own, 1, 1) + mm(maps, dlogit_k)
            part_k = mm(scaled, dscore_prev, 1, 1)
            own_v += mm(dnum_low, all_own.astype(BF16), 1, 1)
            part_v = (
                mm(dnum_low, all_prev.astype(BF16), 1, 1)
                + mm(gstate_low[:HD], fktp_ref[head]) * keep_prev
            )
            next_k = part_k if next_k is None else next_k + part_k
            next_v = part_v if next_v is None else next_v + part_v
            gstate_ref[head] = gstate * joined + mm(dtotal, carried_low, 1, 1)
        key_start = (head_count + group) * HD
        value_start = (head_count + group_count + group) * HD
        grows_ref[key_start : key_start + HD, :] = own_k.astype(BF16)
        grows_ref[value_start : value_start + HD, :] = own_v.astype(BF16)
        ck_ref[group] = next_k
        cv_ref[group] = next_v
    width = lift_ref.shape[1]
    grows_ref[width:, :] = mm(lift_ref[...], grows_ref[:width, :]).astype(BF16)


def attend_forward(last, order, seg_row, seg_col, rows, maps_t, waits=()):
    heads = maps_t.shape[0]
    groups, length = (rows.shape[0] // HD - heads) // 2, rows.shape[1]
    chunks = length // CHUNK
    first = heads // groups

    def before(c):
        return jnp.maximum(c - 1, 0)

    def spec(count, block, shift):
        return pl.BlockSpec((count * HD, CHUNK), lambda c, last, order: (block, order[shift(c)]))

    def here(c):
        return c

    stat = pl.BlockSpec((heads, CHUNK), lambda c, last, order: (0, c))
    feat_t = pl.BlockSpec((heads, FEATS, CHUNK), lambda c, last, order: (0, 0, c))
    return pl.pallas_call(
        ignoring(forward_kernel, 11, len(waits)),
        grid_spec=pltpu.PrefetchScalarGridSpec(
            num_scalar_prefetch=2,
            grid=(chunks,),
            in_specs=[
                pl.BlockSpec((1, CHUNK), lambda c, last, order: (0, c)),
                pl.BlockSpec((CHUNK, 1), lambda c, last, order: (c, 0)),
                pl.BlockSpec((CHUNK, 1), lambda c, last, order: (before(c), 0)),
                spec(heads, 0, here),
                spec(groups, first, here),
                spec(groups, first, before),
                spec(groups, first + 1, here),
                spec(groups, first + 1, before),
                pl.BlockSpec((heads, HD, HD), lambda c, last, order: (0, 0, 0)),
            ]
            + [pl.BlockSpec(memory_space=pl.ANY)] * len(waits),
            out_specs=[
                spec(heads, 0, here), stat, stat,
                feat_t, feat_t,
                pl.BlockSpec((heads, CHUNK, FEATS), lambda c, last, order: (0, c, 0)),
                pl.BlockSpec((1, heads, AUG, FEATS), lambda c, last, order: (c, 0, 0, 0)),
            ],
            scratch_shapes=[
                pltpu.VMEM((heads, AUG, FEATS), F32),
                pltpu.VMEM((heads, CHUNK, FEATS), BF16),
            ],
        ),
        out_shape=[
            jax.ShapeDtypeStruct((heads * HD, length), BF16),
            jax.ShapeDtypeStruct((heads, length), F32),
            jax.ShapeDtypeStruct((heads, length), F32),
            jax.ShapeDtypeStruct((heads, FEATS, length), BF16),
            jax.ShapeDtypeStruct((heads, FEATS, length), BF16),
            jax.ShapeDtypeStruct((heads, length, FEATS), BF16),
            jax.ShapeDtypeStruct((chunks, heads, AUG, FEATS), BF16),
        ],
        compiler_params=pltpu.CompilerParams(
            dimension_semantics=("arbitrary",), vmem_limit_bytes=32 * 2**20
        ),
        cost_estimate=pl.CostEstimate(
            flops=heads * length * 1060000, bytes_accessed=heads * length * 400, transcendentals=0
        ),
        name="attend_forward",
    )(
        last, order, seg_row, seg_col, seg_col, rows, rows, rows, rows, rows, maps_t, *waits
    )


def attend_backward(
    last, order, seg_row, seg_col, rows, maps, lift, saved, grad, waits=()
):
    mixed, peak, den, fq, fkt, fk, states = saved
    heads = maps.shape[0]
    groups, length = (rows.shape[0] // HD - heads) // 2, rows.shape[1]
    chunks = length // CHUNK
    first = heads // groups
    height = lift.shape[0] + lift.shape[1]

    def here(s):
        return chunks - 1 - s

    def before(s):
        return jnp.maximum(chunks - 2 - s, 0)

    def spec(count, block, shift):
        return pl.BlockSpec((count * HD, CHUNK), lambda s, last, order: (block, order[shift(s)]))

    def feat_t(shift):
        return pl.BlockSpec((heads, FEATS, CHUNK), lambda s, last, order: (0, 0, shift(s)))

    def feat(shift):
        return pl.BlockSpec((heads, CHUNK, FEATS), lambda s, last, order: (0, shift(s), 0))

    stat = pl.BlockSpec((heads, CHUNK), lambda s, last, order: (0, here(s)))
    whole = pl.BlockSpec((heads, HD, HD), lambda s, last, order: (0, 0, 0))
    return pl.pallas_call(
        ignoring(backward_kernel, 22, len(waits)),
        grid_spec=pltpu.PrefetchScalarGridSpec(
            num_scalar_prefetch=2,
            grid=(chunks,),
            in_specs=[
                pl.BlockSpec((1, CHUNK), lambda s, last, order: (0, here(s))),
                pl.BlockSpec((CHUNK, 1), lambda s, last, order: (here(s), 0)),
                pl.BlockSpec((CHUNK, 1), lambda s, last, order: (before(s), 0)),
                spec(heads, 0, here),
                spec(groups, first, here), spec(groups, first, before),
                spec(groups, first + 1, here), spec(groups, first + 1, before),
                whole,
                pl.BlockSpec(lift.shape, lambda s, last, order: (0, 0)),
                spec(heads, 0, here), spec(heads, 0, here), stat, stat,
                feat_t(here), feat_t(here), feat_t(before), feat(here), feat(before),
                pl.BlockSpec((1, heads, AUG, FEATS), lambda s, last, order: (here(s), 0, 0, 0)),
            ]
            + [pl.BlockSpec(memory_space=pl.ANY)] * len(waits),
            out_specs=[
                pl.BlockSpec((height, CHUNK), lambda s, last, order: (0, order[here(s)])),
                whole,
            ],
            scratch_shapes=[
                pltpu.VMEM((heads, AUG, FEATS), F32),
                pltpu.VMEM((heads, FEATS, CHUNK), F32),
                pltpu.VMEM((groups, HD, CHUNK), F32),
                pltpu.VMEM((groups, HD, CHUNK), F32),
            ],
        ),
        out_shape=[
            jax.ShapeDtypeStruct((height, length), BF16),
            jax.ShapeDtypeStruct((heads, HD, HD), F32),
        ],
        compiler_params=pltpu.CompilerParams(
            dimension_semantics=("arbitrary",), vmem_limit_bytes=32 * 2**20
        ),
        cost_estimate=pl.CostEstimate(
            flops=heads * length * 2100000, bytes_accessed=heads * length * 600, transcendentals=0
        ),
        name="attend_backward",
    )(
        last, order, seg_row, seg_col, seg_col, rows, rows, rows, rows, rows, maps, lift, mixed, grad, peak, den, fq, fkt, fkt, fk, fk, states, *waits,
    )


def ignoring(kernel, inputs, waits):
    def body(*refs):
        kernel(*refs[:inputs], *refs[inputs + waits :])

    return body


def after(value, *others):
    values = jax.tree.leaves(value)
    tokens = jax.tree.leaves(others)
    anywhere = pl.BlockSpec(memory_space=pl.ANY)
    out = pl.pallas_call(
        lambda *refs: None,
        in_specs=[anywhere] * (len(values) + len(tokens)),
        out_specs=[anywhere] * len(values),
        out_shape=[jax.ShapeDtypeStruct(v.shape, v.dtype) for v in values],
        input_output_aliases={i: i for i in range(len(values))},
        cost_estimate=pl.CostEstimate(flops=0, bytes_accessed=0, transcendentals=0),
        name="after",
    )(*values, *tokens)
    return jax.tree.unflatten(jax.tree.structure(value), out)


def stack_rows(pieces):
    rows, columns = pieces[0].shape
    tall = min(256, rows)
    steps = rows // tall
    count = len(pieces)

    def kernel(*refs):
        for place in range(count):

            @pl.when(pl.program_id(0) == place)
            def _(place=place):
                refs[-1][...] = refs[place][...]

    def spec(place):
        def at(i, j):
            return (jnp.where(i < place, 0, jnp.where(i > place, steps - 1, j)), 0)

        return pl.BlockSpec((tall, columns), at)

    return pl.pallas_call(
        kernel,
        grid=(count, steps),
        in_specs=[spec(place) for place in range(count)],
        out_specs=pl.BlockSpec((tall, columns), lambda i, j: (i * steps + j, 0)),
        out_shape=jax.ShapeDtypeStruct((count * rows, columns), pieces[0].dtype),
        cost_estimate=pl.CostEstimate(
            flops=0, bytes_accessed=count * rows * columns, transcendentals=0
        ),
        name="stack_rows",
    )(*pieces)


def weight_grad_kernel(left_ref, right_ref, out_ref):
    out_ref[...] = mm(left_ref[...], right_ref[...], 0, 0).astype(BF16)


def weight_grad(left, right, part, waits=()):
    tokens, rows = left.shape
    half = right.shape[1] // 2
    tall = min(512, rows)
    return dense_call(
        weight_grad_kernel,
        (rows // tall,),
        [
            pl.BlockSpec((tokens, tall), lambda i: (0, i)),
            pl.BlockSpec((tokens, half), lambda i: (0, part)),
        ],
        pl.BlockSpec((tall, half), lambda i: (i, 0)),
        jax.ShapeDtypeStruct((rows, half), BF16),
        2 * tokens * rows * half,
        "weight_grad",
        waits,
    )(left, right, *waits)


def weight_grad_halves(left, right, swap, waits=()):
    tokens, rows = left.shape
    half = right.shape[1] // 2
    tall = min(512, rows)

    def kernel(swap_ref, left_ref, right_ref, *refs):
        refs[-1][0] = mm(left_ref[...], right_ref[...], 0, 0).astype(BF16)

    return pl.pallas_call(
        kernel,
        grid_spec=pltpu.PrefetchScalarGridSpec(
            num_scalar_prefetch=1,
            grid=(2, rows // tall),
            in_specs=[
                pl.BlockSpec((tokens, tall), lambda p, i, swap: (0, i)),
                pl.BlockSpec((tokens, half), lambda p, i, swap: (0, p + swap[0] - 2 * p * swap[0])),
            ]
            + [pl.BlockSpec(memory_space=pl.ANY)] * len(waits),
            out_specs=pl.BlockSpec((1, tall, half), lambda p, i, swap: (p, i, 0)),
        ),
        out_shape=jax.ShapeDtypeStruct((2, rows, half), BF16),
        compiler_params=pltpu.CompilerParams(
            dimension_semantics=("arbitrary", "arbitrary"), vmem_limit_bytes=48 * 2**20
        ),
        cost_estimate=pl.CostEstimate(
            flops=tokens * rows * half, bytes_accessed=rows * half, transcendentals=0
        ),
        name="weight_grad_halves",
    )(swap, left, right, *waits)


def dense_call(kernel, grid, in_specs, out_specs, out_shape, flops, name, waits=()):
    in_specs = in_specs + [pl.BlockSpec(memory_space=pl.ANY)] * len(waits)
    return pl.pallas_call(
        ignoring(kernel, len(in_specs) - len(waits), len(waits)),
        grid=grid,
        in_specs=in_specs,
        out_specs=out_specs,
        out_shape=out_shape,
        compiler_params=pltpu.CompilerParams(
            dimension_semantics=("arbitrary",) * len(grid), vmem_limit_bytes=48 * 2**20
        ),
        cost_estimate=pl.CostEstimate(
            flops=flops // 3, bytes_accessed=flops // 8000, transcendentals=0
        ),
        name=name,
    )


def sigmoid_of(values):
    return 0.5 * jnp.tanh(0.5 * values) + 0.5


def row_parts(count):
    size = min(PART, count)
    return [slice(at, at + size) for at in range(0, count, size)]


def gate_kernel(rows_ref, own_gate, other_gate, own_up, other_up, gate_ref, up_ref, hidden_ref):
    half = own_gate.shape[1]
    for part in row_parts(rows_ref.shape[0]):
        left = rows_ref[part, :half]
        right = rows_ref[part, half:]
        gate = mm(left, own_gate[...], 1, 1) + mm(right, other_gate[...], 1, 1)
        up = mm(left, own_up[...], 1, 1) + mm(right, other_up[...], 1, 1)
        gate_ref[part, :] = gate.astype(BF16)
        up_ref[part, :] = up.astype(BF16)
        hidden_ref[part, :] = (gate * sigmoid_of(gate) * up).astype(BF16)


def gate_back_kernel(grad_ref, own_down, other_down, gate_ref, up_ref, dgate_ref, dup_ref):
    half = own_down.shape[1]
    for part in row_parts(grad_ref.shape[0]):
        grad = mm(grad_ref[part, :half], own_down[...], 1, 1) + mm(
            grad_ref[part, half:], other_down[...], 1, 1
        )
        gate = gate_ref[part, :].astype(F32)
        sigmoid = sigmoid_of(gate)
        grad_swish = grad * sigmoid
        dup_ref[part, :] = (grad_swish * gate).astype(BF16)
        dgate_ref[part, :] = (
            grad_swish * up_ref[part, :].astype(F32) * (1.0 + gate * (1.0 - sigmoid))
        ).astype(BF16)


def sum_kernel(count, lefts_and_weights, out_ref):
    lefts = lefts_and_weights[:count]
    owns = lefts_and_weights[count : 2 * count]
    others = lefts_and_weights[2 * count :]
    column = pl.program_id(0)

    def write(weights):
        total = mm(lefts[0][...], weights[0][...])
        for left, weight in zip(lefts[1:], weights[1:]):
            total = total + mm(left[...], weight[...])
        out_ref[...] = total.astype(BF16)

    across = pl.num_programs(0) // 2

    @pl.when(column < across)
    def _():
        write(owns)

    @pl.when(column >= across)
    def _():
        write(others)


def gate_forward(rows, own_gate, other_gate, own_up, other_up, waits=()):
    tokens, width = rows.shape
    hidden, half = own_gate.shape
    tall, wide = min(512, tokens), min(1024, hidden)
    weight = pl.BlockSpec((wide, half), lambda j, i: (j, 0))
    out = pl.BlockSpec((tall, wide), lambda j, i: (i, j))
    return dense_call(
        gate_kernel,
        (hidden // wide, tokens // tall),
        [pl.BlockSpec((tall, width), lambda j, i: (i, 0))] + [weight] * 4,
        [out] * 3,
        [jax.ShapeDtypeStruct((tokens, hidden), BF16)] * 3,
        4 * tokens * width * hidden,
        "gate_forward",
        waits,
    )(rows, own_gate, other_gate, own_up, other_up, *waits)


def gate_backward(grad, own_down, other_down, gate, up, waits=()):
    tokens, width = grad.shape
    hidden, half = own_down.shape
    tall, wide = min(512, tokens), min(1024, hidden)
    weight = pl.BlockSpec((wide, half), lambda j, i: (j, 0))
    out = pl.BlockSpec((tall, wide), lambda j, i: (i, j))
    return dense_call(
        gate_back_kernel,
        (hidden // wide, tokens // tall),
        [pl.BlockSpec((tall, width), lambda j, i: (i, 0)), weight, weight, out, out],
        [out] * 2,
        [jax.ShapeDtypeStruct((tokens, hidden), BF16)] * 2,
        2 * tokens * width * hidden,
        "gate_backward",
        waits,
    )(grad, own_down, other_down, gate, up, *waits)


def sum_products(lefts, owns, others, start, tokens, waits=()):
    count = len(lefts)
    depth = lefts[0].shape[1]
    half = owns[0].shape[1]
    tall, wide = math.gcd(math.gcd(start, tokens), 1024), min(512, half)
    across = half // wide
    first = start // tall

    def kernel(*refs):
        sum_kernel(count, refs[:-1], refs[-1])

    left = pl.BlockSpec((tall, depth), lambda j, i: (first + i, 0))
    own = pl.BlockSpec((depth, wide), lambda j, i: (0, jnp.minimum(j, across - 1)))
    other = pl.BlockSpec((depth, wide), lambda j, i: (0, jnp.maximum(j - across, 0)))
    return dense_call(
        kernel,
        (2 * across, tokens // tall),
        [left] * count + [own] * count + [other] * count,
        pl.BlockSpec((tall, wide), lambda j, i: (i, j)),
        jax.ShapeDtypeStruct((tokens, 2 * half), BF16),
        4 * count * tokens * depth * half,
        "sum_products",
        waits,
    )(*lefts, *owns, *others, *waits)


ALL = ("rows", "heads", "seq")
SWAP = [(0, 1), (1, 0)]
LOWS = 32


def over_x(value):
    return lax.ppermute(value, "rows", SWAP)


def over_c(value):
    return lax.ppermute(value, "seq", SWAP)


def body(
    inputs,
    segment_ids,
    cotangent,
    attn_gain,
    ffn_gain,
    query_weight,
    key_weight,
    value_weight,
    output_weight,
    query_down,
    query_lift,
    key_down,
    key_lift,
    value_down,
    value_lift,
    output_down,
    output_lift,
    feature_maps,
    gate_weight,
    up_weight,
    down_weight,
):
    heads_size = lax.axis_size("heads")
    depth = inputs.shape[0]
    wide = heads_size // depth
    per = HEADS // heads_size
    near = depth // 2
    block_rows = per * HD
    rank = query_down.shape[1]
    width = inputs.shape[-1]
    half = width // 2
    share = inputs.shape[3]
    held = depth * share
    head_index = lax.axis_index("heads")
    x = lax.axis_index("rows")
    c = lax.axis_index("seq")
    z = head_index // wide
    y = head_index % wide
    kv_pick = y * per // (HEADS // KV)
    kv_depth = KV // depth

    def over_y(value, k):
        return lax.ppermute(
            value,
            "heads",
            [(a * wide + b, a * wide + (b ^ k)) for a in range(depth) for b in range(wide)],
        )

    def over_z(value, k=1):
        return lax.ppermute(
            value,
            "heads",
            [(a * wide + b, (a + k) % depth * wide + b) for a in range(depth) for b in range(wide)],
        )

    def trade_z(value):
        groups = [[a * wide + b for a in range(depth)] for b in range(wide)]
        return lax.all_to_all(
            value, "heads", split_axis=0, concat_axis=0, tiled=True, axis_index_groups=groups
        )

    def gather_z(block):
        return trade_z(jnp.broadcast_to(block[None], (depth,) + block.shape))

    def scatter_z(blocks):
        return jnp.sum(trade_z(blocks).astype(F32), axis=0)

    def trade_c(value, split, concat):
        return lax.all_to_all(value, "seq", split_axis=split, concat_axis=concat, tiled=True)

    def turn(value, axis):
        return jnp.stack(
            [lax.dynamic_index_in_dim(value, (z - j) % depth, axis, False) for j in range(depth)],
            axis,
        )

    def in_order(kept, moved, axis):
        return jnp.where(
            c == 0,
            jnp.concatenate([kept, moved], axis=axis),
            jnp.concatenate([moved, kept], axis=axis),
        )

    def rotate(value):
        return jnp.where(
            x == 1, jnp.concatenate([value[..., half:], value[..., :half]], axis=-1), value
        )

    def shift_sum(blocks, *waits):
        total = lax.dynamic_index_in_dim(blocks, z, 0, False).astype(F32)
        moved = [
            over_z(lax.dynamic_index_in_dim(blocks, (z + k) % depth, 0, False), k)
            for k in range(1, depth)
        ]
        for block in after(moved, *waits) if waits else moved:
            total = total + block.astype(F32)
        return total

    def gather_tokens(value, *waits):
        pieces = [value, over_c(value)]
        for k in range(1, wide):
            moved = over_y(value, k)
            if waits:
                moved = after(moved, *waits)
            pieces += [moved, over_c(moved)]
        return pieces

    def reduce_tokens(make_chip, make_others, waits=()):
        others = make_others()
        sent = []
        arrived = []
        for k in range(1, wide):
            start = (k - 1) * 2 * held
            mine = others[start : start + held]
            moved = over_c(others[start + held : start + 2 * held])
            sent.append((mine.astype(F32) + moved.astype(F32)).astype(BF16))
            arrived.append(over_y(sent[-1], k))
        chip = make_chip(sent)
        total = chip[:held].astype(F32) + over_c(chip[held:]).astype(F32)
        if waits:
            arrived = [after(piece, *waits) for piece in arrived]
        for piece in arrived:
            total = total + piece.astype(F32)
        return total, sent, (chip, *arrived)

    def rms(values):
        return lax.rsqrt(jnp.mean(values * values, axis=-1, keepdims=True) + 1e-05)

    def norm_back(values, gain, scale, grad):
        unit = values * scale
        scaled = grad * gain
        return (
            scale * (scaled - unit * jnp.mean(scaled * unit, axis=-1, keepdims=True)),
            jnp.sum(grad * unit, axis=0),
        )

    small = (
        attn_gain, ffn_gain, query_down, key_down, value_down, output_lift,
        query_lift, key_lift, value_lift, output_down, feature_maps,
    )
    packed = jnp.concatenate([piece.reshape(-1) for piece in small])
    near_small = in_order(packed[None], over_c(packed)[None], 0)[None]
    step = 1
    while step < wide:
        moved = over_y(near_small, step)
        near_small = jnp.where(
            (y // step) % 2 == 0,
            jnp.concatenate([near_small, moved], axis=0),
            jnp.concatenate([moved, near_small], axis=0),
        )
        step *= 2
    layer_in = rotate(trade_z(inputs[:, 0, 0]).reshape(held, width)).astype(F32)
    near_small = turn(
        jnp.stack([near_small] + [over_z(near_small, k) for k in range(1, depth)]), 0
    ).reshape(heads_size, 2, -1)
    far_small = over_x(near_small)
    turned_small = jnp.stack([near_small, far_small])
    spread_small = jnp.where(x == 0, turned_small, jnp.stack([far_small, near_small]))
    starts = [0]
    for piece in small:
        starts.append(starts[-1] + piece.size)

    def piece(index, turned):
        source = turned_small if turned else spread_small
        return source[..., starts[index] : starts[index + 1]].reshape(
            (2, heads_size, 2) + small[index].shape
        )

    def pick_heads(value):
        value = value.reshape((depth, wide) + value.shape[1:])
        value = lax.dynamic_index_in_dim(value, y, 1, False)
        return lax.dynamic_slice_in_dim(value, c * near, near, 0)

    gain_one = piece(0, True).reshape(width).astype(F32)
    gain_two = piece(1, True).reshape(width).astype(F32)
    downs = [piece(i, True).reshape(width, rank) for i in (2, 3, 4)]
    downs_t = jnp.concatenate(downs + [jnp.zeros((width, LOWS - 3 * rank), BF16)], axis=1).T
    out_lift = jnp.moveaxis(piece(5, True), 3, 0).reshape(rank, width)
    query_raise = jnp.transpose(
        piece(6, False).reshape(2, heads_size, 2, -1, per, HD), (1, 4, 0, 2, 3, 5)
    ).reshape(heads_size, per, rank, HD)
    query_raise = jnp.moveaxis(pick_heads(query_raise), 2, 0).reshape(rank, -1)

    def pick_keys(value):
        value = value.reshape(value.shape[0], depth, kv_depth, HD)
        value = lax.dynamic_index_in_dim(value, kv_pick, 2, False)
        return lax.dynamic_slice_in_dim(value, c * near, near, 1).reshape(value.shape[0], -1)

    def pick_near(value):
        value = value.reshape(value.shape[0], depth, kv_depth, HD)
        value = lax.dynamic_index_in_dim(value, kv_pick, 2, False).reshape(value.shape[0], -1).T
        rows_near = near * HD
        kept = lax.dynamic_slice_in_dim(value, c * rows_near, rows_near, 0)
        return in_order(kept, over_c(lax.dynamic_slice_in_dim(value, (1 - c) * rows_near, rows_near, 0)), 1)

    key_raise = pick_keys(piece(7, False)[:, 0].reshape(rank, KV * HD))
    value_raise = pick_keys(piece(8, False)[:, 0].reshape(rank, KV * HD))
    out_down = jnp.transpose(
        piece(9, False).reshape(2, heads_size, 2, per, HD, -1), (1, 3, 4, 0, 2, 5)
    ).reshape(heads_size, per, HD, rank)
    out_down = pick_heads(out_down).reshape(-1, rank)
    maps = jnp.transpose(piece(10, False), (1, 3, 0, 2, 4, 5)).reshape(heads_size, per, HD, HD)
    maps = pick_heads(maps).reshape(-1, HD, HD)
    query_rows = near * block_rows
    key_rows = near * HD
    lift = jnp.concatenate(
        [
            jnp.pad(query_raise, ((0, 0), (0, 2 * key_rows))),
            jnp.pad(key_raise, ((0, 0), (query_rows, key_rows))),
            jnp.pad(value_raise, ((0, 0), (query_rows + key_rows, 0))),
            jnp.zeros((LOWS - 3 * rank, query_rows + 2 * key_rows), BF16),
        ],
        axis=0,
    )
    row_count = query_rows + 2 * key_rows

    def hidden_rows(place):
        parts = [gate_weight, up_weight, down_weight]
        size = down_weight.shape[0] // 2
        return jnp.stack(
            [lax.dynamic_slice_in_dim(p, place * size, size, 1).T for p in parts[:2]]
            + [lax.dynamic_slice_in_dim(parts[2], place * size, size, 0)]
        )

    kept_pack = hidden_rows(c)
    moved_pack = after(over_c(hidden_rows(1 - c)), far_small)
    ffn_own = [in_order(kept_pack, moved_pack, 2)]
    ffn_other = [over_x(ffn_own[0])]
    ring_pack = jnp.where(
        c != 1,
        jnp.concatenate([kept_pack, moved_pack], axis=2),
        jnp.concatenate([moved_pack, kept_pack], axis=2),
    )
    query_blocks = gather_z(after(query_weight.T, layer_in))
    out_blocks = gather_z(after(output_weight, query_blocks))
    ffn_own.append(over_z(after(ring_pack, out_blocks)))

    def join_heads(blocks):
        kept = lax.dynamic_slice_in_dim(blocks, c * near, near, 0)
        moved = over_c(lax.dynamic_slice_in_dim(blocks, (1 - c) * near, near, 0))
        return in_order(kept, moved, 2).reshape(near * block_rows, half)

    query_own = join_heads(query_blocks)
    kv_own = jnp.concatenate([pick_near(key_weight), pick_near(value_weight)], axis=0)
    both_own = jnp.concatenate([query_own, kv_own], axis=0)
    project_own = jnp.concatenate([both_own, downs_t[:, :half]], axis=0)
    project_other = jnp.concatenate([over_x(both_own), downs_t[:, half:]], axis=0)

    def next_block():
        ffn_own.append(over_z(ffn_own[-1]))

    def next_half():
        ffn_other.append(over_x(ffn_own[len(ffn_other)]))

    scale_one = rms(layer_in)
    normed = gather_tokens((layer_in * scale_one * gain_one).astype(BF16))
    normed = (jnp.concatenate(normed[:2], axis=0), jnp.concatenate(normed[2:], axis=0))

    def project_rows(tokens):
        flat = mm(project_own, tokens[:, :half], 1, 1) + mm(project_other, tokens[:, half:], 1, 1)
        low = flat[row_count:].astype(BF16)
        return (flat[:row_count] + mm(lift, low, 0, 0)).astype(BF16), low

    pieces = [project_rows(tokens) for tokens in normed]
    rows = jnp.concatenate([piece_rows for piece_rows, _ in pieces], axis=1)
    low_rows = jnp.concatenate([low for _, low in pieces], axis=1)

    def flips(value, y_axis, c_axis):
        value = jnp.where(c == 1, jnp.flip(value, c_axis), value)
        step = 1
        while step < wide:
            shape = value.shape
            apart = value.reshape(
                shape[:y_axis] + (wide // (2 * step), 2, step) + shape[y_axis + 1 :]
            )
            value = jnp.where((y // step) % 2 == 1, jnp.flip(apart, y_axis + 1), apart).reshape(shape)
            step *= 2
        return value

    length = wide * 2 * held
    chunks = length // CHUNK
    if share % CHUNK == 0:
        across = share // CHUNK
        numbers = jnp.arange(chunks, dtype=jnp.int32).reshape(2, depth, wide, across)
        order = flips(
            jnp.arange(chunks, dtype=jnp.int32).reshape(wide, 2, depth, across), 0, 1
        )
        order = jnp.transpose(order, (1, 2, 0, 3)).reshape(-1)

        def to_natural(value):
            return value

        from_natural = to_natural
    else:
        order = jnp.arange(chunks, dtype=jnp.int32)

        def to_natural(value):
            apart = flips(value.reshape(-1, wide, 2, depth, share), 1, 2)
            return jnp.transpose(apart, (0, 2, 3, 1, 4)).reshape(value.shape)

        def from_natural(value):
            apart = jnp.transpose(value.reshape(-1, 2, depth, wide, share), (0, 3, 1, 2, 4))
            return flips(apart, 1, 2).reshape(value.shape)

    segment = lax.dynamic_index_in_dim(segment_ids[:, 0], z, 0, False)
    last = segment.reshape(chunks, CHUNK)[:, -1]
    seg_row = segment[None, :]
    seg_col = segment[:, None]
    rows_nat = to_natural(rows)
    next_block()
    next_half()
    saved = attend_forward(
        last, order, seg_row, seg_col, rows_nat, jnp.transpose(maps, (0, 2, 1)),
        (ffn_own[1],),
    )
    mixed = from_natural(saved[0])

    out_own = join_heads(after(out_blocks, ffn_other[0]))
    out_mat = jnp.concatenate([out_own, over_x(out_own)], axis=1)
    rank_rows = mm(out_down, mixed, 0, 0).astype(BF16)
    split = 2 * held

    def branch(part, *waits):
        def make(*sent):
            rows_in = after(mixed[:, part], *waits) if waits else mixed[:, part]
            return (mm(rows_in, out_mat, 0, 0) + mm(rank_rows[:, part], out_lift, 0, 0)).astype(BF16)

        return make

    chip_part, other_part = slice(0, split), slice(split, length)
    last_own = [over_z(ffn_own[2][:2])]
    last_own.append(over_z(after(ffn_own[2][2:], last_own[0])))
    next_half()
    branch_sum, _, _ = reduce_tokens(
        branch(chip_part), branch(other_part, ffn_own[2], ffn_other[1]), (ffn_other[2],)
    )
    middle = layer_in + branch_sum
    last_other = [over_x(part) for part in last_own]

    scale_two = rms(middle)
    ffn_pieces = gather_tokens((middle * scale_two * gain_two).astype(BF16))
    ffn_pieces = ffn_pieces[:2] + after(ffn_pieces[2:], last_own[0])
    ffn_rows = stack_rows(ffn_pieces)
    grad_out = trade_z(after(cotangent[:, 0, 0], last_own[1]))
    grad_out = rotate(after(grad_out, middle).reshape(held, width))
    grads = stack_rows(gather_tokens(grad_out))
    last_other[0] = after(last_other[0], ffn_rows)
    own_gate, own_up, own_down = [
        jnp.concatenate([block[i] for block in ffn_own] + [last_own[i // 2][i % 2]], axis=0)
        for i in range(3)
    ]
    other_gate, other_up, other_down = [
        jnp.concatenate([block[i] for block in ffn_other] + [last_other[i // 2][i % 2]], axis=0)
        for i in range(3)
    ]
    chip_place = (0, split)
    other_place = (split, length - split)
    gates, ups, hidden = gate_forward(
        ffn_rows, own_gate, other_gate, own_up, other_up, (last_other[1],)
    )

    def ffn_forward(place):
        return lambda *sent: sum_products([hidden], [own_down], [other_down], *place)

    swap = x.reshape(1).astype(jnp.int32)

    def sum_x(value):
        return lax.psum_scatter(value, "rows", scatter_dimension=0, tiled=False)

    down_full = weight_grad_halves(hidden, grads, swap)
    down_sums = sum_x(down_full).reshape(depth, -1, half)
    ffn_out, ffn_sent, ffn_parts = reduce_tokens(ffn_forward(chip_place), ffn_forward(other_place))

    grad_gates, grad_ups = gate_backward(
        grads, own_down, other_down, gates, ups, (down_full, ffn_parts[0], *ffn_sent)
    )

    def ffn_back(place, wait):
        return lambda sent=(): sum_products(
            [grad_gates, grad_ups],
            [own_gate, own_up],
            [other_gate, other_up],
            *place,
            (*wait, *sent),
        )

    output = trade_z(rotate((middle + ffn_out).astype(BF16)).reshape(depth, share, width))
    gate_full = weight_grad_halves(grad_gates, ffn_rows, swap, tuple(ffn_parts[1:]))
    gate_sums = sum_x(gate_full).reshape(depth, -1, half)
    up_full = weight_grad_halves(grad_ups, ffn_rows, swap, (gate_full,))
    up_sums = sum_x(up_full).reshape(depth, -1, half)
    down_traded = trade_z(turn(down_sums, 0))
    grad_ffn, grad_ffn_sent, _ = reduce_tokens(
        ffn_back(chip_place, ()),
        ffn_back(other_place, ()),
        (gate_full, up_full, down_traded),
    )

    grad_mid_norm, gain_two_grad = norm_back(middle, gain_two, scale_two, grad_ffn)
    grad_middle = grad_out.astype(F32) + grad_mid_norm

    def halves(value):
        middle_at = value.shape[-1] // 2
        first, second = value[..., :middle_at], value[..., middle_at:]
        return jnp.where(x == 0, first, second), jnp.where(x == 0, second, first)

    grad_branch = stack_rows(gather_tokens(grad_middle.astype(BF16)))
    grad_olow = mm(out_lift, grad_branch, 1, 1).astype(BF16)
    grad_mixed = (mm(out_mat, grad_branch, 1, 1) + mm(out_down, grad_olow)).astype(BF16)
    gate_sums = after(gate_sums, grad_middle)
    up_sums = after(up_sums, grad_branch)
    gate_traded = trade_z(after(turn(gate_sums, 0), output))
    up_shifted = [over_z(up_sums[depth - k], k) for k in range(1, depth)]
    out_lift_grad = mm(rank_rows, grad_branch)
    out_down_grad = mm(mixed, grad_olow, 1, 1)
    out_grads = [mm(mixed, grad_branch[:, cut]) for cut in (slice(0, half), slice(half, width))]
    down_lift = halves(out_down_grad)
    out_halves = [
        jnp.concatenate([a, b], axis=1).astype(BF16) for a, b in zip(out_grads, down_lift)
    ]
    out_moved = over_x(out_halves[1])

    grad_rows, maps_grad = attend_backward(
        last, order, seg_row, seg_col, rows_nat, maps, lift, saved, to_natural(grad_mixed),
        (out_moved, output),
    )
    grad_rows = after(from_natural(grad_rows), gate_traded, up_shifted)

    quarter = half // 2
    rank_own = rank // 4
    maps_own = HD // 4

    def part_of(value, place):
        sizes = (quarter, rank_own, maps_own)
        start = 0
        parts = []
        for size in sizes:
            if start < value.shape[1]:
                parts.append(lax.dynamic_slice_in_dim(value, start + place * size, size, 1))
            start += 2 * size
        return jnp.concatenate(parts, axis=1).astype(BF16)

    def by_depth(value, height):
        return value.reshape(near, height, value.shape[-1])

    def collect(own_half, moved, blocks, *waits):
        summed = own_half.astype(F32) + moved.astype(F32)

        def ready(place):
            return blocks(part_of(summed, place))

        return shift_sum(in_order(ready(c), over_c(ready(1 - c)), 0), *waits)

    def project_back(part):
        def make(*sent):
            return jnp.concatenate(
                [mm(grad_rows[:, part], weight, 0, 0).astype(BF16) for weight in (project_own, project_other)],
                axis=1,
            )

        return make

    grad_normed, normed_sent, _ = reduce_tokens(
        project_back(chip_part), project_back(other_part)
    )
    grad_in_norm, gain_one_grad = norm_back(layer_in, gain_one, scale_one, grad_normed)
    grad_in = rotate((grad_middle + grad_in_norm).astype(BF16)).reshape(depth, share, width)
    input_grad = trade_z(grad_in)

    late_rows = after(grad_rows, *normed_sent)
    project_grad = [
        mm(late_rows[:, chip_part], normed[0][:, cut]) + mm(late_rows[:, other_part], normed[1][:, cut])
        for cut in (slice(0, half), slice(half, width))
    ]
    lift_grad = mm(low_rows, late_rows[:row_count], 1, 1)[: 3 * rank].reshape(3, rank, row_count)
    column = lax.broadcasted_iota(jnp.int32, (3, 1, row_count), 2)
    owner_of = (column >= query_rows).astype(jnp.int32) + (column >= query_rows + key_rows)
    kind = lax.broadcasted_iota(jnp.int32, (3, 1, row_count), 0)
    lift_grad = jnp.sum(jnp.where(owner_of == kind, lift_grad, 0.0), axis=0).T

    out_sum = collect(
        out_halves[0],
        after(out_moved, *normed_sent),
        lambda value: by_depth(value, block_rows),
        grad_in,
    )

    out_grad = out_sum[:, :quarter]
    output_down_grad = out_sum[:, quarter : quarter + rank_own]

    lift_halves = halves(lift_grad)
    maps_halves = halves(
        jnp.concatenate(
            [maps_grad.reshape(query_rows, HD), jnp.zeros((2 * key_rows, HD), F32)], axis=0
        )
    )
    late_halves = [
        jnp.concatenate(
            [project_grad[i][:row_count], lift_halves[i], maps_halves[i]], axis=1
        ).astype(BF16)
        for i in range(2)
    ]
    late_sum = collect(
        late_halves[0],
        after(over_x(late_halves[1]), grad_in),
        lambda value: jnp.concatenate(
            [
                by_depth(value[:query_rows], block_rows),
                by_depth(value[query_rows : query_rows + key_rows], HD),
                by_depth(value[query_rows + key_rows :], HD),
            ],
            axis=1,
        ),
    )
    query_grad = late_sum[:block_rows, :quarter].T
    query_lift_grad = late_sum[:block_rows, quarter : quarter + rank_own].T
    feature_maps_grad = jnp.transpose(
        late_sum[:block_rows, quarter + rank_own :].reshape(per, HD, maps_own), (0, 2, 1)
    )
    kv_sum = late_sum[block_rows:, : quarter + rank_own].reshape(2, HD, quarter + rank_own)
    kv_sum = jnp.where(
        lax.broadcasted_iota(jnp.int32, (kv_depth, 1, 1, 1), 0) == kv_pick, kv_sum[None], 0.0
    ).astype(BF16)
    step = 1
    while step < wide:
        kv_sum = (kv_sum.astype(F32) + over_y(kv_sum, step).astype(F32)).astype(BF16)
        step *= 2
    kv_sum = gather_z(after(kv_sum, input_grad))
    kv_sum = jnp.transpose(kv_sum, (2, 4, 0, 1, 3)).reshape(2, quarter + rank_own, KV * HD)
    kv_sum = kv_sum.astype(F32)

    down_total = jnp.sum(after(down_traded, grad_in).astype(F32), axis=0)
    gate_total = jnp.sum(after(gate_traded, grad_in).astype(F32), axis=0)
    up_total = up_sums[0].astype(F32)
    for block in after(up_shifted, grad_in):
        up_total = up_total + block.astype(F32)

    def to_owner(total):
        total = total.astype(BF16)
        kept = lax.dynamic_slice_in_dim(total, c * quarter, quarter, 1)
        return in_order(kept, over_c(lax.dynamic_slice_in_dim(total, (1 - c) * quarter, quarter, 1)), 0)

    down_grad = to_owner(down_total).astype(F32)
    gate_grad = to_owner(gate_total).T.astype(F32)
    up_grad = to_owner(up_total).T.astype(F32)

    minor = jnp.concatenate(
        [
            gain_one_grad[None],
            gain_two_grad[None],
            jnp.concatenate([part[row_count : row_count + 3 * rank] for part in project_grad], axis=1),
            out_lift_grad,
        ],
        axis=0,
    )
    minor = minor[:, :half] + over_x(after(minor[:, half:], late_sum))
    minor = jnp.moveaxis(minor.reshape(-1, depth, wide, 2, half // (2 * heads_size)), 0, 3)
    minor = shift_sum(minor)
    total = lax.dynamic_index_in_dim(minor, y, 0, False)
    for k in range(1, wide):
        total = total + over_y(lax.dynamic_index_in_dim(minor, y ^ k, 0, False), k)
    minor = lax.dynamic_index_in_dim(total, c, 0, False) + over_c(
        lax.dynamic_index_in_dim(total, 1 - c, 0, False)
    )
    minor = minor.T
    return (
        output[:, None, None],
        input_grad[:, None, None].astype(F32),
        minor[:, 0],
        minor[:, 1],
        query_grad,
        kv_sum[0, :quarter],
        kv_sum[1, :quarter],
        out_grad,
        minor[:, 2 : 2 + rank],
        query_lift_grad,
        minor[:, 2 + rank : 2 + 2 * rank],
        kv_sum[0, quarter:],
        minor[:, 2 + 2 * rank : 2 + 3 * rank],
        kv_sum[1, quarter:],
        output_down_grad,
        minor[:, 2 + 3 * rank :].T,
        feature_maps_grad,
        gate_grad,
        up_grad,
        down_grad,
    )


def solution(mesh):
    placed = (
        P(None, "rows", "seq", "heads", None),
        P(None, "rows", None),
        P(None, "rows", "seq", "heads", None),
        P(("rows", "heads", "seq")),
        P(("rows", "heads", "seq")),
        P(("rows", "seq"), "heads"),
        P(("rows", "seq"), None),
        P(("rows", "seq"), None),
        P("heads", ("rows", "seq")),
        P(("rows", "heads", "seq"), None),
        P(("rows", "seq"), "heads"),
        P(("rows", "heads", "seq"), None),
        P(("rows", "seq"), None),
        P(("rows", "heads", "seq"), None),
        P(("rows", "seq"), None),
        P("heads", ("rows", "seq")),
        P(None, ("rows", "heads", "seq")),
        P("heads", ("rows", "seq"), None),
        P(("rows", "seq"), "heads"),
        P(("rows", "seq"), "heads"),
        P("heads", ("rows", "seq")),
    )
    return jax.shard_map(
        body,
        mesh=mesh,
        in_specs=placed,
        out_specs=(
            P(None, "rows", "seq", "heads", None),
            P(None, "rows", "seq", "heads", None),
            P(("rows", "heads", "seq")),
            P(("rows", "heads", "seq")),
            P(("rows", "seq"), "heads"),
            P(("rows", "seq"), None),
            P(("rows", "seq"), None),
            P("heads", ("rows", "seq")),
            P(("rows", "heads", "seq"), None),
            P(("rows", "seq"), "heads"),
            P(("rows", "heads", "seq"), None),
            P(("rows", "seq"), None),
            P(("rows", "heads", "seq"), None),
            P(("rows", "seq"), None),
            P("heads", ("rows", "seq")),
            P(None, ("rows", "heads", "seq")),
            P("heads", ("rows", "seq"), None),
            P(("rows", "seq"), "heads"),
            P(("rows", "seq"), "heads"),
            P("heads", ("rows", "seq")),
        ),
        check_vma=False,
    )
```

```python
import math

import jax
import jax.numpy as jnp
from jax import lax
from jax.experimental import pallas as pl
from jax.experimental.pallas import tpu as pltpu
from jax.sharding import PartitionSpec as P

HEADS = 32
KV = 8
HD = 64
WINDOW = 64
CHUNK = 2 * WINDOW
FEATS = 2 * HD
AUG = HD + 16
F32 = jnp.float32
PART = 512
BF16 = jnp.bfloat16


def mm(left, right, left_dim=1, right_dim=0):
    return lax.dot_general(
        left, right, (((left_dim,), (right_dim,)), ((), ())), preferred_element_type=F32
    )


def chunk_masks(chunk, seg_row, seg_own, seg_prev):
    place = lax.broadcasted_iota(jnp.int32, (CHUNK, CHUNK), 1)
    key = lax.broadcasted_iota(jnp.int32, (CHUNK, CHUNK), 0)
    same_own = seg_own == seg_row
    same_prev = (seg_prev - jnp.where(chunk == 0, 100, 0)) == seg_row
    far = -1e30
    bias_own = jnp.where(same_own & (key <= place) & (key > place - WINDOW), 0.0, far)
    bias_prev = jnp.where(same_prev & (key > place + WINDOW), 0.0, far)
    linear_prev = jnp.where(same_prev & (key <= place + WINDOW), 1.0, 0.0)
    linear_own = jnp.where(same_own & (key <= place - WINDOW), 1.0, 0.0)
    return bias_prev[WINDOW:], bias_own, linear_prev, linear_own[:WINDOW]


def turned(values):
    return jnp.transpose(values.astype(F32)).astype(BF16)


def with_ones(values):
    return jnp.concatenate([values, jnp.ones((AUG - HD, CHUNK), values.dtype)], axis=0)


def features_of(vectors, maps_t):
    logits = mm(maps_t, vectors)
    high = jnp.exp(logits - jnp.max(logits, axis=0, keepdims=True))
    low = jnp.exp(jnp.min(logits, axis=0, keepdims=True) - logits)
    high = high * (1.0 / jnp.sum(high, axis=0, keepdims=True))
    low = low * (1.0 / jnp.sum(low, axis=0, keepdims=True))
    return jnp.concatenate([high, low], axis=0)


def features_back(features, grad):
    product = features * grad
    high = product[:HD] - features[:HD] * jnp.sum(product[:HD], axis=0, keepdims=True)
    low = product[HD:] - features[HD:] * jnp.sum(product[HD:], axis=0, keepdims=True)
    return high - low


def forward_kernel(
    last_ref, order_ref, seg_row_ref, seg_own_ref, seg_prev_ref,
    q_ref, kt_ref, ktp_ref, vt_ref, vtp_ref, maps_t_ref,
    mixed_ref, peak_ref, den_ref, fq_ref, fkt_ref, fk_ref, state_out_ref,
    state_ref, fk_prev_ref,
):
    chunk = pl.program_id(0)
    head_count = fq_ref.shape[0]
    per_key = head_count * HD // kt_ref.shape[0]

    @pl.when(chunk == 0)
    def _():
        state_ref[...] = jnp.zeros_like(state_ref)
        fk_prev_ref[...] = jnp.zeros_like(fk_prev_ref)

    seg_row = seg_row_ref[...]
    bias_prev, bias_own, linear_prev, linear_own = chunk_masks(
        chunk, seg_row, seg_own_ref[...], seg_prev_ref[...]
    )
    tag_state = jnp.where(chunk >= 2, last_ref[jnp.maximum(chunk - 2, 0)], -1)
    tag_prev = jnp.where(chunk >= 1, last_ref[jnp.maximum(chunk - 1, 0)], -2)
    carried = jnp.where(seg_row == tag_state, 1.0, 0.0)
    joined = jnp.where(tag_state == tag_prev, 1.0, 0.0)
    keep_prev = jnp.where(seg_prev_ref[...] == tag_prev, 1.0, 0.0).astype(BF16)
    k_own = turned(kt_ref[...])
    k_prev = turned(ktp_ref[...])
    for head in range(head_count):
        group = head // per_key
        rows = slice(head * HD, (head + 1) * HD)
        key_rows = slice(group * HD, (group + 1) * HD)
        query = q_ref[rows, :]
        maps_t = maps_t_ref[head]
        feat_q = features_of(query, maps_t)
        feat_kt = features_of(kt_ref[key_rows, :], maps_t)
        fq_ref[head] = feat_q.astype(BF16)
        fkt_ref[head] = feat_kt.astype(BF16)
        feat_k = jnp.transpose(feat_kt).astype(BF16)
        fk_ref[head] = feat_k
        scaled = query * jnp.asarray(HD**-0.5, BF16)
        score_prev = mm(k_prev[WINDOW:, key_rows], scaled) + bias_prev
        score_own = mm(k_own[:, key_rows], scaled) + bias_own
        peak = jnp.maximum(
            jnp.max(score_prev, axis=0, keepdims=True), jnp.max(score_own, axis=0, keepdims=True)
        )
        weight_prev = jnp.exp(score_prev - peak)
        weight_own = jnp.exp(score_own - peak)
        damped = feat_q * jnp.exp(-peak)
        damped_low = damped.astype(BF16)
        fk_prev = fk_prev_ref[head]
        lin_prev = mm(fk_prev, damped_low) * linear_prev
        lin_own = mm(feat_k[:WINDOW], damped_low) * linear_own
        all_prev = jnp.concatenate([lin_prev[:WINDOW], lin_prev[WINDOW:] + weight_prev], axis=0)
        all_own = jnp.concatenate([lin_own + weight_own[:WINDOW], weight_own[WINDOW:]], axis=0)
        value_prev = with_ones(vtp_ref[key_rows, :])
        state = state_ref[head]
        state_low = state.astype(BF16)
        state_out_ref[0, head] = state_low
        total = (
            mm(value_prev, all_prev.astype(BF16))
            + mm(with_ones(vt_ref[key_rows, :]), all_own.astype(BF16))
            + mm(state_low, (damped * carried).astype(BF16))
        )
        den = total[HD : HD + 1]
        mixed_ref[rows, :] = (total[:HD] * (1.0 / den)).astype(BF16)
        peak_ref[head : head + 1, :] = peak
        den_ref[head : head + 1, :] = den
        state_ref[head] = state * joined + mm(value_prev, fk_prev * keep_prev)
        fk_prev_ref[head] = feat_k


def backward_kernel(
    last_ref, order_ref, seg_row_ref, seg_own_ref, seg_prev_ref,
    q_ref, kt_ref, ktp_ref, vt_ref, vtp_ref, maps_ref, lift_ref,
    mixed_ref, grad_ref, peak_ref, den_ref, fq_ref, fkt_ref, fktp_ref, fk_ref, fkp_ref, state_ref,
    grows_ref, gmaps_ref,
    gstate_ref, cphi_ref, ck_ref, cv_ref,
):
    step = pl.program_id(0)
    chunk = pl.num_programs(0) - 1 - step
    head_count = fq_ref.shape[0]
    group_count = kt_ref.shape[0] // HD
    per_key = head_count // group_count

    @pl.when(step == 0)
    def _():
        gstate_ref[...] = jnp.zeros_like(gstate_ref)
        cphi_ref[...] = jnp.zeros_like(cphi_ref)
        ck_ref[...] = jnp.zeros_like(ck_ref)
        cv_ref[...] = jnp.zeros_like(cv_ref)
        gmaps_ref[...] = jnp.zeros_like(gmaps_ref)

    seg_row = seg_row_ref[...]
    bias_prev, bias_own, linear_prev, linear_own = chunk_masks(
        chunk, seg_row, seg_own_ref[...], seg_prev_ref[...]
    )
    tag_state = jnp.where(chunk >= 2, last_ref[jnp.maximum(chunk - 2, 0)], -1)
    tag_prev = jnp.where(chunk >= 1, last_ref[jnp.maximum(chunk - 1, 0)], -2)
    carried = jnp.where(seg_row == tag_state, 1.0, 0.0)
    joined = jnp.where(tag_state == tag_prev, 1.0, 0.0)
    keep_col = jnp.where(seg_prev_ref[...] == tag_prev, 1.0, 0.0)
    keep_prev = jnp.transpose(jnp.broadcast_to(keep_col, (CHUNK, CHUNK)))[:1]
    scale = HD**-0.5
    none = jnp.zeros((WINDOW, CHUNK), F32)
    k_own = turned(kt_ref[...])
    k_prev = turned(ktp_ref[...])
    v_own = turned(vt_ref[...])
    v_prev = turned(vtp_ref[...])
    for group in range(group_count):
        key_rows = slice(group * HD, (group + 1) * HD)
        key_t = kt_ref[key_rows, :]
        value_prev = with_ones(vtp_ref[key_rows, :])
        own_k = ck_ref[group]
        own_v = cv_ref[group]
        next_k = None
        next_v = None
        for head in range(group * per_key, (group + 1) * per_key):
            rows = slice(head * HD, (head + 1) * HD)
            query = q_ref[rows, :]
            scaled = query * jnp.asarray(scale, BF16)
            peak = peak_ref[head : head + 1, :]
            den = den_ref[head : head + 1, :]
            weight_prev = jnp.exp(mm(k_prev[WINDOW:, key_rows], scaled) + bias_prev - peak)
            weight_own = jnp.exp(mm(k_own[:, key_rows], scaled) + bias_own - peak)
            damp = jnp.exp(-peak)
            feat_q = fq_ref[head].astype(F32)
            damped = feat_q * damp
            damped_low = damped.astype(BF16)
            carried_low = (damped * carried).astype(BF16)
            lin_prev = mm(fkp_ref[head], damped_low) * linear_prev
            lin_own = mm(fk_ref[head, :WINDOW, :], damped_low) * linear_own
            all_prev = jnp.concatenate([lin_prev[:WINDOW], lin_prev[WINDOW:] + weight_prev], axis=0)
            all_own = jnp.concatenate([lin_own + weight_own[:WINDOW], weight_own[WINDOW:]], axis=0)
            grad = grad_ref[rows, :].astype(F32)
            dnum = grad * (1.0 / den)
            dden = -jnp.sum(dnum * mixed_ref[rows, :].astype(F32), axis=0, keepdims=True)
            dnum_low = dnum.astype(BF16)
            dtotal = jnp.concatenate(
                [dnum, dden, jnp.zeros((AUG - HD - 1, CHUNK), F32)], axis=0
            ).astype(BF16)
            dall_prev = mm(v_prev[:, key_rows], dnum_low) + dden
            dall_own = mm(v_own[:, key_rows], dnum_low) + dden
            dscore_prev = jnp.concatenate([none, weight_prev * dall_prev[WINDOW:]], axis=0).astype(BF16)
            dscore_own = (weight_own * dall_own).astype(BF16)
            dlin_prev = (linear_prev * dall_prev).astype(BF16)
            dlin_own = jnp.concatenate([linear_own * dall_own[:WINDOW], none], axis=0).astype(BF16)
            gstate = gstate_ref[head]
            gstate_low = gstate.astype(BF16)
            ddamped = (
                mm(fktp_ref[head], dlin_prev)
                + mm(fkt_ref[head], dlin_own)
                + carried * mm(state_ref[0, head], dtotal, 0, 0)
            )
            dlogit_q = features_back(feat_q, ddamped * damp).astype(BF16)
            maps = maps_ref[head]
            grad_q = (
                mm(ktp_ref[key_rows, :], dscore_prev) + mm(key_t, dscore_own)
            ) * scale + mm(maps, dlogit_q)
            grows_ref[rows, :] = grad_q.astype(BF16)
            dphi_own = cphi_ref[head] + mm(damped_low, dlin_own, 1, 1)
            cphi_ref[head] = (
                mm(damped_low, dlin_prev, 1, 1) + mm(gstate_low, value_prev, 0, 0) * keep_prev
            )
            dlogit_k = features_back(fkt_ref[head].astype(F32), dphi_own).astype(BF16)
            gmaps_ref[head] += mm(dlogit_q, query, 1, 1) + mm(dlogit_k, key_t, 1, 1)
            own_k += mm(scaled, dscore_own, 1, 1) + mm(maps, dlogit_k)
            part_k = mm(scaled, dscore_prev, 1, 1)
            own_v += mm(dnum_low, all_own.astype(BF16), 1, 1)
            part_v = (
                mm(dnum_low, all_prev.astype(BF16), 1, 1)
                + mm(gstate_low[:HD], fktp_ref[head]) * keep_prev
            )
            next_k = part_k if next_k is None else next_k + part_k
            next_v = part_v if next_v is None else next_v + part_v
            gstate_ref[head] = gstate * joined + mm(dtotal, carried_low, 1, 1)
        key_start = (head_count + group) * HD
        value_start = (head_count + group_count + group) * HD
        grows_ref[key_start : key_start + HD, :] = own_k.astype(BF16)
        grows_ref[value_start : value_start + HD, :] = own_v.astype(BF16)
        ck_ref[group] = next_k
        cv_ref[group] = next_v
    width = lift_ref.shape[1]
    grows_ref[width:, :] = mm(lift_ref[...], grows_ref[:width, :]).astype(BF16)


def attend_forward(last, order, seg_row, seg_col, rows, maps_t, waits=()):
    heads = maps_t.shape[0]
    groups, length = (rows.shape[0] // HD - heads) // 2, rows.shape[1]
    chunks = length // CHUNK
    first = heads // groups

    def before(c):
        return jnp.maximum(c - 1, 0)

    def spec(count, block, shift):
        return pl.BlockSpec((count * HD, CHUNK), lambda c, last, order: (block, order[shift(c)]))

    def here(c):
        return c

    stat = pl.BlockSpec((heads, CHUNK), lambda c, last, order: (0, c))
    feat_t = pl.BlockSpec((heads, FEATS, CHUNK), lambda c, last, order: (0, 0, c))
    return pl.pallas_call(
        ignoring(forward_kernel, 11, len(waits)),
        grid_spec=pltpu.PrefetchScalarGridSpec(
            num_scalar_prefetch=2,
            grid=(chunks,),
            in_specs=[
                pl.BlockSpec((1, CHUNK), lambda c, last, order: (0, c)),
                pl.BlockSpec((CHUNK, 1), lambda c, last, order: (c, 0)),
                pl.BlockSpec((CHUNK, 1), lambda c, last, order: (before(c), 0)),
                spec(heads, 0, here),
                spec(groups, first, here),
                spec(groups, first, before),
                spec(groups, first + 1, here),
                spec(groups, first + 1, before),
                pl.BlockSpec((heads, HD, HD), lambda c, last, order: (0, 0, 0)),
            ]
            + [pl.BlockSpec(memory_space=pl.ANY)] * len(waits),
            out_specs=[
                spec(heads, 0, here), stat, stat,
                feat_t, feat_t,
                pl.BlockSpec((heads, CHUNK, FEATS), lambda c, last, order: (0, c, 0)),
                pl.BlockSpec((1, heads, AUG, FEATS), lambda c, last, order: (c, 0, 0, 0)),
            ],
            scratch_shapes=[
                pltpu.VMEM((heads, AUG, FEATS), F32),
                pltpu.VMEM((heads, CHUNK, FEATS), BF16),
            ],
        ),
        out_shape=[
            jax.ShapeDtypeStruct((heads * HD, length), BF16),
            jax.ShapeDtypeStruct((heads, length), F32),
            jax.ShapeDtypeStruct((heads, length), F32),
            jax.ShapeDtypeStruct((heads, FEATS, length), BF16),
            jax.ShapeDtypeStruct((heads, FEATS, length), BF16),
            jax.ShapeDtypeStruct((heads, length, FEATS), BF16),
            jax.ShapeDtypeStruct((chunks, heads, AUG, FEATS), BF16),
        ],
        compiler_params=pltpu.CompilerParams(
            dimension_semantics=("arbitrary",), vmem_limit_bytes=32 * 2**20
        ),
        cost_estimate=pl.CostEstimate(
            flops=heads * length * 1060000, bytes_accessed=heads * length * 400, transcendentals=0
        ),
        name="attend_forward",
    )(
        last, order, seg_row, seg_col, seg_col, rows, rows, rows, rows, rows, maps_t, *waits
    )


def attend_backward(
    last, order, seg_row, seg_col, rows, maps, lift, saved, grad, waits=()
):
    mixed, peak, den, fq, fkt, fk, states = saved
    heads = maps.shape[0]
    groups, length = (rows.shape[0] // HD - heads) // 2, rows.shape[1]
    chunks = length // CHUNK
    first = heads // groups
    height = lift.shape[0] + lift.shape[1]

    def here(s):
        return chunks - 1 - s

    def before(s):
        return jnp.maximum(chunks - 2 - s, 0)

    def spec(count, block, shift):
        return pl.BlockSpec((count * HD, CHUNK), lambda s, last, order: (block, order[shift(s)]))

    def feat_t(shift):
        return pl.BlockSpec((heads, FEATS, CHUNK), lambda s, last, order: (0, 0, shift(s)))

    def feat(shift):
        return pl.BlockSpec((heads, CHUNK, FEATS), lambda s, last, order: (0, shift(s), 0))

    stat = pl.BlockSpec((heads, CHUNK), lambda s, last, order: (0, here(s)))
    whole = pl.BlockSpec((heads, HD, HD), lambda s, last, order: (0, 0, 0))
    return pl.pallas_call(
        ignoring(backward_kernel, 22, len(waits)),
        grid_spec=pltpu.PrefetchScalarGridSpec(
            num_scalar_prefetch=2,
            grid=(chunks,),
            in_specs=[
                pl.BlockSpec((1, CHUNK), lambda s, last, order: (0, here(s))),
                pl.BlockSpec((CHUNK, 1), lambda s, last, order: (here(s), 0)),
                pl.BlockSpec((CHUNK, 1), lambda s, last, order: (before(s), 0)),
                spec(heads, 0, here),
                spec(groups, first, here), spec(groups, first, before),
                spec(groups, first + 1, here), spec(groups, first + 1, before),
                whole,
                pl.BlockSpec(lift.shape, lambda s, last, order: (0, 0)),
                spec(heads, 0, here), spec(heads, 0, here), stat, stat,
                feat_t(here), feat_t(here), feat_t(before), feat(here), feat(before),
                pl.BlockSpec((1, heads, AUG, FEATS), lambda s, last, order: (here(s), 0, 0, 0)),
            ]
            + [pl.BlockSpec(memory_space=pl.ANY)] * len(waits),
            out_specs=[
                pl.BlockSpec((height, CHUNK), lambda s, last, order: (0, order[here(s)])),
                whole,
            ],
            scratch_shapes=[
                pltpu.VMEM((heads, AUG, FEATS), F32),
                pltpu.VMEM((heads, FEATS, CHUNK), F32),
                pltpu.VMEM((groups, HD, CHUNK), F32),
                pltpu.VMEM((groups, HD, CHUNK), F32),
            ],
        ),
        out_shape=[
            jax.ShapeDtypeStruct((height, length), BF16),
            jax.ShapeDtypeStruct((heads, HD, HD), F32),
        ],
        compiler_params=pltpu.CompilerParams(
            dimension_semantics=("arbitrary",), vmem_limit_bytes=32 * 2**20
        ),
        cost_estimate=pl.CostEstimate(
            flops=heads * length * 2100000, bytes_accessed=heads * length * 600, transcendentals=0
        ),
        name="attend_backward",
    )(
        last, order, seg_row, seg_col, seg_col, rows, rows, rows, rows, rows, maps, lift, mixed, grad, peak, den, fq, fkt, fkt, fk, fk, states, *waits,
    )


def ignoring(kernel, inputs, waits):
    def body(*refs):
        kernel(*refs[:inputs], *refs[inputs + waits :])

    return body


def after(value, *others):
    values = jax.tree.leaves(value)
    tokens = jax.tree.leaves(others)
    anywhere = pl.BlockSpec(memory_space=pl.ANY)
    out = pl.pallas_call(
        lambda *refs: None,
        in_specs=[anywhere] * (len(values) + len(tokens)),
        out_specs=[anywhere] * len(values),
        out_shape=[jax.ShapeDtypeStruct(v.shape, v.dtype) for v in values],
        input_output_aliases={i: i for i in range(len(values))},
        cost_estimate=pl.CostEstimate(flops=0, bytes_accessed=0, transcendentals=0),
        name="after",
    )(*values, *tokens)
    return jax.tree.unflatten(jax.tree.structure(value), out)


def stack_rows(pieces):
    rows, columns = pieces[0].shape
    tall = min(256, rows)
    steps = rows // tall
    count = len(pieces)

    def kernel(*refs):
        for place in range(count):

            @pl.when(pl.program_id(0) == place)
            def _(place=place):
                refs[-1][...] = refs[place][...]

    def spec(place):
        def at(i, j):
            return (jnp.where(i < place, 0, jnp.where(i > place, steps - 1, j)), 0)

        return pl.BlockSpec((tall, columns), at)

    return pl.pallas_call(
        kernel,
        grid=(count, steps),
        in_specs=[spec(place) for place in range(count)],
        out_specs=pl.BlockSpec((tall, columns), lambda i, j: (i * steps + j, 0)),
        out_shape=jax.ShapeDtypeStruct((count * rows, columns), pieces[0].dtype),
        cost_estimate=pl.CostEstimate(
            flops=0, bytes_accessed=count * rows * columns, transcendentals=0
        ),
        name="stack_rows",
    )(*pieces)


def weight_grad_kernel(left_ref, right_ref, out_ref):
    out_ref[...] = mm(left_ref[...], right_ref[...], 0, 0).astype(BF16)


def weight_grad(left, right, part, waits=()):
    tokens, rows = left.shape
    half = right.shape[1] // 2
    tall = min(512, rows)
    return dense_call(
        weight_grad_kernel,
        (rows // tall,),
        [
            pl.BlockSpec((tokens, tall), lambda i: (0, i)),
            pl.BlockSpec((tokens, half), lambda i: (0, part)),
        ],
        pl.BlockSpec((tall, half), lambda i: (i, 0)),
        jax.ShapeDtypeStruct((rows, half), BF16),
        2 * tokens * rows * half,
        "weight_grad",
        waits,
    )(left, right, *waits)


def weight_grad_halves(left, right, swap, waits=()):
    tokens, rows = left.shape
    half = right.shape[1] // 2
    tall = min(512, rows)

    def kernel(swap_ref, left_ref, right_ref, *refs):
        refs[-1][0] = mm(left_ref[...], right_ref[...], 0, 0).astype(BF16)

    return pl.pallas_call(
        kernel,
        grid_spec=pltpu.PrefetchScalarGridSpec(
            num_scalar_prefetch=1,
            grid=(2, rows // tall),
            in_specs=[
                pl.BlockSpec((tokens, tall), lambda p, i, swap: (0, i)),
                pl.BlockSpec((tokens, half), lambda p, i, swap: (0, p + swap[0] - 2 * p * swap[0])),
            ]
            + [pl.BlockSpec(memory_space=pl.ANY)] * len(waits),
            out_specs=pl.BlockSpec((1, tall, half), lambda p, i, swap: (p, i, 0)),
        ),
        out_shape=jax.ShapeDtypeStruct((2, rows, half), BF16),
        compiler_params=pltpu.CompilerParams(
            dimension_semantics=("arbitrary", "arbitrary"), vmem_limit_bytes=48 * 2**20
        ),
        cost_estimate=pl.CostEstimate(
            flops=tokens * rows * half, bytes_accessed=rows * half, transcendentals=0
        ),
        name="weight_grad_halves",
    )(swap, left, right, *waits)


def dense_call(kernel, grid, in_specs, out_specs, out_shape, flops, name, waits=()):
    in_specs = in_specs + [pl.BlockSpec(memory_space=pl.ANY)] * len(waits)
    return pl.pallas_call(
        ignoring(kernel, len(in_specs) - len(waits), len(waits)),
        grid=grid,
        in_specs=in_specs,
        out_specs=out_specs,
        out_shape=out_shape,
        compiler_params=pltpu.CompilerParams(
            dimension_semantics=("arbitrary",) * len(grid), vmem_limit_bytes=48 * 2**20
        ),
        cost_estimate=pl.CostEstimate(
            flops=flops // 3, bytes_accessed=flops // 8000, transcendentals=0
        ),
        name=name,
    )


def sigmoid_of(values):
    return 0.5 * jnp.tanh(0.5 * values) + 0.5


def row_parts(count):
    size = min(PART, count)
    return [slice(at, at + size) for at in range(0, count, size)]


def gate_kernel(rows_ref, own_gate, other_gate, own_up, other_up, gate_ref, up_ref, hidden_ref):
    half = own_gate.shape[1]
    for part in row_parts(rows_ref.shape[0]):
        left = rows_ref[part, :half]
        right = rows_ref[part, half:]
        gate = mm(left, own_gate[...], 1, 1) + mm(right, other_gate[...], 1, 1)
        up = mm(left, own_up[...], 1, 1) + mm(right, other_up[...], 1, 1)
        gate_ref[part, :] = gate.astype(BF16)
        up_ref[part, :] = up.astype(BF16)
        hidden_ref[part, :] = (gate * sigmoid_of(gate) * up).astype(BF16)


def gate_back_kernel(grad_ref, own_down, other_down, gate_ref, up_ref, dgate_ref, dup_ref):
    half = own_down.shape[1]
    for part in row_parts(grad_ref.shape[0]):
        grad = mm(grad_ref[part, :half], own_down[...], 1, 1) + mm(
            grad_ref[part, half:], other_down[...], 1, 1
        )
        gate = gate_ref[part, :].astype(F32)
        sigmoid = sigmoid_of(gate)
        grad_swish = grad * sigmoid
        dup_ref[part, :] = (grad_swish * gate).astype(BF16)
        dgate_ref[part, :] = (
            grad_swish * up_ref[part, :].astype(F32) * (1.0 + gate * (1.0 - sigmoid))
        ).astype(BF16)


def sum_kernel(count, lefts_and_weights, out_ref):
    lefts = lefts_and_weights[:count]
    owns = lefts_and_weights[count : 2 * count]
    others = lefts_and_weights[2 * count :]
    column = pl.program_id(0)

    def write(weights):
        total = mm(lefts[0][...], weights[0][...])
        for left, weight in zip(lefts[1:], weights[1:]):
            total = total + mm(left[...], weight[...])
        out_ref[...] = total.astype(BF16)

    across = pl.num_programs(0) // 2

    @pl.when(column < across)
    def _():
        write(owns)

    @pl.when(column >= across)
    def _():
        write(others)


def gate_forward(rows, own_gate, other_gate, own_up, other_up, waits=()):
    tokens, width = rows.shape
    hidden, half = own_gate.shape
    tall, wide = min(512, tokens), min(1024, hidden)
    weight = pl.BlockSpec((wide, half), lambda j, i: (j, 0))
    out = pl.BlockSpec((tall, wide), lambda j, i: (i, j))
    return dense_call(
        gate_kernel,
        (hidden // wide, tokens // tall),
        [pl.BlockSpec((tall, width), lambda j, i: (i, 0))] + [weight] * 4,
        [out] * 3,
        [jax.ShapeDtypeStruct((tokens, hidden), BF16)] * 3,
        4 * tokens * width * hidden,
        "gate_forward",
        waits,
    )(rows, own_gate, other_gate, own_up, other_up, *waits)


def gate_backward(grad, own_down, other_down, gate, up, waits=()):
    tokens, width = grad.shape
    hidden, half = own_down.shape
    tall, wide = min(512, tokens), min(1024, hidden)
    weight = pl.BlockSpec((wide, half), lambda j, i: (j, 0))
    out = pl.BlockSpec((tall, wide), lambda j, i: (i, j))
    return dense_call(
        gate_back_kernel,
        (hidden // wide, tokens // tall),
        [pl.BlockSpec((tall, width), lambda j, i: (i, 0)), weight, weight, out, out],
        [out] * 2,
        [jax.ShapeDtypeStruct((tokens, hidden), BF16)] * 2,
        2 * tokens * width * hidden,
        "gate_backward",
        waits,
    )(grad, own_down, other_down, gate, up, *waits)


def sum_products(lefts, owns, others, start, tokens, waits=()):
    count = len(lefts)
    depth = lefts[0].shape[1]
    half = owns[0].shape[1]
    tall, wide = math.gcd(math.gcd(start, tokens), 1024), min(512, half)
    across = half // wide
    first = start // tall

    def kernel(*refs):
        sum_kernel(count, refs[:-1], refs[-1])

    left = pl.BlockSpec((tall, depth), lambda j, i: (first + i, 0))
    own = pl.BlockSpec((depth, wide), lambda j, i: (0, jnp.minimum(j, across - 1)))
    other = pl.BlockSpec((depth, wide), lambda j, i: (0, jnp.maximum(j - across, 0)))
    return dense_call(
        kernel,
        (2 * across, tokens // tall),
        [left] * count + [own] * count + [other] * count,
        pl.BlockSpec((tall, wide), lambda j, i: (i, j)),
        jax.ShapeDtypeStruct((tokens, 2 * half), BF16),
        4 * count * tokens * depth * half,
        "sum_products",
        waits,
    )(*lefts, *owns, *others, *waits)


ALL = ("rows", "heads", "seq")
SWAP = [(0, 1), (1, 0)]
LOWS = 32


def over_x(value):
    return lax.ppermute(value, "rows", SWAP)


def over_c(value):
    return lax.ppermute(value, "seq", SWAP)


def body(
    inputs,
    segment_ids,
    cotangent,
    attn_gain,
    ffn_gain,
    query_weight,
    key_weight,
    value_weight,
    output_weight,
    query_down,
    query_lift,
    key_down,
    key_lift,
    value_down,
    value_lift,
    output_down,
    output_lift,
    feature_maps,
    gate_weight,
    up_weight,
    down_weight,
):
    heads_size = lax.axis_size("heads")
    depth = inputs.shape[0]
    wide = heads_size // depth
    per = HEADS // heads_size
    near = depth // 2
    block_rows = per * HD
    rank = query_down.shape[1]
    width = inputs.shape[-1]
    half = width // 2
    share = inputs.shape[3]
    held = depth * share
    head_index = lax.axis_index("heads")
    x = lax.axis_index("rows")
    c = lax.axis_index("seq")
    z = head_index // wide
    y = head_index % wide
    kv_pick = y * per // (HEADS // KV)
    kv_depth = KV // depth

    def over_y(value, k):
        return lax.ppermute(
            value,
            "heads",
            [(a * wide + b, a * wide + (b ^ k)) for a in range(depth) for b in range(wide)],
        )

    def over_z(value, k=1):
        return lax.ppermute(
            value,
            "heads",
            [(a * wide + b, (a + k) % depth * wide + b) for a in range(depth) for b in range(wide)],
        )

    def trade_z(value):
        groups = [[a * wide + b for a in range(depth)] for b in range(wide)]
        return lax.all_to_all(
            value, "heads", split_axis=0, concat_axis=0, tiled=True, axis_index_groups=groups
        )

    def gather_z(block):
        return trade_z(jnp.broadcast_to(block[None], (depth,) + block.shape))

    def scatter_z(blocks):
        return jnp.sum(trade_z(blocks).astype(F32), axis=0)

    def trade_c(value, split, concat):
        return lax.all_to_all(value, "seq", split_axis=split, concat_axis=concat, tiled=True)

    def turn(value, axis):
        return jnp.stack(
            [lax.dynamic_index_in_dim(value, (z - j) % depth, axis, False) for j in range(depth)],
            axis,
        )

    def in_order(kept, moved, axis):
        return jnp.where(
            c == 0,
            jnp.concatenate([kept, moved], axis=axis),
            jnp.concatenate([moved, kept], axis=axis),
        )

    def rotate(value):
        return jnp.where(
            x == 1, jnp.concatenate([value[..., half:], value[..., :half]], axis=-1), value
        )

    def shift_sum(blocks, *waits):
        total = lax.dynamic_index_in_dim(blocks, z, 0, False).astype(F32)
        moved = [
            over_z(lax.dynamic_index_in_dim(blocks, (z + k) % depth, 0, False), k)
            for k in range(1, depth)
        ]
        for block in after(moved, *waits) if waits else moved:
            total = total + block.astype(F32)
        return total

    def gather_tokens(value, *waits):
        pieces = [value, over_c(value)]
        for k in range(1, wide):
            moved = over_y(value, k)
            if waits:
                moved = after(moved, *waits)
            pieces += [moved, over_c(moved)]
        return pieces

    def reduce_tokens(make_chip, make_others, waits=()):
        others = make_others()
        sent = []
        arrived = []
        for k in range(1, wide):
            start = (k - 1) * 2 * held
            mine = others[start : start + held]
            moved = over_c(others[start + held : start + 2 * held])
            sent.append((mine.astype(F32) + moved.astype(F32)).astype(BF16))
            arrived.append(over_y(sent[-1], k))
        chip = make_chip(sent)
        total = chip[:held].astype(F32) + over_c(chip[held:]).astype(F32)
        if waits:
            arrived = [after(piece, *waits) for piece in arrived]
        for piece in arrived:
            total = total + piece.astype(F32)
        return total, sent, (chip, *arrived)

    def rms(values):
        return lax.rsqrt(jnp.mean(values * values, axis=-1, keepdims=True) + 1e-05)

    def norm_back(values, gain, scale, grad):
        unit = values * scale
        scaled = grad * gain
        return (
            scale * (scaled - unit * jnp.mean(scaled * unit, axis=-1, keepdims=True)),
            jnp.sum(grad * unit, axis=0),
        )

    small = (
        attn_gain, ffn_gain, query_down, key_down, value_down, output_lift,
        query_lift, key_lift, value_lift, output_down, feature_maps,
    )
    packed = jnp.concatenate([piece.reshape(-1) for piece in small])
    near_small = in_order(packed[None], over_c(packed)[None], 0)[None]
    step = 1
    while step < wide:
        moved = over_y(near_small, step)
        near_small = jnp.where(
            (y // step) % 2 == 0,
            jnp.concatenate([near_small, moved], axis=0),
            jnp.concatenate([moved, near_small], axis=0),
        )
        step *= 2
    layer_in = rotate(trade_z(inputs[:, 0, 0]).reshape(held, width)).astype(F32)
    near_small = turn(
        jnp.stack([near_small] + [over_z(near_small, k) for k in range(1, depth)]), 0
    ).reshape(heads_size, 2, -1)
    far_small = over_x(near_small)
    turned_small = jnp.stack([near_small, far_small])
    spread_small = jnp.where(x == 0, turned_small, jnp.stack([far_small, near_small]))
    starts = [0]
    for piece in small:
        starts.append(starts[-1] + piece.size)

    def piece(index, turned):
        source = turned_small if turned else spread_small
        return source[..., starts[index] : starts[index + 1]].reshape(
            (2, heads_size, 2) + small[index].shape
        )

    def pick_heads(value):
        value = value.reshape((depth, wide) + value.shape[1:])
        value = lax.dynamic_index_in_dim(value, y, 1, False)
        return lax.dynamic_slice_in_dim(value, c * near, near, 0)

    gain_one = piece(0, True).reshape(width).astype(F32)
    gain_two = piece(1, True).reshape(width).astype(F32)
    downs = [piece(i, True).reshape(width, rank) for i in (2, 3, 4)]
    downs_t = jnp.concatenate(downs + [jnp.zeros((width, LOWS - 3 * rank), BF16)], axis=1).T
    out_lift = jnp.moveaxis(piece(5, True), 3, 0).reshape(rank, width)
    query_raise = jnp.transpose(
        piece(6, False).reshape(2, heads_size, 2, -1, per, HD), (1, 4, 0, 2, 3, 5)
    ).reshape(heads_size, per, rank, HD)
    query_raise = jnp.moveaxis(pick_heads(query_raise), 2, 0).reshape(rank, -1)

    def pick_keys(value):
        value = value.reshape(value.shape[0], depth, kv_depth, HD)
        value = lax.dynamic_index_in_dim(value, kv_pick, 2, False)
        return lax.dynamic_slice_in_dim(value, c * near, near, 1).reshape(value.shape[0], -1)

    def pick_near(value):
        value = value.reshape(value.shape[0], depth, kv_depth, HD)
        value = lax.dynamic_index_in_dim(value, kv_pick, 2, False).reshape(value.shape[0], -1).T
        rows_near = near * HD
        kept = lax.dynamic_slice_in_dim(value, c * rows_near, rows_near, 0)
        return in_order(kept, over_c(lax.dynamic_slice_in_dim(value, (1 - c) * rows_near, rows_near, 0)), 1)

    key_raise = pick_keys(piece(7, False)[:, 0].reshape(rank, KV * HD))
    value_raise = pick_keys(piece(8, False)[:, 0].reshape(rank, KV * HD))
    out_down = jnp.transpose(
        piece(9, False).reshape(2, heads_size, 2, per, HD, -1), (1, 3, 4, 0, 2, 5)
    ).reshape(heads_size, per, HD, rank)
    out_down = pick_heads(out_down).reshape(-1, rank)
    maps = jnp.transpose(piece(10, False), (1, 3, 0, 2, 4, 5)).reshape(heads_size, per, HD, HD)
    maps = pick_heads(maps).reshape(-1, HD, HD)
    query_rows = near * block_rows
    key_rows = near * HD
    lift = jnp.concatenate(
        [
            jnp.pad(query_raise, ((0, 0), (0, 2 * key_rows))),
            jnp.pad(key_raise, ((0, 0), (query_rows, key_rows))),
            jnp.pad(value_raise, ((0, 0), (query_rows + key_rows, 0))),
            jnp.zeros((LOWS - 3 * rank, query_rows + 2 * key_rows), BF16),
        ],
        axis=0,
    )
    row_count = query_rows + 2 * key_rows

    def hidden_rows(place):
        parts = [gate_weight, up_weight, down_weight]
        size = down_weight.shape[0] // 2
        return jnp.stack(
            [lax.dynamic_slice_in_dim(p, place * size, size, 1).T for p in parts[:2]]
            + [lax.dynamic_slice_in_dim(parts[2], place * size, size, 0)]
        )

    kept_pack = hidden_rows(c)
    moved_pack = after(over_c(hidden_rows(1 - c)), far_small)
    ffn_own = [in_order(kept_pack, moved_pack, 2)]
    ffn_other = [over_x(ffn_own[0])]
    ring_pack = jnp.where(
        c != 1,
        jnp.concatenate([kept_pack, moved_pack], axis=2),
        jnp.concatenate([moved_pack, kept_pack], axis=2),
    )
    query_blocks = gather_z(after(query_weight.T, layer_in))
    out_blocks = gather_z(after(output_weight, query_blocks))
    ffn_own.append(over_z(after(ring_pack, out_blocks)))

    def join_heads(blocks):
        kept = lax.dynamic_slice_in_dim(blocks, c * near, near, 0)
        moved = over_c(lax.dynamic_slice_in_dim(blocks, (1 - c) * near, near, 0))
        return in_order(kept, moved, 2).reshape(near * block_rows, half)

    query_own = join_heads(query_blocks)
    kv_own = jnp.concatenate([pick_near(key_weight), pick_near(value_weight)], axis=0)
    both_own = jnp.concatenate([query_own, kv_own], axis=0)
    project_own = jnp.concatenate([both_own, downs_t[:, :half]], axis=0)
    project_other = jnp.concatenate([over_x(both_own), downs_t[:, half:]], axis=0)

    def next_block():
        ffn_own.append(over_z(ffn_own[-1]))

    def next_half():
        ffn_other.append(over_x(ffn_own[len(ffn_other)]))

    scale_one = rms(layer_in)
    normed = gather_tokens((layer_in * scale_one * gain_one).astype(BF16))
    normed = (jnp.concatenate(normed[:2], axis=0), jnp.concatenate(normed[2:], axis=0))

    def project_rows(tokens):
        flat = mm(project_own, tokens[:, :half], 1, 1) + mm(project_other, tokens[:, half:], 1, 1)
        low = flat[row_count:].astype(BF16)
        return (flat[:row_count] + mm(lift, low, 0, 0)).astype(BF16), low

    pieces = [project_rows(tokens) for tokens in normed]
    rows = jnp.concatenate([piece_rows for piece_rows, _ in pieces], axis=1)
    low_rows = jnp.concatenate([low for _, low in pieces], axis=1)

    def flips(value, y_axis, c_axis):
        value = jnp.where(c == 1, jnp.flip(value, c_axis), value)
        step = 1
        while step < wide:
            shape = value.shape
            apart = value.reshape(
                shape[:y_axis] + (wide // (2 * step), 2, step) + shape[y_axis + 1 :]
            )
            value = jnp.where((y // step) % 2 == 1, jnp.flip(apart, y_axis + 1), apart).reshape(shape)
            step *= 2
        return value

    length = wide * 2 * held
    chunks = length // CHUNK
    if share % CHUNK == 0:
        across = share // CHUNK
        numbers = jnp.arange(chunks, dtype=jnp.int32).reshape(2, depth, wide, across)
        order = flips(
            jnp.arange(chunks, dtype=jnp.int32).reshape(wide, 2, depth, across), 0, 1
        )
        order = jnp.transpose(order, (1, 2, 0, 3)).reshape(-1)

        def to_natural(value):
            return value

        from_natural = to_natural
    else:
        order = jnp.arange(chunks, dtype=jnp.int32)

        def to_natural(value):
            apart = flips(value.reshape(-1, wide, 2, depth, share), 1, 2)
            return jnp.transpose(apart, (0, 2, 3, 1, 4)).reshape(value.shape)

        def from_natural(value):
            apart = jnp.transpose(value.reshape(-1, 2, depth, wide, share), (0, 3, 1, 2, 4))
            return flips(apart, 1, 2).reshape(value.shape)

    segment = lax.dynamic_index_in_dim(segment_ids[:, 0], z, 0, False)
    last = segment.reshape(chunks, CHUNK)[:, -1]
    seg_row = segment[None, :]
    seg_col = segment[:, None]
    rows_nat = to_natural(rows)
    next_block()
    next_half()
    saved = attend_forward(
        last, order, seg_row, seg_col, rows_nat, jnp.transpose(maps, (0, 2, 1)),
        (ffn_own[1],),
    )
    mixed = from_natural(saved[0])

    out_own = join_heads(after(out_blocks, ffn_other[0]))
    out_mat = jnp.concatenate([out_own, over_x(out_own)], axis=1)
    rank_rows = mm(out_down, mixed, 0, 0).astype(BF16)
    split = 2 * held

    def branch(part, *waits):
        def make(*sent):
            rows_in = after(mixed[:, part], *waits) if waits else mixed[:, part]
            return (mm(rows_in, out_mat, 0, 0) + mm(rank_rows[:, part], out_lift, 0, 0)).astype(BF16)

        return make

    chip_part, other_part = slice(0, split), slice(split, length)
    last_own = [over_z(ffn_own[2][:2])]
    next_half()
    branch_sum, _, _ = reduce_tokens(
        branch(chip_part), branch(other_part, ffn_own[2], ffn_other[1])
    )
    middle = layer_in + branch_sum
    last_own.append(over_z(after(ffn_own[2][2:], last_own[0], branch_sum)))
    last_other = [over_x(part) for part in last_own]

    scale_two = rms(middle)
    ffn_rows = stack_rows(
        gather_tokens(
            after((middle * scale_two * gain_two).astype(BF16), ffn_other[2]), last_own[1]
        )
    )
    grad_out = trade_z(after(cotangent[:, 0, 0], last_own[0], branch_sum))
    grad_out = rotate(after(grad_out, middle).reshape(held, width))
    grads = stack_rows(gather_tokens(grad_out))
    last_other[0] = after(last_other[0], ffn_rows)
    own_gate, own_up, own_down = [
        jnp.concatenate([block[i] for block in ffn_own] + [last_own[i // 2][i % 2]], axis=0)
        for i in range(3)
    ]
    other_gate, other_up, other_down = [
        jnp.concatenate([block[i] for block in ffn_other] + [last_other[i // 2][i % 2]], axis=0)
        for i in range(3)
    ]
    chip_place = (0, split)
    other_place = (split, length - split)
    gates, ups, hidden = gate_forward(
        ffn_rows, own_gate, other_gate, own_up, other_up, (last_other[1],)
    )

    def ffn_forward(place):
        return lambda *sent: sum_products([hidden], [own_down], [other_down], *place)

    swap = x.reshape(1).astype(jnp.int32)

    def sum_x(value):
        return lax.psum_scatter(value, "rows", scatter_dimension=0, tiled=False)

    down_full = weight_grad_halves(hidden, grads, swap)
    down_sums = sum_x(down_full).reshape(depth, -1, half)
    ffn_out, ffn_sent, ffn_parts = reduce_tokens(ffn_forward(chip_place), ffn_forward(other_place))

    grad_gates, grad_ups = gate_backward(
        grads, own_down, other_down, gates, ups, (down_full, ffn_parts[0], *ffn_sent)
    )

    def ffn_back(place, wait):
        return lambda sent=(): sum_products(
            [grad_gates, grad_ups],
            [own_gate, own_up],
            [other_gate, other_up],
            *place,
            (*wait, *sent),
        )

    output = trade_z(rotate((middle + ffn_out).astype(BF16)).reshape(depth, share, width))
    gate_full = weight_grad_halves(grad_gates, ffn_rows, swap, tuple(ffn_parts[1:]))
    gate_sums = sum_x(gate_full).reshape(depth, -1, half)
    up_full = weight_grad_halves(grad_ups, ffn_rows, swap, (gate_full,))
    up_sums = sum_x(up_full).reshape(depth, -1, half)
    down_traded = trade_z(turn(down_sums, 0))
    grad_ffn, grad_ffn_sent, _ = reduce_tokens(
        ffn_back(chip_place, ()),
        ffn_back(other_place, ()),
        (gate_full, up_full, down_traded),
    )

    grad_mid_norm, gain_two_grad = norm_back(middle, gain_two, scale_two, grad_ffn)
    grad_middle = grad_out.astype(F32) + grad_mid_norm

    def halves(value):
        middle_at = value.shape[-1] // 2
        first, second = value[..., :middle_at], value[..., middle_at:]
        return jnp.where(x == 0, first, second), jnp.where(x == 0, second, first)

    grad_branch = stack_rows(gather_tokens(grad_middle.astype(BF16)))
    grad_olow = mm(out_lift, grad_branch, 1, 1).astype(BF16)
    grad_mixed = (mm(out_mat, grad_branch, 1, 1) + mm(out_down, grad_olow)).astype(BF16)
    gate_sums = after(gate_sums, grad_middle)
    up_sums = after(up_sums, grad_branch)
    gate_traded = trade_z(after(turn(gate_sums, 0), output))
    up_shifted = [over_z(up_sums[depth - k], k) for k in range(1, depth)]
    out_lift_grad = mm(rank_rows, grad_branch)
    out_down_grad = mm(mixed, grad_olow, 1, 1)
    out_grads = [mm(mixed, grad_branch[:, cut]) for cut in (slice(0, half), slice(half, width))]
    down_lift = halves(out_down_grad)
    out_halves = [
        jnp.concatenate([a, b], axis=1).astype(BF16) for a, b in zip(out_grads, down_lift)
    ]
    out_moved = over_x(out_halves[1])

    grad_rows, maps_grad = attend_backward(
        last, order, seg_row, seg_col, rows_nat, maps, lift, saved, to_natural(grad_mixed),
        (out_moved, output),
    )
    grad_rows = after(from_natural(grad_rows), gate_traded, up_shifted)

    quarter = half // 2
    rank_own = rank // 4
    maps_own = HD // 4

    def part_of(value, place):
        sizes = (quarter, rank_own, maps_own)
        start = 0
        parts = []
        for size in sizes:
            if start < value.shape[1]:
                parts.append(lax.dynamic_slice_in_dim(value, start + place * size, size, 1))
            start += 2 * size
        return jnp.concatenate(parts, axis=1).astype(BF16)

    def by_depth(value, height):
        return value.reshape(near, height, value.shape[-1])

    def collect(own_half, moved, blocks, *waits):
        summed = own_half.astype(F32) + moved.astype(F32)

        def ready(place):
            return blocks(part_of(summed, place))

        return shift_sum(in_order(ready(c), over_c(ready(1 - c)), 0), *waits)

    def project_back(part):
        def make(*sent):
            return jnp.concatenate(
                [mm(grad_rows[:, part], weight, 0, 0).astype(BF16) for weight in (project_own, project_other)],
                axis=1,
            )

        return make

    grad_normed, normed_sent, _ = reduce_tokens(
        project_back(chip_part), project_back(other_part)
    )
    grad_in_norm, gain_one_grad = norm_back(layer_in, gain_one, scale_one, grad_normed)
    grad_in = rotate((grad_middle + grad_in_norm).astype(BF16)).reshape(depth, share, width)
    input_grad = trade_z(grad_in)

    late_rows = after(grad_rows, *normed_sent)
    project_grad = [
        mm(late_rows[:, chip_part], normed[0][:, cut]) + mm(late_rows[:, other_part], normed[1][:, cut])
        for cut in (slice(0, half), slice(half, width))
    ]
    lift_grad = mm(low_rows, late_rows[:row_count], 1, 1)[: 3 * rank].reshape(3, rank, row_count)
    column = lax.broadcasted_iota(jnp.int32, (3, 1, row_count), 2)
    owner_of = (column >= query_rows).astype(jnp.int32) + (column >= query_rows + key_rows)
    kind = lax.broadcasted_iota(jnp.int32, (3, 1, row_count), 0)
    lift_grad = jnp.sum(jnp.where(owner_of == kind, lift_grad, 0.0), axis=0).T

    out_sum = collect(
        out_halves[0],
        after(out_moved, *normed_sent),
        lambda value: by_depth(value, block_rows),
        grad_in,
    )

    out_grad = out_sum[:, :quarter]
    output_down_grad = out_sum[:, quarter : quarter + rank_own]

    lift_halves = halves(lift_grad)
    maps_halves = halves(
        jnp.concatenate(
            [maps_grad.reshape(query_rows, HD), jnp.zeros((2 * key_rows, HD), F32)], axis=0
        )
    )
    late_halves = [
        jnp.concatenate(
            [project_grad[i][:row_count], lift_halves[i], maps_halves[i]], axis=1
        ).astype(BF16)
        for i in range(2)
    ]
    late_sum = collect(
        late_halves[0],
        after(over_x(late_halves[1]), grad_in),
        lambda value: jnp.concatenate(
            [
                by_depth(value[:query_rows], block_rows),
                by_depth(value[query_rows : query_rows + key_rows], HD),
                by_depth(value[query_rows + key_rows :], HD),
            ],
            axis=1,
        ),
    )
    query_grad = late_sum[:block_rows, :quarter].T
    query_lift_grad = late_sum[:block_rows, quarter : quarter + rank_own].T
    feature_maps_grad = jnp.transpose(
        late_sum[:block_rows, quarter + rank_own :].reshape(per, HD, maps_own), (0, 2, 1)
    )
    kv_sum = late_sum[block_rows:, : quarter + rank_own].reshape(2, HD, quarter + rank_own)
    kv_sum = jnp.where(
        lax.broadcasted_iota(jnp.int32, (kv_depth, 1, 1, 1), 0) == kv_pick, kv_sum[None], 0.0
    ).astype(BF16)
    step = 1
    while step < wide:
        kv_sum = (kv_sum.astype(F32) + over_y(kv_sum, step).astype(F32)).astype(BF16)
        step *= 2
    kv_sum = gather_z(after(kv_sum, input_grad))
    kv_sum = jnp.transpose(kv_sum, (2, 4, 0, 1, 3)).reshape(2, quarter + rank_own, KV * HD)
    kv_sum = kv_sum.astype(F32)

    down_total = jnp.sum(after(down_traded, grad_in).astype(F32), axis=0)
    gate_total = jnp.sum(after(gate_traded, grad_in).astype(F32), axis=0)
    up_total = up_sums[0].astype(F32)
    for block in after(up_shifted, grad_in):
        up_total = up_total + block.astype(F32)

    def to_owner(total):
        total = total.astype(BF16)
        kept = lax.dynamic_slice_in_dim(total, c * quarter, quarter, 1)
        return in_order(kept, over_c(lax.dynamic_slice_in_dim(total, (1 - c) * quarter, quarter, 1)), 0)

    down_grad = to_owner(down_total).astype(F32)
    gate_grad = to_owner(gate_total).T.astype(F32)
    up_grad = to_owner(up_total).T.astype(F32)

    minor = jnp.concatenate(
        [
            gain_one_grad[None],
            gain_two_grad[None],
            jnp.concatenate([part[row_count : row_count + 3 * rank] for part in project_grad], axis=1),
            out_lift_grad,
        ],
        axis=0,
    )
    minor = minor[:, :half] + over_x(after(minor[:, half:], late_sum))
    minor = jnp.moveaxis(minor.reshape(-1, depth, wide, 2, half // (2 * heads_size)), 0, 3)
    minor = shift_sum(minor)
    total = lax.dynamic_index_in_dim(minor, y, 0, False)
    for k in range(1, wide):
        total = total + over_y(lax.dynamic_index_in_dim(minor, y ^ k, 0, False), k)
    minor = lax.dynamic_index_in_dim(total, c, 0, False) + over_c(
        lax.dynamic_index_in_dim(total, 1 - c, 0, False)
    )
    minor = minor.T
    return (
        output[:, None, None],
        input_grad[:, None, None].astype(F32),
        minor[:, 0],
        minor[:, 1],
        query_grad,
        kv_sum[0, :quarter],
        kv_sum[1, :quarter],
        out_grad,
        minor[:, 2 : 2 + rank],
        query_lift_grad,
        minor[:, 2 + rank : 2 + 2 * rank],
        kv_sum[0, quarter:],
        minor[:, 2 + 2 * rank : 2 + 3 * rank],
        kv_sum[1, quarter:],
        output_down_grad,
        minor[:, 2 + 3 * rank :].T,
        feature_maps_grad,
        gate_grad,
        up_grad,
        down_grad,
    )


def solution(mesh):
    placed = (
        P(None, "rows", "seq", "heads", None),
        P(None, "rows", None),
        P(None, "rows", "seq", "heads", None),
        P(("rows", "heads", "seq")),
        P(("rows", "heads", "seq")),
        P(("rows", "seq"), "heads"),
        P(("rows", "seq"), None),
        P(("rows", "seq"), None),
        P("heads", ("rows", "seq")),
        P(("rows", "heads", "seq"), None),
        P(("rows", "seq"), "heads"),
        P(("rows", "heads", "seq"), None),
        P(("rows", "seq"), None),
        P(("rows", "heads", "seq"), None),
        P(("rows", "seq"), None),
        P("heads", ("rows", "seq")),
        P(None, ("rows", "heads", "seq")),
        P("heads", ("rows", "seq"), None),
        P(("rows", "seq"), "heads"),
        P(("rows", "seq"), "heads"),
        P("heads", ("rows", "seq")),
    )
    return jax.shard_map(
        body,
        mesh=mesh,
        in_specs=placed,
        out_specs=(
            P(None, "rows", "seq", "heads", None),
            P(None, "rows", "seq", "heads", None),
            P(("rows", "heads", "seq")),
            P(("rows", "heads", "seq")),
            P(("rows", "seq"), "heads"),
            P(("rows", "seq"), None),
            P(("rows", "seq"), None),
            P("heads", ("rows", "seq")),
            P(("rows", "heads", "seq"), None),
            P(("rows", "seq"), "heads"),
            P(("rows", "heads", "seq"), None),
            P(("rows", "seq"), None),
            P(("rows", "heads", "seq"), None),
            P(("rows", "seq"), None),
            P("heads", ("rows", "seq")),
            P(None, ("rows", "heads", "seq")),
            P("heads", ("rows", "seq"), None),
            P(("rows", "seq"), "heads"),
            P(("rows", "seq"), "heads"),
            P("heads", ("rows", "seq")),
        ),
        check_vma=False,
    )
```

```python
import math

import jax
import jax.numpy as jnp
from jax import lax
from jax.experimental import pallas as pl
from jax.experimental.pallas import tpu as pltpu
from jax.sharding import PartitionSpec as P

HEADS = 32
KV = 8
HD = 64
WINDOW = 64
CHUNK = 2 * WINDOW
FEATS = 2 * HD
AUG = HD + 16
F32 = jnp.float32
PART = 512
BF16 = jnp.bfloat16


def mm(left, right, left_dim=1, right_dim=0):
    return lax.dot_general(
        left, right, (((left_dim,), (right_dim,)), ((), ())), preferred_element_type=F32
    )


def chunk_masks(chunk, seg_row, seg_own, seg_prev):
    place = lax.broadcasted_iota(jnp.int32, (CHUNK, CHUNK), 1)
    key = lax.broadcasted_iota(jnp.int32, (CHUNK, CHUNK), 0)
    same_own = seg_own == seg_row
    same_prev = (seg_prev - jnp.where(chunk == 0, 100, 0)) == seg_row
    far = -1e30
    bias_own = jnp.where(same_own & (key <= place) & (key > place - WINDOW), 0.0, far)
    bias_prev = jnp.where(same_prev & (key > place + WINDOW), 0.0, far)
    linear_prev = jnp.where(same_prev & (key <= place + WINDOW), 1.0, 0.0)
    linear_own = jnp.where(same_own & (key <= place - WINDOW), 1.0, 0.0)
    return bias_prev[WINDOW:], bias_own, linear_prev, linear_own[:WINDOW]


def turned(values):
    return jnp.transpose(values.astype(F32)).astype(BF16)


def with_ones(values):
    return jnp.concatenate([values, jnp.ones((AUG - HD, CHUNK), values.dtype)], axis=0)


def features_of(vectors, maps_t):
    logits = mm(maps_t, vectors)
    high = jnp.exp(logits - jnp.max(logits, axis=0, keepdims=True))
    low = jnp.exp(jnp.min(logits, axis=0, keepdims=True) - logits)
    high = high * (1.0 / jnp.sum(high, axis=0, keepdims=True))
    low = low * (1.0 / jnp.sum(low, axis=0, keepdims=True))
    return jnp.concatenate([high, low], axis=0)


def features_back(features, grad):
    product = features * grad
    high = product[:HD] - features[:HD] * jnp.sum(product[:HD], axis=0, keepdims=True)
    low = product[HD:] - features[HD:] * jnp.sum(product[HD:], axis=0, keepdims=True)
    return high - low


def forward_kernel(
    last_ref, order_ref, seg_row_ref, seg_own_ref, seg_prev_ref,
    q_ref, kt_ref, ktp_ref, vt_ref, vtp_ref, maps_t_ref,
    mixed_ref, peak_ref, den_ref, fq_ref, fkt_ref, fk_ref, state_out_ref,
    state_ref, fk_prev_ref,
):
    chunk = pl.program_id(0)
    head_count = fq_ref.shape[0]
    per_key = head_count * HD // kt_ref.shape[0]

    @pl.when(chunk == 0)
    def _():
        state_ref[...] = jnp.zeros_like(state_ref)
        fk_prev_ref[...] = jnp.zeros_like(fk_prev_ref)

    seg_row = seg_row_ref[...]
    bias_prev, bias_own, linear_prev, linear_own = chunk_masks(
        chunk, seg_row, seg_own_ref[...], seg_prev_ref[...]
    )
    tag_state = jnp.where(chunk >= 2, last_ref[jnp.maximum(chunk - 2, 0)], -1)
    tag_prev = jnp.where(chunk >= 1, last_ref[jnp.maximum(chunk - 1, 0)], -2)
    carried = jnp.where(seg_row == tag_state, 1.0, 0.0)
    joined = jnp.where(tag_state == tag_prev, 1.0, 0.0)
    keep_prev = jnp.where(seg_prev_ref[...] == tag_prev, 1.0, 0.0).astype(BF16)
    k_own = turned(kt_ref[...])
    k_prev = turned(ktp_ref[...])
    for head in range(head_count):
        group = head // per_key
        rows = slice(head * HD, (head + 1) * HD)
        key_rows = slice(group * HD, (group + 1) * HD)
        query = q_ref[rows, :]
        maps_t = maps_t_ref[head]
        feat_q = features_of(query, maps_t)
        feat_kt = features_of(kt_ref[key_rows, :], maps_t)
        fq_ref[head] = feat_q.astype(BF16)
        fkt_ref[head] = feat_kt.astype(BF16)
        feat_k = jnp.transpose(feat_kt).astype(BF16)
        fk_ref[head] = feat_k
        scaled = query * jnp.asarray(HD**-0.5, BF16)
        score_prev = mm(k_prev[WINDOW:, key_rows], scaled) + bias_prev
        score_own = mm(k_own[:, key_rows], scaled) + bias_own
        peak = jnp.maximum(
            jnp.max(score_prev, axis=0, keepdims=True), jnp.max(score_own, axis=0, keepdims=True)
        )
        weight_prev = jnp.exp(score_prev - peak)
        weight_own = jnp.exp(score_own - peak)
        damped = feat_q * jnp.exp(-peak)
        damped_low = damped.astype(BF16)
        fk_prev = fk_prev_ref[head]
        lin_prev = mm(fk_prev, damped_low) * linear_prev
        lin_own = mm(feat_k[:WINDOW], damped_low) * linear_own
        all_prev = jnp.concatenate([lin_prev[:WINDOW], lin_prev[WINDOW:] + weight_prev], axis=0)
        all_own = jnp.concatenate([lin_own + weight_own[:WINDOW], weight_own[WINDOW:]], axis=0)
        value_prev = with_ones(vtp_ref[key_rows, :])
        state = state_ref[head]
        state_low = state.astype(BF16)
        state_out_ref[0, head] = state_low
        total = (
            mm(value_prev, all_prev.astype(BF16))
            + mm(with_ones(vt_ref[key_rows, :]), all_own.astype(BF16))
            + mm(state_low, (damped * carried).astype(BF16))
        )
        den = total[HD : HD + 1]
        mixed_ref[rows, :] = (total[:HD] * (1.0 / den)).astype(BF16)
        peak_ref[head : head + 1, :] = peak
        den_ref[head : head + 1, :] = den
        state_ref[head] = state * joined + mm(value_prev, fk_prev * keep_prev)
        fk_prev_ref[head] = feat_k


def backward_kernel(
    last_ref, order_ref, seg_row_ref, seg_own_ref, seg_prev_ref,
    q_ref, kt_ref, ktp_ref, vt_ref, vtp_ref, maps_ref, lift_ref,
    mixed_ref, grad_ref, peak_ref, den_ref, fq_ref, fkt_ref, fktp_ref, fk_ref, fkp_ref, state_ref,
    grows_ref, gmaps_ref,
    gstate_ref, cphi_ref, ck_ref, cv_ref,
):
    step = pl.program_id(0)
    chunk = pl.num_programs(0) - 1 - step
    head_count = fq_ref.shape[0]
    group_count = kt_ref.shape[0] // HD
    per_key = head_count // group_count

    @pl.when(step == 0)
    def _():
        gstate_ref[...] = jnp.zeros_like(gstate_ref)
        cphi_ref[...] = jnp.zeros_like(cphi_ref)
        ck_ref[...] = jnp.zeros_like(ck_ref)
        cv_ref[...] = jnp.zeros_like(cv_ref)
        gmaps_ref[...] = jnp.zeros_like(gmaps_ref)

    seg_row = seg_row_ref[...]
    bias_prev, bias_own, linear_prev, linear_own = chunk_masks(
        chunk, seg_row, seg_own_ref[...], seg_prev_ref[...]
    )
    tag_state = jnp.where(chunk >= 2, last_ref[jnp.maximum(chunk - 2, 0)], -1)
    tag_prev = jnp.where(chunk >= 1, last_ref[jnp.maximum(chunk - 1, 0)], -2)
    carried = jnp.where(seg_row == tag_state, 1.0, 0.0)
    joined = jnp.where(tag_state == tag_prev, 1.0, 0.0)
    keep_col = jnp.where(seg_prev_ref[...] == tag_prev, 1.0, 0.0)
    keep_prev = jnp.transpose(jnp.broadcast_to(keep_col, (CHUNK, CHUNK)))[:1]
    scale = HD**-0.5
    none = jnp.zeros((WINDOW, CHUNK), F32)
    k_own = turned(kt_ref[...])
    k_prev = turned(ktp_ref[...])
    v_own = turned(vt_ref[...])
    v_prev = turned(vtp_ref[...])
    for group in range(group_count):
        key_rows = slice(group * HD, (group + 1) * HD)
        key_t = kt_ref[key_rows, :]
        value_prev = with_ones(vtp_ref[key_rows, :])
        own_k = ck_ref[group]
        own_v = cv_ref[group]
        next_k = None
        next_v = None
        for head in range(group * per_key, (group + 1) * per_key):
            rows = slice(head * HD, (head + 1) * HD)
            query = q_ref[rows, :]
            scaled = query * jnp.asarray(scale, BF16)
            peak = peak_ref[head : head + 1, :]
            den = den_ref[head : head + 1, :]
            weight_prev = jnp.exp(mm(k_prev[WINDOW:, key_rows], scaled) + bias_prev - peak)
            weight_own = jnp.exp(mm(k_own[:, key_rows], scaled) + bias_own - peak)
            damp = jnp.exp(-peak)
            feat_q = fq_ref[head].astype(F32)
            damped = feat_q * damp
            damped_low = damped.astype(BF16)
            carried_low = (damped * carried).astype(BF16)
            lin_prev = mm(fkp_ref[head], damped_low) * linear_prev
            lin_own = mm(fk_ref[head, :WINDOW, :], damped_low) * linear_own
            all_prev = jnp.concatenate([lin_prev[:WINDOW], lin_prev[WINDOW:] + weight_prev], axis=0)
            all_own = jnp.concatenate([lin_own + weight_own[:WINDOW], weight_own[WINDOW:]], axis=0)
            grad = grad_ref[rows, :].astype(F32)
            dnum = grad * (1.0 / den)
            dden = -jnp.sum(dnum * mixed_ref[rows, :].astype(F32), axis=0, keepdims=True)
            dnum_low = dnum.astype(BF16)
            dtotal = jnp.concatenate(
                [dnum, dden, jnp.zeros((AUG - HD - 1, CHUNK), F32)], axis=0
            ).astype(BF16)
            dall_prev = mm(v_prev[:, key_rows], dnum_low) + dden
            dall_own = mm(v_own[:, key_rows], dnum_low) + dden
            dscore_prev = jnp.concatenate([none, weight_prev * dall_prev[WINDOW:]], axis=0).astype(BF16)
            dscore_own = (weight_own * dall_own).astype(BF16)
            dlin_prev = (linear_prev * dall_prev).astype(BF16)
            dlin_own = jnp.concatenate([linear_own * dall_own[:WINDOW], none], axis=0).astype(BF16)
            gstate = gstate_ref[head]
            gstate_low = gstate.astype(BF16)
            ddamped = (
                mm(fktp_ref[head], dlin_prev)
                + mm(fkt_ref[head], dlin_own)
                + carried * mm(state_ref[0, head], dtotal, 0, 0)
            )
            dlogit_q = features_back(feat_q, ddamped * damp).astype(BF16)
            maps = maps_ref[head]
            grad_q = (
                mm(ktp_ref[key_rows, :], dscore_prev) + mm(key_t, dscore_own)
            ) * scale + mm(maps, dlogit_q)
            grows_ref[rows, :] = grad_q.astype(BF16)
            dphi_own = cphi_ref[head] + mm(damped_low, dlin_own, 1, 1)
            cphi_ref[head] = (
                mm(damped_low, dlin_prev, 1, 1) + mm(gstate_low, value_prev, 0, 0) * keep_prev
            )
            dlogit_k = features_back(fkt_ref[head].astype(F32), dphi_own).astype(BF16)
            gmaps_ref[head] += mm(dlogit_q, query, 1, 1) + mm(dlogit_k, key_t, 1, 1)
            own_k += mm(scaled, dscore_own, 1, 1) + mm(maps, dlogit_k)
            part_k = mm(scaled, dscore_prev, 1, 1)
            own_v += mm(dnum_low, all_own.astype(BF16), 1, 1)
            part_v = (
                mm(dnum_low, all_prev.astype(BF16), 1, 1)
                + mm(gstate_low[:HD], fktp_ref[head]) * keep_prev
            )
            next_k = part_k if next_k is None else next_k + part_k
            next_v = part_v if next_v is None else next_v + part_v
            gstate_ref[head] = gstate * joined + mm(dtotal, carried_low, 1, 1)
        key_start = (head_count + group) * HD
        value_start = (head_count + group_count + group) * HD
        grows_ref[key_start : key_start + HD, :] = own_k.astype(BF16)
        grows_ref[value_start : value_start + HD, :] = own_v.astype(BF16)
        ck_ref[group] = next_k
        cv_ref[group] = next_v
    width = lift_ref.shape[1]
    grows_ref[width:, :] = mm(lift_ref[...], grows_ref[:width, :]).astype(BF16)


def attend_forward(last, order, seg_row, seg_col, rows, maps_t, waits=()):
    heads = maps_t.shape[0]
    groups, length = (rows.shape[0] // HD - heads) // 2, rows.shape[1]
    chunks = length // CHUNK
    first = heads // groups

    def before(c):
        return jnp.maximum(c - 1, 0)

    def spec(count, block, shift):
        return pl.BlockSpec((count * HD, CHUNK), lambda c, last, order: (block, order[shift(c)]))

    def here(c):
        return c

    stat = pl.BlockSpec((heads, CHUNK), lambda c, last, order: (0, c))
    feat_t = pl.BlockSpec((heads, FEATS, CHUNK), lambda c, last, order: (0, 0, c))
    return pl.pallas_call(
        ignoring(forward_kernel, 11, len(waits)),
        grid_spec=pltpu.PrefetchScalarGridSpec(
            num_scalar_prefetch=2,
            grid=(chunks,),
            in_specs=[
                pl.BlockSpec((1, CHUNK), lambda c, last, order: (0, c)),
                pl.BlockSpec((CHUNK, 1), lambda c, last, order: (c, 0)),
                pl.BlockSpec((CHUNK, 1), lambda c, last, order: (before(c), 0)),
                spec(heads, 0, here),
                spec(groups, first, here),
                spec(groups, first, before),
                spec(groups, first + 1, here),
                spec(groups, first + 1, before),
                pl.BlockSpec((heads, HD, HD), lambda c, last, order: (0, 0, 0)),
            ]
            + [pl.BlockSpec(memory_space=pl.ANY)] * len(waits),
            out_specs=[
                spec(heads, 0, here), stat, stat,
                feat_t, feat_t,
                pl.BlockSpec((heads, CHUNK, FEATS), lambda c, last, order: (0, c, 0)),
                pl.BlockSpec((1, heads, AUG, FEATS), lambda c, last, order: (c, 0, 0, 0)),
            ],
            scratch_shapes=[
                pltpu.VMEM((heads, AUG, FEATS), F32),
                pltpu.VMEM((heads, CHUNK, FEATS), BF16),
            ],
        ),
        out_shape=[
            jax.ShapeDtypeStruct((heads * HD, length), BF16),
            jax.ShapeDtypeStruct((heads, length), F32),
            jax.ShapeDtypeStruct((heads, length), F32),
            jax.ShapeDtypeStruct((heads, FEATS, length), BF16),
            jax.ShapeDtypeStruct((heads, FEATS, length), BF16),
            jax.ShapeDtypeStruct((heads, length, FEATS), BF16),
            jax.ShapeDtypeStruct((chunks, heads, AUG, FEATS), BF16),
        ],
        compiler_params=pltpu.CompilerParams(
            dimension_semantics=("arbitrary",), vmem_limit_bytes=32 * 2**20
        ),
        cost_estimate=pl.CostEstimate(
            flops=heads * length * 1060000, bytes_accessed=heads * length * 400, transcendentals=0
        ),
        name="attend_forward",
    )(
        last, order, seg_row, seg_col, seg_col, rows, rows, rows, rows, rows, maps_t, *waits
    )


def attend_backward(
    last, order, seg_row, seg_col, rows, maps, lift, saved, grad, waits=()
):
    mixed, peak, den, fq, fkt, fk, states = saved
    heads = maps.shape[0]
    groups, length = (rows.shape[0] // HD - heads) // 2, rows.shape[1]
    chunks = length // CHUNK
    first = heads // groups
    height = lift.shape[0] + lift.shape[1]

    def here(s):
        return chunks - 1 - s

    def before(s):
        return jnp.maximum(chunks - 2 - s, 0)

    def spec(count, block, shift):
        return pl.BlockSpec((count * HD, CHUNK), lambda s, last, order: (block, order[shift(s)]))

    def feat_t(shift):
        return pl.BlockSpec((heads, FEATS, CHUNK), lambda s, last, order: (0, 0, shift(s)))

    def feat(shift):
        return pl.BlockSpec((heads, CHUNK, FEATS), lambda s, last, order: (0, shift(s), 0))

    stat = pl.BlockSpec((heads, CHUNK), lambda s, last, order: (0, here(s)))
    whole = pl.BlockSpec((heads, HD, HD), lambda s, last, order: (0, 0, 0))
    return pl.pallas_call(
        ignoring(backward_kernel, 22, len(waits)),
        grid_spec=pltpu.PrefetchScalarGridSpec(
            num_scalar_prefetch=2,
            grid=(chunks,),
            in_specs=[
                pl.BlockSpec((1, CHUNK), lambda s, last, order: (0, here(s))),
                pl.BlockSpec((CHUNK, 1), lambda s, last, order: (here(s), 0)),
                pl.BlockSpec((CHUNK, 1), lambda s, last, order: (before(s), 0)),
                spec(heads, 0, here),
                spec(groups, first, here), spec(groups, first, before),
                spec(groups, first + 1, here), spec(groups, first + 1, before),
                whole,
                pl.BlockSpec(lift.shape, lambda s, last, order: (0, 0)),
                spec(heads, 0, here), spec(heads, 0, here), stat, stat,
                feat_t(here), feat_t(here), feat_t(before), feat(here), feat(before),
                pl.BlockSpec((1, heads, AUG, FEATS), lambda s, last, order: (here(s), 0, 0, 0)),
            ]
            + [pl.BlockSpec(memory_space=pl.ANY)] * len(waits),
            out_specs=[
                pl.BlockSpec((height, CHUNK), lambda s, last, order: (0, order[here(s)])),
                whole,
            ],
            scratch_shapes=[
                pltpu.VMEM((heads, AUG, FEATS), F32),
                pltpu.VMEM((heads, FEATS, CHUNK), F32),
                pltpu.VMEM((groups, HD, CHUNK), F32),
                pltpu.VMEM((groups, HD, CHUNK), F32),
            ],
        ),
        out_shape=[
            jax.ShapeDtypeStruct((height, length), BF16),
            jax.ShapeDtypeStruct((heads, HD, HD), F32),
        ],
        compiler_params=pltpu.CompilerParams(
            dimension_semantics=("arbitrary",), vmem_limit_bytes=32 * 2**20
        ),
        cost_estimate=pl.CostEstimate(
            flops=heads * length * 2100000, bytes_accessed=heads * length * 600, transcendentals=0
        ),
        name="attend_backward",
    )(
        last, order, seg_row, seg_col, seg_col, rows, rows, rows, rows, rows, maps, lift, mixed, grad, peak, den, fq, fkt, fkt, fk, fk, states, *waits,
    )


def ignoring(kernel, inputs, waits):
    def body(*refs):
        kernel(*refs[:inputs], *refs[inputs + waits :])

    return body


def after(value, *others):
    values = jax.tree.leaves(value)
    tokens = jax.tree.leaves(others)
    anywhere = pl.BlockSpec(memory_space=pl.ANY)
    out = pl.pallas_call(
        lambda *refs: None,
        in_specs=[anywhere] * (len(values) + len(tokens)),
        out_specs=[anywhere] * len(values),
        out_shape=[jax.ShapeDtypeStruct(v.shape, v.dtype) for v in values],
        input_output_aliases={i: i for i in range(len(values))},
        cost_estimate=pl.CostEstimate(flops=0, bytes_accessed=0, transcendentals=0),
        name="after",
    )(*values, *tokens)
    return jax.tree.unflatten(jax.tree.structure(value), out)


def stack_rows(pieces):
    rows, columns = pieces[0].shape
    tall = min(256, rows)
    steps = rows // tall
    count = len(pieces)

    def kernel(*refs):
        for place in range(count):

            @pl.when(pl.program_id(0) == place)
            def _(place=place):
                refs[-1][...] = refs[place][...]

    def spec(place):
        def at(i, j):
            return (jnp.where(i < place, 0, jnp.where(i > place, steps - 1, j)), 0)

        return pl.BlockSpec((tall, columns), at)

    return pl.pallas_call(
        kernel,
        grid=(count, steps),
        in_specs=[spec(place) for place in range(count)],
        out_specs=pl.BlockSpec((tall, columns), lambda i, j: (i * steps + j, 0)),
        out_shape=jax.ShapeDtypeStruct((count * rows, columns), pieces[0].dtype),
        cost_estimate=pl.CostEstimate(
            flops=0, bytes_accessed=count * rows * columns, transcendentals=0
        ),
        name="stack_rows",
    )(*pieces)


def weight_grad_kernel(left_ref, right_ref, out_ref):
    out_ref[...] = mm(left_ref[...], right_ref[...], 0, 0).astype(BF16)


def weight_grad(left, right, part, waits=()):
    tokens, rows = left.shape
    half = right.shape[1] // 2
    tall = min(512, rows)
    return dense_call(
        weight_grad_kernel,
        (rows // tall,),
        [
            pl.BlockSpec((tokens, tall), lambda i: (0, i)),
            pl.BlockSpec((tokens, half), lambda i: (0, part)),
        ],
        pl.BlockSpec((tall, half), lambda i: (i, 0)),
        jax.ShapeDtypeStruct((rows, half), BF16),
        2 * tokens * rows * half,
        "weight_grad",
        waits,
    )(left, right, *waits)


def weight_grad_halves(left, right, swap, waits=()):
    tokens, rows = left.shape
    half = right.shape[1] // 2
    tall = min(512, rows)

    def kernel(swap_ref, left_ref, right_ref, *refs):
        refs[-1][0] = mm(left_ref[...], right_ref[...], 0, 0).astype(BF16)

    return pl.pallas_call(
        kernel,
        grid_spec=pltpu.PrefetchScalarGridSpec(
            num_scalar_prefetch=1,
            grid=(2, rows // tall),
            in_specs=[
                pl.BlockSpec((tokens, tall), lambda p, i, swap: (0, i)),
                pl.BlockSpec((tokens, half), lambda p, i, swap: (0, p + swap[0] - 2 * p * swap[0])),
            ]
            + [pl.BlockSpec(memory_space=pl.ANY)] * len(waits),
            out_specs=pl.BlockSpec((1, tall, half), lambda p, i, swap: (p, i, 0)),
        ),
        out_shape=jax.ShapeDtypeStruct((2, rows, half), BF16),
        compiler_params=pltpu.CompilerParams(
            dimension_semantics=("arbitrary", "arbitrary"), vmem_limit_bytes=48 * 2**20
        ),
        cost_estimate=pl.CostEstimate(
            flops=tokens * rows * half, bytes_accessed=rows * half, transcendentals=0
        ),
        name="weight_grad_halves",
    )(swap, left, right, *waits)


def dense_call(kernel, grid, in_specs, out_specs, out_shape, flops, name, waits=()):
    in_specs = in_specs + [pl.BlockSpec(memory_space=pl.ANY)] * len(waits)
    return pl.pallas_call(
        ignoring(kernel, len(in_specs) - len(waits), len(waits)),
        grid=grid,
        in_specs=in_specs,
        out_specs=out_specs,
        out_shape=out_shape,
        compiler_params=pltpu.CompilerParams(
            dimension_semantics=("arbitrary",) * len(grid), vmem_limit_bytes=48 * 2**20
        ),
        cost_estimate=pl.CostEstimate(
            flops=flops // 3, bytes_accessed=flops // 8000, transcendentals=0
        ),
        name=name,
    )


def sigmoid_of(values):
    return 0.5 * jnp.tanh(0.5 * values) + 0.5


def row_parts(count):
    size = min(PART, count)
    return [slice(at, at + size) for at in range(0, count, size)]


def gate_kernel(rows_ref, own_gate, other_gate, own_up, other_up, gate_ref, up_ref, hidden_ref):
    half = own_gate.shape[1]
    for part in row_parts(rows_ref.shape[0]):
        left = rows_ref[part, :half]
        right = rows_ref[part, half:]
        gate = mm(left, own_gate[...], 1, 1) + mm(right, other_gate[...], 1, 1)
        up = mm(left, own_up[...], 1, 1) + mm(right, other_up[...], 1, 1)
        gate_ref[part, :] = gate.astype(BF16)
        up_ref[part, :] = up.astype(BF16)
        hidden_ref[part, :] = (gate * sigmoid_of(gate) * up).astype(BF16)


def gate_back_kernel(grad_ref, own_down, other_down, gate_ref, up_ref, dgate_ref, dup_ref):
    half = own_down.shape[1]
    for part in row_parts(grad_ref.shape[0]):
        grad = mm(grad_ref[part, :half], own_down[...], 1, 1) + mm(
            grad_ref[part, half:], other_down[...], 1, 1
        )
        gate = gate_ref[part, :].astype(F32)
        sigmoid = sigmoid_of(gate)
        grad_swish = grad * sigmoid
        dup_ref[part, :] = (grad_swish * gate).astype(BF16)
        dgate_ref[part, :] = (
            grad_swish * up_ref[part, :].astype(F32) * (1.0 + gate * (1.0 - sigmoid))
        ).astype(BF16)


def sum_kernel(count, lefts_and_weights, out_ref):
    lefts = lefts_and_weights[:count]
    owns = lefts_and_weights[count : 2 * count]
    others = lefts_and_weights[2 * count :]
    column = pl.program_id(0)

    def write(weights):
        total = mm(lefts[0][...], weights[0][...])
        for left, weight in zip(lefts[1:], weights[1:]):
            total = total + mm(left[...], weight[...])
        out_ref[...] = total.astype(BF16)

    across = pl.num_programs(0) // 2

    @pl.when(column < across)
    def _():
        write(owns)

    @pl.when(column >= across)
    def _():
        write(others)


def gate_forward(rows, own_gate, other_gate, own_up, other_up, waits=()):
    tokens, width = rows.shape
    hidden, half = own_gate.shape
    tall, wide = min(512, tokens), min(1024, hidden)
    weight = pl.BlockSpec((wide, half), lambda j, i: (j, 0))
    out = pl.BlockSpec((tall, wide), lambda j, i: (i, j))
    return dense_call(
        gate_kernel,
        (hidden // wide, tokens // tall),
        [pl.BlockSpec((tall, width), lambda j, i: (i, 0))] + [weight] * 4,
        [out] * 3,
        [jax.ShapeDtypeStruct((tokens, hidden), BF16)] * 3,
        4 * tokens * width * hidden,
        "gate_forward",
        waits,
    )(rows, own_gate, other_gate, own_up, other_up, *waits)


def gate_backward(grad, own_down, other_down, gate, up, waits=()):
    tokens, width = grad.shape
    hidden, half = own_down.shape
    tall, wide = min(512, tokens), min(1024, hidden)
    weight = pl.BlockSpec((wide, half), lambda j, i: (j, 0))
    out = pl.BlockSpec((tall, wide), lambda j, i: (i, j))
    return dense_call(
        gate_back_kernel,
        (hidden // wide, tokens // tall),
        [pl.BlockSpec((tall, width), lambda j, i: (i, 0)), weight, weight, out, out],
        [out] * 2,
        [jax.ShapeDtypeStruct((tokens, hidden), BF16)] * 2,
        2 * tokens * width * hidden,
        "gate_backward",
        waits,
    )(grad, own_down, other_down, gate, up, *waits)


def sum_products(lefts, owns, others, start, tokens, waits=()):
    count = len(lefts)
    depth = lefts[0].shape[1]
    half = owns[0].shape[1]
    tall, wide = math.gcd(math.gcd(start, tokens), 1024), min(512, half)
    across = half // wide
    first = start // tall

    def kernel(*refs):
        sum_kernel(count, refs[:-1], refs[-1])

    left = pl.BlockSpec((tall, depth), lambda j, i: (first + i, 0))
    own = pl.BlockSpec((depth, wide), lambda j, i: (0, jnp.minimum(j, across - 1)))
    other = pl.BlockSpec((depth, wide), lambda j, i: (0, jnp.maximum(j - across, 0)))
    return dense_call(
        kernel,
        (2 * across, tokens // tall),
        [left] * count + [own] * count + [other] * count,
        pl.BlockSpec((tall, wide), lambda j, i: (i, j)),
        jax.ShapeDtypeStruct((tokens, 2 * half), BF16),
        4 * count * tokens * depth * half,
        "sum_products",
        waits,
    )(*lefts, *owns, *others, *waits)


ALL = ("rows", "heads", "seq")
SWAP = [(0, 1), (1, 0)]
LOWS = 32


def over_x(value):
    return lax.ppermute(value, "rows", SWAP)


def over_c(value):
    return lax.ppermute(value, "seq", SWAP)


def body(
    inputs,
    segment_ids,
    cotangent,
    attn_gain,
    ffn_gain,
    query_weight,
    key_weight,
    value_weight,
    output_weight,
    query_down,
    query_lift,
    key_down,
    key_lift,
    value_down,
    value_lift,
    output_down,
    output_lift,
    feature_maps,
    gate_weight,
    up_weight,
    down_weight,
):
    heads_size = lax.axis_size("heads")
    depth = inputs.shape[0]
    wide = heads_size // depth
    per = HEADS // heads_size
    near = depth // 2
    block_rows = per * HD
    rank = query_down.shape[1]
    width = inputs.shape[-1]
    half = width // 2
    share = inputs.shape[3]
    held = depth * share
    head_index = lax.axis_index("heads")
    x = lax.axis_index("rows")
    c = lax.axis_index("seq")
    z = head_index // wide
    y = head_index % wide
    kv_pick = y * per // (HEADS // KV)
    kv_depth = KV // depth

    def over_y(value, k):
        return lax.ppermute(
            value,
            "heads",
            [(a * wide + b, a * wide + (b ^ k)) for a in range(depth) for b in range(wide)],
        )

    def over_z(value, k=1):
        return lax.ppermute(
            value,
            "heads",
            [(a * wide + b, (a + k) % depth * wide + b) for a in range(depth) for b in range(wide)],
        )

    def trade_z(value):
        groups = [[a * wide + b for a in range(depth)] for b in range(wide)]
        return lax.all_to_all(
            value, "heads", split_axis=0, concat_axis=0, tiled=True, axis_index_groups=groups
        )

    def gather_z(block):
        return trade_z(jnp.broadcast_to(block[None], (depth,) + block.shape))

    def scatter_z(blocks):
        return jnp.sum(trade_z(blocks).astype(F32), axis=0)

    def trade_c(value, split, concat):
        return lax.all_to_all(value, "seq", split_axis=split, concat_axis=concat, tiled=True)

    def turn(value, axis):
        return jnp.stack(
            [lax.dynamic_index_in_dim(value, (z - j) % depth, axis, False) for j in range(depth)],
            axis,
        )

    def in_order(kept, moved, axis):
        return jnp.where(
            c == 0,
            jnp.concatenate([kept, moved], axis=axis),
            jnp.concatenate([moved, kept], axis=axis),
        )

    def rotate(value):
        return jnp.where(
            x == 1, jnp.concatenate([value[..., half:], value[..., :half]], axis=-1), value
        )

    def shift_sum(blocks, *waits):
        total = lax.dynamic_index_in_dim(blocks, z, 0, False).astype(F32)
        moved = [
            over_z(lax.dynamic_index_in_dim(blocks, (z + k) % depth, 0, False), k)
            for k in range(1, depth)
        ]
        for block in after(moved, *waits) if waits else moved:
            total = total + block.astype(F32)
        return total

    def gather_tokens(value, *waits):
        pieces = [value, over_c(value)]
        for k in range(1, wide):
            moved = over_y(value, k)
            if waits:
                moved = after(moved, *waits)
            pieces += [moved, over_c(moved)]
        return pieces

    def reduce_tokens(make_chip, make_others, waits=()):
        others = make_others()
        sent = []
        arrived = []
        for k in range(1, wide):
            start = (k - 1) * 2 * held
            mine = others[start : start + held]
            moved = over_c(others[start + held : start + 2 * held])
            sent.append((mine.astype(F32) + moved.astype(F32)).astype(BF16))
            arrived.append(over_y(sent[-1], k))
        chip = make_chip(sent)
        total = chip[:held].astype(F32) + over_c(chip[held:]).astype(F32)
        if waits:
            arrived = [after(piece, *waits) for piece in arrived]
        for piece in arrived:
            total = total + piece.astype(F32)
        return total, sent, (chip, *arrived)

    def rms(values):
        return lax.rsqrt(jnp.mean(values * values, axis=-1, keepdims=True) + 1e-05)

    def norm_back(values, gain, scale, grad):
        unit = values * scale
        scaled = grad * gain
        return (
            scale * (scaled - unit * jnp.mean(scaled * unit, axis=-1, keepdims=True)),
            jnp.sum(grad * unit, axis=0),
        )

    small = (
        attn_gain, ffn_gain, query_down, key_down, value_down, output_lift,
        query_lift, key_lift, value_lift, output_down, feature_maps,
    )
    packed = jnp.concatenate([piece.reshape(-1) for piece in small])
    near_small = in_order(packed[None], over_c(packed)[None], 0)[None]
    step = 1
    while step < wide:
        moved = over_y(near_small, step)
        near_small = jnp.where(
            (y // step) % 2 == 0,
            jnp.concatenate([near_small, moved], axis=0),
            jnp.concatenate([moved, near_small], axis=0),
        )
        step *= 2
    layer_in = rotate(trade_z(inputs[:, 0, 0]).reshape(held, width)).astype(F32)
    near_small = turn(
        jnp.stack([near_small] + [over_z(near_small, k) for k in range(1, depth)]), 0
    ).reshape(heads_size, 2, -1)
    far_small = over_x(near_small)
    turned_small = jnp.stack([near_small, far_small])
    spread_small = jnp.where(x == 0, turned_small, jnp.stack([far_small, near_small]))
    starts = [0]
    for piece in small:
        starts.append(starts[-1] + piece.size)

    def piece(index, turned):
        source = turned_small if turned else spread_small
        return source[..., starts[index] : starts[index + 1]].reshape(
            (2, heads_size, 2) + small[index].shape
        )

    def pick_heads(value):
        value = value.reshape((depth, wide) + value.shape[1:])
        value = lax.dynamic_index_in_dim(value, y, 1, False)
        return lax.dynamic_slice_in_dim(value, c * near, near, 0)

    gain_one = piece(0, True).reshape(width).astype(F32)
    gain_two = piece(1, True).reshape(width).astype(F32)
    downs = [piece(i, True).reshape(width, rank) for i in (2, 3, 4)]
    downs_t = jnp.concatenate(downs + [jnp.zeros((width, LOWS - 3 * rank), BF16)], axis=1).T
    out_lift = jnp.moveaxis(piece(5, True), 3, 0).reshape(rank, width)
    query_raise = jnp.transpose(
        piece(6, False).reshape(2, heads_size, 2, -1, per, HD), (1, 4, 0, 2, 3, 5)
    ).reshape(heads_size, per, rank, HD)
    query_raise = jnp.moveaxis(pick_heads(query_raise), 2, 0).reshape(rank, -1)

    def pick_keys(value):
        value = value.reshape(value.shape[0], depth, kv_depth, HD)
        value = lax.dynamic_index_in_dim(value, kv_pick, 2, False)
        return lax.dynamic_slice_in_dim(value, c * near, near, 1).reshape(value.shape[0], -1)

    def pick_near(value):
        value = value.reshape(value.shape[0], depth, kv_depth, HD)
        value = lax.dynamic_index_in_dim(value, kv_pick, 2, False).reshape(value.shape[0], -1).T
        rows_near = near * HD
        kept = lax.dynamic_slice_in_dim(value, c * rows_near, rows_near, 0)
        return in_order(kept, over_c(lax.dynamic_slice_in_dim(value, (1 - c) * rows_near, rows_near, 0)), 1)

    key_raise = pick_keys(piece(7, False)[:, 0].reshape(rank, KV * HD))
    value_raise = pick_keys(piece(8, False)[:, 0].reshape(rank, KV * HD))
    out_down = jnp.transpose(
        piece(9, False).reshape(2, heads_size, 2, per, HD, -1), (1, 3, 4, 0, 2, 5)
    ).reshape(heads_size, per, HD, rank)
    out_down = pick_heads(out_down).reshape(-1, rank)
    maps = jnp.transpose(piece(10, False), (1, 3, 0, 2, 4, 5)).reshape(heads_size, per, HD, HD)
    maps = pick_heads(maps).reshape(-1, HD, HD)
    query_rows = near * block_rows
    key_rows = near * HD
    lift = jnp.concatenate(
        [
            jnp.pad(query_raise, ((0, 0), (0, 2 * key_rows))),
            jnp.pad(key_raise, ((0, 0), (query_rows, key_rows))),
            jnp.pad(value_raise, ((0, 0), (query_rows + key_rows, 0))),
            jnp.zeros((LOWS - 3 * rank, query_rows + 2 * key_rows), BF16),
        ],
        axis=0,
    )
    row_count = query_rows + 2 * key_rows

    def hidden_rows(place):
        parts = [gate_weight, up_weight, down_weight]
        size = down_weight.shape[0] // 2
        return jnp.stack(
            [lax.dynamic_slice_in_dim(p, place * size, size, 1).T for p in parts[:2]]
            + [lax.dynamic_slice_in_dim(parts[2], place * size, size, 0)]
        )

    kept_pack = hidden_rows(c)
    moved_pack = after(over_c(hidden_rows(1 - c)), far_small)
    ffn_own = [in_order(kept_pack, moved_pack, 2)]
    ffn_other = [over_x(ffn_own[0])]
    ring_pack = jnp.where(
        c != 1,
        jnp.concatenate([kept_pack, moved_pack], axis=2),
        jnp.concatenate([moved_pack, kept_pack], axis=2),
    )
    query_blocks = gather_z(after(query_weight.T, layer_in))
    out_blocks = gather_z(after(output_weight, query_blocks))
    ffn_own.append(over_z(after(ring_pack, out_blocks)))

    def join_heads(blocks):
        kept = lax.dynamic_slice_in_dim(blocks, c * near, near, 0)
        moved = over_c(lax.dynamic_slice_in_dim(blocks, (1 - c) * near, near, 0))
        return in_order(kept, moved, 2).reshape(near * block_rows, half)

    query_own = join_heads(query_blocks)
    kv_own = jnp.concatenate([pick_near(key_weight), pick_near(value_weight)], axis=0)
    both_own = jnp.concatenate([query_own, kv_own], axis=0)
    project_own = jnp.concatenate([both_own, downs_t[:, :half]], axis=0)
    project_other = jnp.concatenate([over_x(both_own), downs_t[:, half:]], axis=0)

    def next_block():
        ffn_own.append(over_z(ffn_own[-1]))

    def next_half():
        ffn_other.append(over_x(ffn_own[len(ffn_other)]))

    scale_one = rms(layer_in)
    normed = gather_tokens((layer_in * scale_one * gain_one).astype(BF16))
    normed = (jnp.concatenate(normed[:2], axis=0), jnp.concatenate(normed[2:], axis=0))

    def project_rows(tokens):
        flat = mm(project_own, tokens[:, :half], 1, 1) + mm(project_other, tokens[:, half:], 1, 1)
        low = flat[row_count:].astype(BF16)
        return (flat[:row_count] + mm(lift, low, 0, 0)).astype(BF16), low

    pieces = [project_rows(tokens) for tokens in normed]
    rows = jnp.concatenate([piece_rows for piece_rows, _ in pieces], axis=1)
    low_rows = jnp.concatenate([low for _, low in pieces], axis=1)

    def flips(value, y_axis, c_axis):
        value = jnp.where(c == 1, jnp.flip(value, c_axis), value)
        step = 1
        while step < wide:
            shape = value.shape
            apart = value.reshape(
                shape[:y_axis] + (wide // (2 * step), 2, step) + shape[y_axis + 1 :]
            )
            value = jnp.where((y // step) % 2 == 1, jnp.flip(apart, y_axis + 1), apart).reshape(shape)
            step *= 2
        return value

    length = wide * 2 * held
    chunks = length // CHUNK
    if share % CHUNK == 0:
        across = share // CHUNK
        numbers = jnp.arange(chunks, dtype=jnp.int32).reshape(2, depth, wide, across)
        order = flips(
            jnp.arange(chunks, dtype=jnp.int32).reshape(wide, 2, depth, across), 0, 1
        )
        order = jnp.transpose(order, (1, 2, 0, 3)).reshape(-1)

        def to_natural(value):
            return value

        from_natural = to_natural
    else:
        order = jnp.arange(chunks, dtype=jnp.int32)

        def to_natural(value):
            apart = flips(value.reshape(-1, wide, 2, depth, share), 1, 2)
            return jnp.transpose(apart, (0, 2, 3, 1, 4)).reshape(value.shape)

        def from_natural(value):
            apart = jnp.transpose(value.reshape(-1, 2, depth, wide, share), (0, 3, 1, 2, 4))
            return flips(apart, 1, 2).reshape(value.shape)

    segment = lax.dynamic_index_in_dim(segment_ids[:, 0], z, 0, False)
    last = segment.reshape(chunks, CHUNK)[:, -1]
    seg_row = segment[None, :]
    seg_col = segment[:, None]
    rows_nat = to_natural(rows)
    next_block()
    next_half()
    saved = attend_forward(
        last, order, seg_row, seg_col, rows_nat, jnp.transpose(maps, (0, 2, 1)),
        (ffn_own[1],),
    )
    mixed = from_natural(saved[0])

    out_own = join_heads(after(out_blocks, ffn_other[0]))
    out_mat = jnp.concatenate([out_own, over_x(out_own)], axis=1)
    rank_rows = mm(out_down, mixed, 0, 0).astype(BF16)
    split = 2 * held

    def branch(part, *waits):
        def make(*sent):
            rows_in = after(mixed[:, part], *waits) if waits else mixed[:, part]
            return (mm(rows_in, out_mat, 0, 0) + mm(rank_rows[:, part], out_lift, 0, 0)).astype(BF16)

        return make

    chip_part, other_part = slice(0, split), slice(split, length)
    last_own = [over_z(ffn_own[2][:2])]
    next_half()
    branch_sum, _, _ = reduce_tokens(
        branch(chip_part), branch(other_part, ffn_own[2], ffn_other[1])
    )
    middle = layer_in + branch_sum
    last_own.append(over_z(after(ffn_own[2][2:], last_own[0], branch_sum)))
    last_other = [over_x(part) for part in last_own]

    scale_two = rms(middle)
    ffn_rows = stack_rows(
        gather_tokens(
            after((middle * scale_two * gain_two).astype(BF16), ffn_other[2]), last_own[1]
        )
    )
    grad_out = trade_z(after(cotangent[:, 0, 0], last_own[0], branch_sum))
    grad_out = rotate(after(grad_out, middle).reshape(held, width))
    last_other[0] = after(last_other[0], ffn_rows)
    own_gate, own_up, own_down = [
        jnp.concatenate([block[i] for block in ffn_own] + [last_own[i // 2][i % 2]], axis=0)
        for i in range(3)
    ]
    other_gate, other_up, other_down = [
        jnp.concatenate([block[i] for block in ffn_other] + [last_other[i // 2][i % 2]], axis=0)
        for i in range(3)
    ]
    chip_place = (0, split)
    other_place = (split, length - split)
    gates, ups, hidden = gate_forward(
        ffn_rows, own_gate, other_gate, own_up, other_up, (last_other[1],)
    )

    grads = stack_rows(gather_tokens(grad_out, hidden))

    def ffn_forward(place):
        return lambda *sent: sum_products([hidden], [own_down], [other_down], *place)

    swap = x.reshape(1).astype(jnp.int32)

    def sum_x(value):
        return lax.psum_scatter(value, "rows", scatter_dimension=0, tiled=False)

    down_full = weight_grad_halves(hidden, grads, swap)
    down_sums = sum_x(down_full).reshape(depth, -1, half)
    ffn_out, ffn_sent, ffn_parts = reduce_tokens(ffn_forward(chip_place), ffn_forward(other_place))

    grad_gates, grad_ups = gate_backward(
        grads, own_down, other_down, gates, ups, (down_full, ffn_parts[0], *ffn_sent)
    )

    def ffn_back(place, wait):
        return lambda sent=(): sum_products(
            [grad_gates, grad_ups],
            [own_gate, own_up],
            [other_gate, other_up],
            *place,
            (*wait, *sent),
        )

    output = trade_z(rotate((middle + ffn_out).astype(BF16)).reshape(depth, share, width))
    gate_full = weight_grad_halves(grad_gates, ffn_rows, swap, tuple(ffn_parts[1:]))
    gate_sums = sum_x(gate_full).reshape(depth, -1, half)
    down_turned = turn(down_sums, 0)
    up_full = weight_grad_halves(grad_ups, ffn_rows, swap, (gate_full, down_turned))
    up_sums = sum_x(up_full).reshape(depth, -1, half)
    down_traded = trade_z(down_turned)
    grad_ffn, grad_ffn_sent, _ = reduce_tokens(
        ffn_back(chip_place, ()),
        ffn_back(other_place, ()),
        (gate_full, up_full, down_traded),
    )

    grad_mid_norm, gain_two_grad = norm_back(middle, gain_two, scale_two, grad_ffn)
    grad_middle = grad_out.astype(F32) + grad_mid_norm

    def halves(value):
        middle_at = value.shape[-1] // 2
        first, second = value[..., :middle_at], value[..., middle_at:]
        return jnp.where(x == 0, first, second), jnp.where(x == 0, second, first)

    grad_branch = stack_rows(gather_tokens(grad_middle.astype(BF16)))
    grad_olow = mm(out_lift, grad_branch, 1, 1).astype(BF16)
    grad_mixed = (mm(out_mat, grad_branch, 1, 1) + mm(out_down, grad_olow)).astype(BF16)
    gate_sums = after(gate_sums, grad_middle)
    up_sums = after(up_sums, grad_branch)
    gate_traded = trade_z(after(turn(gate_sums, 0), output))
    up_shifted = [over_z(up_sums[depth - k], k) for k in range(1, depth)]
    out_lift_grad = mm(rank_rows, grad_branch)
    out_down_grad = mm(mixed, grad_olow, 1, 1)
    out_grads = [mm(mixed, grad_branch[:, cut]) for cut in (slice(0, half), slice(half, width))]
    down_lift = halves(out_down_grad)
    out_halves = [
        jnp.concatenate([a, b], axis=1).astype(BF16) for a, b in zip(out_grads, down_lift)
    ]
    out_moved = over_x(out_halves[1])

    grad_rows, maps_grad = attend_backward(
        last, order, seg_row, seg_col, rows_nat, maps, lift, saved, to_natural(grad_mixed),
        (out_moved, output),
    )
    grad_rows = after(from_natural(grad_rows), gate_traded, up_shifted)

    quarter = half // 2
    rank_own = rank // 4
    maps_own = HD // 4

    def part_of(value, place):
        sizes = (quarter, rank_own, maps_own)
        start = 0
        parts = []
        for size in sizes:
            if start < value.shape[1]:
                parts.append(lax.dynamic_slice_in_dim(value, start + place * size, size, 1))
            start += 2 * size
        return jnp.concatenate(parts, axis=1).astype(BF16)

    def by_depth(value, height):
        return value.reshape(near, height, value.shape[-1])

    def collect(own_half, moved, blocks, *waits):
        summed = own_half.astype(F32) + moved.astype(F32)

        def ready(place):
            return blocks(part_of(summed, place))

        return shift_sum(in_order(ready(c), over_c(ready(1 - c)), 0), *waits)

    def project_back(part):
        def make(*sent):
            return jnp.concatenate(
                [mm(grad_rows[:, part], weight, 0, 0).astype(BF16) for weight in (project_own, project_other)],
                axis=1,
            )

        return make

    grad_normed, normed_sent, _ = reduce_tokens(
        project_back(chip_part), project_back(other_part)
    )
    grad_in_norm, gain_one_grad = norm_back(layer_in, gain_one, scale_one, grad_normed)
    grad_in = rotate((grad_middle + grad_in_norm).astype(BF16)).reshape(depth, share, width)
    input_grad = trade_z(grad_in)

    late_rows = after(grad_rows, *normed_sent)
    project_grad = [
        mm(late_rows[:, chip_part], normed[0][:, cut]) + mm(late_rows[:, other_part], normed[1][:, cut])
        for cut in (slice(0, half), slice(half, width))
    ]
    lift_grad = mm(low_rows, late_rows[:row_count], 1, 1)[: 3 * rank].reshape(3, rank, row_count)
    column = lax.broadcasted_iota(jnp.int32, (3, 1, row_count), 2)
    owner_of = (column >= query_rows).astype(jnp.int32) + (column >= query_rows + key_rows)
    kind = lax.broadcasted_iota(jnp.int32, (3, 1, row_count), 0)
    lift_grad = jnp.sum(jnp.where(owner_of == kind, lift_grad, 0.0), axis=0).T

    out_sum = collect(
        out_halves[0],
        after(out_moved, *normed_sent),
        lambda value: by_depth(value, block_rows),
        grad_in,
    )

    out_grad = out_sum[:, :quarter]
    output_down_grad = out_sum[:, quarter : quarter + rank_own]

    lift_halves = halves(lift_grad)
    maps_halves = halves(
        jnp.concatenate(
            [maps_grad.reshape(query_rows, HD), jnp.zeros((2 * key_rows, HD), F32)], axis=0
        )
    )
    late_halves = [
        jnp.concatenate(
            [project_grad[i][:row_count], lift_halves[i], maps_halves[i]], axis=1
        ).astype(BF16)
        for i in range(2)
    ]
    late_sum = collect(
        late_halves[0],
        after(over_x(late_halves[1]), grad_in),
        lambda value: jnp.concatenate(
            [
                by_depth(value[:query_rows], block_rows),
                by_depth(value[query_rows : query_rows + key_rows], HD),
                by_depth(value[query_rows + key_rows :], HD),
            ],
            axis=1,
        ),
    )
    query_grad = late_sum[:block_rows, :quarter].T
    query_lift_grad = late_sum[:block_rows, quarter : quarter + rank_own].T
    feature_maps_grad = jnp.transpose(
        late_sum[:block_rows, quarter + rank_own :].reshape(per, HD, maps_own), (0, 2, 1)
    )
    kv_sum = late_sum[block_rows:, : quarter + rank_own].reshape(2, HD, quarter + rank_own)
    kv_sum = jnp.where(
        lax.broadcasted_iota(jnp.int32, (kv_depth, 1, 1, 1), 0) == kv_pick, kv_sum[None], 0.0
    ).astype(BF16)
    step = 1
    while step < wide:
        kv_sum = (kv_sum.astype(F32) + over_y(kv_sum, step).astype(F32)).astype(BF16)
        step *= 2
    kv_sum = gather_z(after(kv_sum, input_grad))
    kv_sum = jnp.transpose(kv_sum, (2, 4, 0, 1, 3)).reshape(2, quarter + rank_own, KV * HD)
    kv_sum = kv_sum.astype(F32)

    down_total = jnp.sum(after(down_traded, grad_in).astype(F32), axis=0)
    gate_total = jnp.sum(after(gate_traded, grad_in).astype(F32), axis=0)
    up_total = up_sums[0].astype(F32)
    for block in after(up_shifted, grad_in):
        up_total = up_total + block.astype(F32)

    def to_owner(total):
        total = total.astype(BF16)
        kept = lax.dynamic_slice_in_dim(total, c * quarter, quarter, 1)
        return in_order(kept, over_c(lax.dynamic_slice_in_dim(total, (1 - c) * quarter, quarter, 1)), 0)

    down_grad = to_owner(down_total).astype(F32)
    gate_grad = to_owner(gate_total).T.astype(F32)
    up_grad = to_owner(up_total).T.astype(F32)

    minor = jnp.concatenate(
        [
            gain_one_grad[None],
            gain_two_grad[None],
            jnp.concatenate([part[row_count : row_count + 3 * rank] for part in project_grad], axis=1),
            out_lift_grad,
        ],
        axis=0,
    )
    minor = minor[:, :half] + over_x(after(minor[:, half:], late_sum))
    minor = jnp.moveaxis(minor.reshape(-1, depth, wide, 2, half // (2 * heads_size)), 0, 3)
    minor = shift_sum(minor)
    total = lax.dynamic_index_in_dim(minor, y, 0, False)
    for k in range(1, wide):
        total = total + over_y(lax.dynamic_index_in_dim(minor, y ^ k, 0, False), k)
    minor = lax.dynamic_index_in_dim(total, c, 0, False) + over_c(
        lax.dynamic_index_in_dim(total, 1 - c, 0, False)
    )
    minor = minor.T
    return (
        output[:, None, None],
        input_grad[:, None, None].astype(F32),
        minor[:, 0],
        minor[:, 1],
        query_grad,
        kv_sum[0, :quarter],
        kv_sum[1, :quarter],
        out_grad,
        minor[:, 2 : 2 + rank],
        query_lift_grad,
        minor[:, 2 + rank : 2 + 2 * rank],
        kv_sum[0, quarter:],
        minor[:, 2 + 2 * rank : 2 + 3 * rank],
        kv_sum[1, quarter:],
        output_down_grad,
        minor[:, 2 + 3 * rank :].T,
        feature_maps_grad,
        gate_grad,
        up_grad,
        down_grad,
    )


def solution(mesh):
    placed = (
        P(None, "rows", "seq", "heads", None),
        P(None, "rows", None),
        P(None, "rows", "seq", "heads", None),
        P(("rows", "heads", "seq")),
        P(("rows", "heads", "seq")),
        P(("rows", "seq"), "heads"),
        P(("rows", "seq"), None),
        P(("rows", "seq"), None),
        P("heads", ("rows", "seq")),
        P(("rows", "heads", "seq"), None),
        P(("rows", "seq"), "heads"),
        P(("rows", "heads", "seq"), None),
        P(("rows", "seq"), None),
        P(("rows", "heads", "seq"), None),
        P(("rows", "seq"), None),
        P("heads", ("rows", "seq")),
        P(None, ("rows", "heads", "seq")),
        P("heads", ("rows", "seq"), None),
        P(("rows", "seq"), "heads"),
        P(("rows", "seq"), "heads"),
        P("heads", ("rows", "seq")),
    )
    return jax.shard_map(
        body,
        mesh=mesh,
        in_specs=placed,
        out_specs=(
            P(None, "rows", "seq", "heads", None),
            P(None, "rows", "seq", "heads", None),
            P(("rows", "heads", "seq")),
            P(("rows", "heads", "seq")),
            P(("rows", "seq"), "heads"),
            P(("rows", "seq"), None),
            P(("rows", "seq"), None),
            P("heads", ("rows", "seq")),
            P(("rows", "heads", "seq"), None),
            P(("rows", "seq"), "heads"),
            P(("rows", "heads", "seq"), None),
            P(("rows", "seq"), None),
            P(("rows", "heads", "seq"), None),
            P(("rows", "seq"), None),
            P("heads", ("rows", "seq")),
            P(None, ("rows", "heads", "seq")),
            P("heads", ("rows", "seq"), None),
            P(("rows", "seq"), "heads"),
            P(("rows", "seq"), "heads"),
            P("heads", ("rows", "seq")),
        ),
        check_vma=False,
    )
```
